32 devices in a mesh: pat: 8 (over z, x), obj: 4 (over y, core).
Axes of the slice: x: 2, y: 2, z: 4, core: 2. Of those that a mesh axis runs over, the one named last changes fastest.
Arguments:
- object_image: bfloat16 [2, 2048, 3072], P(None, 'obj'), may hold values from -4 to 4
- probe: float32 [2, 512, 512], replicated, may hold values from -4 to 4
- amplitudes: bfloat16 [64, 512, 512], P(('pat', 'obj')), may hold values from 0.19921875 to 3
- pos_tile: int32 [64, 2], P(('pat', 'obj')), may hold values from 0 to 9, as said below
- pos_offset: int32 [64, 2], P(('pat', 'obj')), may hold values from 0 to 255
Outputs:
- object_next: bfloat16 [2, 2048, 3072], P(None, 'obj')
- probe_next: float32 [2, 512, 512], replicated
The draws below stay inside these ranges and needn't reach their ends.
Inputs may be any that keep to these rules, and one draw needn't show every extreme that they name: On each device (aligned blocks of 2 rows) the tile rows pos_tile[:, 0] of its positions differ by at most one, and so do the tile columns pos_tile[:, 1]; every patch lies inside the object: pos_tile[:, 0] <= 5 and pos_tile[:, 1] <= 9.
All inputs are finite; a program needn't handle non-finite values.
Results may differ from the reference program's by a relative error of at most 0.01.
The reference program's roundings to bfloat16 on the way count: a program that leaves them out, or rounds other values in their place, can miss the bound.
Values may be sent and summed in bfloat16 or wider, within the bound.
No kernel may reach another device: no remote copies, remote signals or barrier semaphores. Data moves between devices by JAX's collectives and lax.ppermute only.
A program may use at most 128 MiB of HBM per device.

```python
import math
import jax
import jax.numpy as jnp
from jax import lax

PATCH = 512
TILE = 256
POS_DEV = 2
TCOLS = 12
TROWS = 8
POSITIONS = 64
N_PAT = 8
N_OBJ = 4
DEVICES = 32


def draw_pos_tile(key, part):
    key = jax.random.fold_in(key, 11)
    split_keys = jax.random.split(key, 7)
    pat_rows = DEVICES // N_OBJ
    forced = jax.random.randint(split_keys[0], (), 0, pat_rows)
    row_ids = jnp.arange(pat_rows)
    hot_rows = (jax.random.randint(split_keys[1], (pat_rows,), 0, 4) == 0) | (row_ids == forced)
    hot_owner = jax.random.randint(split_keys[2], (pat_rows,), 0, N_OBJ - 1)
    hot_owner = jnp.where(row_ids == forced, 0, hot_owner)
    dev_ids = jnp.arange(DEVICES)
    dev_row = dev_ids // N_OBJ
    dev_hot = hot_rows[dev_row]
    free_top = jax.random.randint(split_keys[3], (DEVICES,), 0, TROWS - 3)
    top_row = jnp.where(dev_hot, 2 * hot_owner[dev_row], free_top)
    left_col = jax.random.randint(split_keys[4], (DEVICES,), 0, TCOLS - 3)
    left_col = jnp.where(dev_ids == forced * N_OBJ, TCOLS - 4, left_col)
    cycled = (jnp.arange(POS_DEV)[None, :] + jax.random.randint(split_keys[5], (DEVICES, 1), 0, 2)) % 2
    random_steps = jax.random.randint(split_keys[6], (DEVICES, POS_DEV, 2), 0, 2)
    row_step = jnp.where(dev_hot[:, None], cycled, random_steps[:, :, 0])
    col_step = jnp.where(dev_hot[:, None], cycled, random_steps[:, :, 1])
    tile_row = top_row[:, None] + row_step
    tile_col = left_col[:, None] + col_step
    return jnp.stack([tile_row, tile_col], -1).reshape(POSITIONS, 2).astype(jnp.int32)


def set_ends(drawn, own_key, smallest, largest):
    shape = drawn.shape
    spot = [jax.random.randint(jax.random.fold_in(own_key, axis), (), 0, shape[axis]) for axis in range(len(shape))]
    drawn = drawn.at[tuple(spot)].set(smallest)
    longest = shape.index(max(shape))
    spot[longest] = (spot[longest] + 1) % shape[longest]
    return drawn.at[tuple(spot)].set(largest)


def block_scale(own_key, dims, cuts, least, largest):
    def one(dim, blocks):
        heights = jax.random.uniform(jax.random.fold_in(jax.random.fold_in(own_key, 6), dim), (blocks,), jnp.float32, least / len(cuts), largest / len(cuts))
        return jnp.repeat(jnp.exp(heights), dims[dim] // blocks).reshape((-1,) + (1,) * (len(dims) - dim - 1))

    level = one(*cuts[0])
    for cut in cuts[1:]:
        level = level * one(*cut)
    return level


def gaussian(key, dims, width, bound, cuts=(), kind=jnp.bfloat16):
    entries = jax.random.normal(key, dims, jnp.float32) * width
    if len(cuts) > 0:
        entries = block_scale(key, dims, cuts, -0.22, 0.18) * entries
    return jnp.clip(entries, min=-bound, max=bound).astype(kind)


def setup_inputs(seed: int = 0) -> dict:
    seeds = jax.random.split(jax.random.key(seed), 6)
    return {
        "object_image": gaussian(seeds[0], (2, TROWS * TILE, TCOLS * TILE), 0.7, 4.0, ((1, 4),)),
        "probe": gaussian(seeds[1], (2, PATCH, PATCH), 0.7, 4.0, (), jnp.float32),
        "amplitudes": jnp.clip(jnp.exp(math.log(3.0) - 2.7119641 * jax.random.uniform(seeds[2], (POSITIONS, PATCH, PATCH), jnp.float32) ** block_scale(seeds[2], (POSITIONS, PATCH, PATCH), ((0, 32),), -0.2, 0.2)), 0.19921875, 3.0).astype(jnp.bfloat16),
        "pos_tile": draw_pos_tile(jax.random.fold_in(seeds[5], 71), 0),
        "pos_offset": set_ends(jax.random.randint(seeds[4], (POSITIONS, 2), 0, TILE), jax.random.fold_in(seeds[4], 1), 0, TILE - 1).astype(jnp.int32),
    }


OBJECT_RATE = 0.1
PROBE_RATE = 0.05
MAGNITUDE_FLOOR = 0.5

def dft_tables(length):
    counter = jnp.arange(length, dtype=jnp.int32)
    phase_angle = (counter[:, None] * counter[None, :] % length).astype(jnp.float32) * (2.0 * math.pi / length)
    factor = 1.0 / math.sqrt(length)
    cosine = (jnp.cos(phase_angle) * factor).astype(jnp.bfloat16)
    sine_part = (-jnp.sin(phase_angle) * factor).astype(jnp.bfloat16)
    return (cosine, sine_part)

def operator_pair(cosine, sine_part):
    left_side = jnp.stack([jnp.stack([cosine, -sine_part]), jnp.stack([sine_part, cosine])])
    right_side = jnp.stack([jnp.stack([cosine, sine_part]), jnp.stack([-sine_part, cosine])])
    return (left_side, right_side)

def transform(wave_field, left_side, right_side):
    half_done = jnp.einsum('ocjk,bckn->bojn', left_side.astype(jnp.float32), wave_field.astype(jnp.float32)).astype(jnp.bfloat16)
    return jnp.einsum('bcjk,cokn->bojn', half_done.astype(jnp.float32), right_side.astype(jnp.float32))

def reference(object_image, probe, amplitudes, pos_tile, pos_offset):
    devices = N_PAT * N_OBJ
    zero_index = jnp.zeros((), jnp.int32)
    cosine, sine_part = dft_tables(PATCH)
    forward_left, forward_right = operator_pair(cosine, sine_part)
    inverse_left, inverse_right = operator_pair(cosine, -sine_part)
    dev_tiles = pos_tile.reshape(devices, POS_DEV, 2)
    dev_offsets = pos_offset.reshape(devices, POS_DEV, 2)
    dev_amps = amplitudes.reshape(devices, POS_DEV, PATCH, PATCH)
    probe_real = probe[0]
    probe_imag = probe[1]

    def device_step(running, items):
        object_grad, probe_grad = running
        my_tiles, my_offsets, my_amps = items
        top_row = jnp.minimum(jnp.min(my_tiles[:, 0]), TROWS - 4).astype(jnp.int32)
        left_col = jnp.minimum(jnp.min(my_tiles[:, 1]), TCOLS - 4).astype(jnp.int32)
        top_pixel = (top_row * TILE).astype(jnp.int32)
        left_pixel = (left_col * TILE).astype(jnp.int32)
        window = lax.dynamic_slice(object_image, (zero_index, top_pixel, left_pixel), (2, 4 * TILE, 4 * TILE))
        row_starts = ((my_tiles[:, 0] - top_row) * TILE + my_offsets[:, 0]).astype(jnp.int32)
        col_starts = ((my_tiles[:, 1] - left_col) * TILE + my_offsets[:, 1]).astype(jnp.int32)

        def slice_patch(row_at, col_at):
            return lax.dynamic_slice(window, (zero_index, row_at.astype(jnp.int32), col_at.astype(jnp.int32)), (2, PATCH, PATCH))
        patches = jax.vmap(slice_patch)(row_starts, col_starts)
        patch_real = patches[:, 0].astype(jnp.float32)
        patch_imag = patches[:, 1].astype(jnp.float32)
        exit_wave = jnp.stack([probe_real * patch_real - probe_imag * patch_imag, probe_real * patch_imag + probe_imag * patch_real], 1).astype(jnp.bfloat16)
        far_field = transform(exit_wave, forward_left, forward_right)
        modulus = jnp.sqrt(far_field[:, 0] * far_field[:, 0] + far_field[:, 1] * far_field[:, 1])
        keep_share = 1.0 - my_amps.astype(jnp.float32) / jnp.maximum(modulus, MAGNITUDE_FLOOR)
        residual = (far_field * keep_share[:, None]).astype(jnp.bfloat16)
        back_field = transform(residual, inverse_left, inverse_right)
        back_real = back_field[:, 0]
        back_imag = back_field[:, 1]
        patch_grad = jnp.stack([probe_real * back_real + probe_imag * back_imag, probe_real * back_imag - probe_imag * back_real], 1)
        probe_term = jnp.stack([lax.optimization_barrier(jnp.sum(patch_real * back_real + patch_imag * back_imag, 0)), lax.optimization_barrier(jnp.sum(patch_real * back_imag - patch_imag * back_real, 0))])

        def place(item_index, accumulated):
            corner_at = (zero_index, row_starts[item_index].astype(jnp.int32), col_starts[item_index].astype(jnp.int32))
            current = lax.dynamic_slice(accumulated, corner_at, (2, PATCH, PATCH))
            return lax.dynamic_update_slice(accumulated, current + patch_grad[item_index], corner_at)
        window_grad = lax.fori_loop(0, POS_DEV, place, jnp.zeros((2, 4 * TILE, 4 * TILE), jnp.float32))
        rounded = lax.optimization_barrier(window_grad.astype(jnp.bfloat16)).astype(jnp.float32)
        corner_at = (zero_index, top_pixel, left_pixel)
        current = lax.dynamic_slice(object_grad, corner_at, (2, 4 * TILE, 4 * TILE))
        object_grad = lax.dynamic_update_slice(object_grad, current + rounded, corner_at)
        return ((object_grad, probe_grad + probe_term), None)
    starting = (jnp.zeros((2, TROWS * TILE, TCOLS * TILE), jnp.float32), jnp.zeros((2, PATCH, PATCH), jnp.float32))
    finished, ignored = lax.scan(device_step, starting, (dev_tiles, dev_offsets, dev_amps))
    object_grad, probe_grad = finished
    object_next = (object_image.astype(jnp.float32) - OBJECT_RATE * object_grad).astype(jnp.bfloat16)
    probe_next = probe - PROBE_RATE * probe_grad
    return (object_next, probe_next)
```

```python
import functools
import math

import jax
import jax.numpy as jnp
from jax import lax
from jax.experimental import pallas as pl
from jax.experimental.pallas import tpu as pltpu
from jax.sharding import PartitionSpec as P

PATCH = 512
TILE = 256
LANES = 128
WIDE = PATCH + LANES

OBJECT_RATE = 0.1
PROBE_RATE = 0.05
MAGNITUDE_FLOOR = 0.5
VMEM_LIMIT = 56 * 1024 * 1024


def dft_matrices(length):
    counter = jnp.arange(length, dtype=jnp.int32)
    phase_angle = (counter[:, None] * counter[None, :] % length).astype(jnp.float32) * (
        2.0 * math.pi / length
    )
    factor = 1.0 / math.sqrt(length)
    cosine = (jnp.cos(phase_angle) * factor).astype(jnp.bfloat16)
    sine_part = (-jnp.sin(phase_angle) * factor).astype(jnp.bfloat16)
    top = jnp.concatenate([cosine, -sine_part], 1)
    bottom = jnp.concatenate([sine_part, cosine], 1)
    left = jnp.concatenate([top, bottom], 0)
    top = jnp.concatenate([cosine, sine_part], 1)
    bottom = jnp.concatenate([-sine_part, cosine], 1)
    right = jnp.concatenate([top, bottom], 0)
    return left, right


def first_row(pos, index):
    return pos[index, 0] * TILE + pos[index, 2]


def first_col(pos, index):
    return pos[index, 1] * TILE + pos[index, 3]


def shifted_left(wide, amount):
    return pltpu.roll(wide, lax.rem(WIDE - amount, WIDE), axis=1)[:, :PATCH]


def band_of_rows(row_at, start, count):
    rows = lax.broadcasted_iota(jnp.int32, (count, PATCH), 0) + start
    return row_at // PATCH + (rows < lax.rem(row_at, PATCH)).astype(jnp.int32)


CHUNK = 64
SUBLANES = 8


def rows_from(ref, plane, start, count):
    aligned = pl.multiple_of(start // SUBLANES * SUBLANES, SUBLANES)
    tall = count + SUBLANES
    data = ref[plane, pl.ds(aligned, tall), :]
    return pltpu.roll(data, lax.rem(tall - lax.rem(start, SUBLANES), tall), axis=0)[:count]


def cut_kernel(flips, pos, me, *refs):
    step = pl.program_id(0)
    blocks, out = refs[:-1], refs[-1]
    target = lax.bitwise_xor(me[0], flips[0])
    for k in range(1, len(flips)):
        target = jnp.where(step // 2 == k, lax.bitwise_xor(me[0], flips[k]), target)
    amount = lax.rem(first_col(pos, 2 * target + lax.rem(step, 2)), LANES)

    def body(i, carry):
        rows = pl.ds(pl.multiple_of(i * CHUNK, CHUNK), CHUNK)
        for plane in range(2):
            wide = jnp.concatenate([b[plane, rows, :] for b in blocks], 1)
            out[0, plane, rows, :] = shifted_left(wide.astype(jnp.float32), amount).astype(
                jnp.bfloat16
            )
        return carry

    lax.fori_loop(0, PATCH // CHUNK, body, 0)


def cut(band, pos, me, flips):
    def block(k):
        def index(i, pos, me):
            target = lax.bitwise_xor(me[0], flips[0])
            for j in range(1, len(flips)):
                target = jnp.where(i // 2 == j, lax.bitwise_xor(me[0], flips[j]), target)
            return (0, 0, first_col(pos, 2 * target + lax.rem(i, 2)) // LANES + k)

        return pl.BlockSpec((2, PATCH, LANES), index)

    count = 2 * len(flips)
    return pl.pallas_call(
        functools.partial(cut_kernel, flips),
        grid_spec=pltpu.PrefetchScalarGridSpec(
            num_scalar_prefetch=2,
            grid=(count,),
            in_specs=[block(k) for k in range(WIDE // LANES)],
            out_specs=pl.BlockSpec((1, 2, PATCH, PATCH), lambda i, pos, me: (i, 0, 0, 0)),
        ),
        out_shape=jax.ShapeDtypeStruct((count, 2, PATCH, PATCH), jnp.bfloat16),
        compiler_params=pltpu.CompilerParams(vmem_limit_bytes=VMEM_LIMIT),
        cost_estimate=pl.CostEstimate(
            flops=count * 2 * PATCH * WIDE, bytes_accessed=count * 2300000, transcendentals=0
        ),
    )(pos, me, *([band] * (WIDE // LANES)))


def merge_kernel(which, pos, me, *refs):
    blocks, sibling, out = refs[:-2], refs[-2], refs[-1]
    index = 2 * lax.bitwise_xor(me[0], 2) + which
    amount = lax.rem(first_col(pos, index), LANES)
    row_at = first_row(pos, index)

    def body(i, carry):
        rows = pl.ds(pl.multiple_of(i * CHUNK, CHUNK), CHUNK)
        mine = band_of_rows(row_at, i * CHUNK, CHUNK) == me[0]
        for plane in range(2):
            wide = jnp.concatenate([b[plane, rows, :] for b in blocks], 1)
            own = shifted_left(wide.astype(jnp.float32), amount)
            other = sibling[0, plane, rows, :].astype(jnp.float32)
            out[plane, rows, :] = jnp.where(mine, own, other).astype(jnp.bfloat16)
        return carry

    lax.fori_loop(0, PATCH // CHUNK, body, 0)


def cut_and_merge(band, sibling, pos, me, which):
    def block(k):
        def index(i, pos, me):
            return (0, 0, first_col(pos, 2 * lax.bitwise_xor(me[0], 2) + which) // LANES + k)

        return pl.BlockSpec((2, PATCH, LANES), index)

    return pl.pallas_call(
        functools.partial(merge_kernel, which),
        grid_spec=pltpu.PrefetchScalarGridSpec(
            num_scalar_prefetch=2,
            grid=(1,),
            in_specs=[block(k) for k in range(WIDE // LANES)]
            + [pl.BlockSpec((1, 2, PATCH, PATCH), lambda i, pos, me: (which, 0, 0, 0))],
            out_specs=pl.BlockSpec((2, PATCH, PATCH), lambda i, pos, me: (0, 0, 0)),
        ),
        out_shape=jax.ShapeDtypeStruct((2, PATCH, PATCH), jnp.bfloat16),
        compiler_params=pltpu.CompilerParams(vmem_limit_bytes=VMEM_LIMIT),
        cost_estimate=pl.CostEstimate(
            flops=2 * PATCH * WIDE, bytes_accessed=3300000, transcendentals=0
        ),
    )(pos, me, *([band] * (WIDE // LANES)), sibling)


def wave_kernel(which, has_term, pos, me, band, sibling, across, probe, amplitudes, left, right, *refs):
    if has_term:
        term_in, grad, term, *scratch = refs
    else:
        grad, term, *scratch = refs
    window, sib_v, far_v, probe_v, amp_v, left_v, right_v, term_v, patch_v, twice, field, half, sems = scratch
    index = 2 * me[0] + which
    col_at = first_col(pos, index)
    row_at = first_row(pos, index)
    start = pl.multiple_of(col_at // LANES * LANES, LANES)
    pairs = [
        (band.at[:, :, pl.ds(start, WIDE)], window),
        (sibling.at[which], sib_v),
        (across, far_v),
        (probe, probe_v),
        (left, left_v),
        (right, right_v),
        (amplitudes.at[which], amp_v),
    ]
    if has_term:
        pairs.append((term_in, term_v))
    copies = [pltpu.make_async_copy(a, b, sems.at[k]) for k, (a, b) in enumerate(pairs)]
    for copy in copies:
        copy.start()
    for copy in copies[:3]:
        copy.wait()
    amount = lax.rem(col_at, LANES)
    down = lax.rem(row_at, PATCH)

    def assemble(i, carry):
        at = pl.multiple_of(i * CHUNK, CHUNK)
        rows = pl.ds(at, CHUNK)
        owner = band_of_rows(row_at, at, CHUNK)
        mine = owner == me[0]
        near = owner == lax.bitwise_xor(me[0], 1)
        for plane in range(2):
            own = shifted_left(window[plane, rows, :].astype(jnp.float32), amount)
            beside = sib_v[plane, rows, :].astype(jnp.float32)
            beyond = far_v[plane, rows, :].astype(jnp.float32)
            patch = jnp.where(mine, own, jnp.where(near, beside, beyond))
            twice[plane, rows, :] = patch
            twice[plane, pl.ds(pl.multiple_of(at + PATCH, CHUNK), CHUNK), :] = patch
        return carry

    lax.fori_loop(0, PATCH // CHUNK, assemble, 0)
    copies[3].wait()

    def illuminate(i, carry):
        at = pl.multiple_of(i * CHUNK, CHUNK)
        rows = pl.ds(at, CHUNK)
        patch_real = rows_from(twice, 0, at + down, CHUNK)
        patch_imag = rows_from(twice, 1, at + down, CHUNK)
        patch_v[0, rows, :] = patch_real.astype(jnp.bfloat16)
        patch_v[1, rows, :] = patch_imag.astype(jnp.bfloat16)
        probe_real = probe_v[0, rows, :]
        probe_imag = probe_v[1, rows, :]
        field[rows, :] = (probe_real * patch_real - probe_imag * patch_imag).astype(jnp.bfloat16)
        field[pl.ds(pl.multiple_of(at + PATCH, CHUNK), CHUNK), :] = (
            probe_real * patch_imag + probe_imag * patch_real
        ).astype(jnp.bfloat16)
        return carry

    lax.fori_loop(0, PATCH // CHUNK, illuminate, 0)
    copies[4].wait()

    def over_rows(table):
        for k in range(4):
            part = jnp.dot(
                table[256 * k : 256 * (k + 1), :], field[...], preferred_element_type=jnp.float32
            ).astype(jnp.bfloat16)
            half[256 * (k % 2) : 256 * (k % 2 + 1), PATCH * (k // 2) : PATCH * (k // 2 + 1)] = part

    over_rows(left_v)
    copies[5].wait()
    copies[6].wait()
    for k in range(2):
        rows = slice(256 * k, 256 * (k + 1))
        far = jnp.dot(half[rows, :], right_v[...], preferred_element_type=jnp.float32)
        far_real = far[:, :PATCH]
        far_imag = far[:, PATCH:]
        power = far_real * far_real + far_imag * far_imag
        keep = 1.0 - amp_v[rows, :].astype(jnp.float32) * lax.rsqrt(
            jnp.maximum(power, MAGNITUDE_FLOOR * MAGNITUDE_FLOOR)
        )
        field[rows, :] = (far_real * keep).astype(jnp.bfloat16)
        field[PATCH + 256 * k : PATCH + 256 * (k + 1), :] = (far_imag * keep).astype(jnp.bfloat16)
    over_rows(right_v)
    if has_term:
        copies[7].wait()
    for k in range(2):
        rows = slice(256 * k, 256 * (k + 1))
        back = jnp.dot(half[rows, :], left_v[...], preferred_element_type=jnp.float32)
        back_real = back[:, :PATCH]
        back_imag = back[:, PATCH:]
        patch_real = patch_v[0, rows, :].astype(jnp.float32)
        patch_imag = patch_v[1, rows, :].astype(jnp.float32)
        term_real = patch_real * back_real + patch_imag * back_imag
        term_imag = patch_real * back_imag - patch_imag * back_real
        if has_term:
            term_real = term_real + term_v[0, rows, :]
            term_imag = term_imag + term_v[1, rows, :]
        term[0, rows, :] = term_real
        term[1, rows, :] = term_imag
        term_v[0, rows, :] = back_real
        term_v[1, rows, :] = back_imag

    def weigh(i, carry):
        at = pl.multiple_of(i * CHUNK, CHUNK)
        rows = pl.ds(at, CHUNK)
        again = pl.ds(pl.multiple_of(at + PATCH, CHUNK), CHUNK)
        probe_real = probe_v[0, rows, :]
        probe_imag = probe_v[1, rows, :]
        back_real = term_v[0, rows, :]
        back_imag = term_v[1, rows, :]
        grad_real = probe_real * back_real + probe_imag * back_imag
        grad_imag = probe_real * back_imag - probe_imag * back_real
        twice[0, rows, :] = grad_real
        twice[0, again, :] = grad_real
        twice[1, rows, :] = grad_imag
        twice[1, again, :] = grad_imag
        return carry

    lax.fori_loop(0, PATCH // CHUNK, weigh, 0)
    classes, height = grad.shape[0], grad.shape[2]

    def spread(k, carry):
        for plane in range(2):
            grad[k, plane] = rows_from(twice, plane, PATCH - down + k * height, height).astype(
                jnp.bfloat16
            )
        return carry

    lax.fori_loop(0, classes, spread, 0)


def wave(which, classes, pos, me, band, sibling, across, probe, amplitudes, left, right, term):
    has_term = term is not None
    operands = [band, sibling, across, probe, amplitudes, left, right] + ([term] if has_term else [])
    smem = pl.BlockSpec(memory_space=pltpu.SMEM)
    hbm = pl.BlockSpec(memory_space=pl.ANY)
    vmem = pl.BlockSpec(memory_space=pltpu.VMEM)
    planes = (2, PATCH, PATCH)
    return pl.pallas_call(
        functools.partial(wave_kernel, which, has_term),
        in_specs=[smem, smem] + [hbm] * len(operands),
        out_specs=[vmem, vmem],
        out_shape=[
            jax.ShapeDtypeStruct((classes, 2, PATCH // classes, PATCH), jnp.bfloat16),
            jax.ShapeDtypeStruct(planes, jnp.float32),
        ],
        scratch_shapes=[
            pltpu.VMEM((2, PATCH, WIDE), jnp.bfloat16),
            pltpu.VMEM(planes, jnp.bfloat16),
            pltpu.VMEM(planes, jnp.bfloat16),
            pltpu.VMEM(planes, jnp.float32),
            pltpu.VMEM((PATCH, PATCH), jnp.bfloat16),
            pltpu.VMEM((2 * PATCH, 2 * PATCH), jnp.bfloat16),
            pltpu.VMEM((2 * PATCH, 2 * PATCH), jnp.bfloat16),
            pltpu.VMEM(planes, jnp.float32),
            pltpu.VMEM(planes, jnp.bfloat16),
            pltpu.VMEM((2, 2 * PATCH + SUBLANES, PATCH), jnp.float32),
            pltpu.VMEM((2 * PATCH, PATCH), jnp.bfloat16),
            pltpu.VMEM((PATCH, 2 * PATCH), jnp.bfloat16),
            pltpu.SemaphoreType.DMA((8,)),
        ],
        compiler_params=pltpu.CompilerParams(vmem_limit_bytes=VMEM_LIMIT),
        cost_estimate=pl.CostEstimate(
            flops=32 * PATCH**3, bytes_accessed=14000000, transcendentals=PATCH * PATCH
        ),
    )(pos, me, *operands)


def sum_kernel(pos, me, first, second, own, away, canvas):
    classes, height = first.shape[0], first.shape[2]
    start = me[1] * height
    canvas[...] = jnp.zeros_like(canvas)
    rows = lax.broadcasted_iota(jnp.int32, (2 * height, WIDE), 0)
    rows = start + jnp.where(rows >= height, rows - height, rows)

    def piece(k, source, which):
        index = 2 * k + which
        row_at = first_row(pos, index)
        col_at = first_col(pos, index)
        down = lax.rem(row_at, PATCH)
        at = pl.ds(pl.multiple_of(col_at // LANES * LANES, LANES), WIDE)
        data = source[k].astype(jnp.float32).reshape(2 * height, PATCH)
        data = jnp.concatenate([data, jnp.zeros((2 * height, LANES), jnp.float32)], 1)
        data = pltpu.roll(data, lax.rem(col_at, LANES), axis=1)

        @pl.when(down < start + height)
        def _():
            canvas[row_at // PATCH, :, at] += jnp.where(rows >= down, data, 0.0)

        @pl.when(down > start)
        def _():
            canvas[row_at // PATCH + 1, :, at] += jnp.where(rows < down, data, 0.0)

    def body(k, carry):
        piece(k, first, 0)
        piece(k, second, 1)
        return carry

    lax.fori_loop(0, classes, body, 0)
    shape = own.shape[1:]
    for k in range(2):
        keep = lax.bitwise_xor(me[0], 2 - 2 * k)
        give = lax.bitwise_xor(me[0], 3 - 2 * k)
        own[k] = canvas[keep].reshape(shape)
        away[k] = canvas[give].reshape(shape).astype(jnp.bfloat16)


def sum_pieces(pos, me, first, second, bands, width):
    height = first.shape[2]
    smem = pl.BlockSpec(memory_space=pltpu.SMEM)
    vmem = pl.BlockSpec(memory_space=pltpu.VMEM)
    shape = (2, 2, height, width)
    return pl.pallas_call(
        sum_kernel,
        in_specs=[smem, smem, vmem, vmem],
        out_specs=[vmem, vmem],
        out_shape=[
            jax.ShapeDtypeStruct(shape, jnp.float32),
            jax.ShapeDtypeStruct(shape, jnp.bfloat16),
        ],
        scratch_shapes=[pltpu.VMEM((bands, 2 * height, width), jnp.float32)],
        compiler_params=pltpu.CompilerParams(vmem_limit_bytes=VMEM_LIMIT),
        cost_estimate=pl.CostEstimate(
            flops=8 * first.size, bytes_accessed=4 * first.size + 6 * math.prod(shape), transcendentals=0
        ),
    )(pos, me, first, second)


def shards(object_image, probe, amplitudes, pos_tile, pos_offset):
    owners = lax.axis_size("obj")
    classes = lax.axis_size("pat")
    my_owner = lax.axis_index("obj").astype(jnp.int32)
    my_class = lax.axis_index("pat").astype(jnp.int32)
    me = jnp.stack([my_owner, my_class])
    height = PATCH // classes
    width = object_image.shape[2]
    assert owners == 4 and object_image.shape[1] == PATCH and pos_tile.shape[0] == 2

    def flip(value, bit):
        return lax.ppermute(value, "obj", [(k, k ^ bit) for k in range(owners)])

    own_pos = jnp.concatenate([pos_tile, pos_offset], 1)
    pos = lax.all_gather(own_pos, "obj", axis=0, tiled=True)
    pos_pat = lax.all_gather(own_pos, "pat", axis=0, tiled=True)

    relay = flip(cut(object_image, pos, me, (3,)), 1)
    across = [flip(cut_and_merge(object_image, relay, pos, me, k), 2) for k in range(2)]
    sibling = flip(cut(object_image, pos, me, (1,)), 1)

    left, right = dft_matrices(PATCH)
    grad_0, term = wave(
        0, classes, pos, me, object_image, sibling, across[0], probe, amplitudes, left, right, None
    )
    part_0 = lax.all_to_all(grad_0, "pat", split_axis=0, concat_axis=0, tiled=True)
    grad_1, term = wave(
        1, classes, pos, me, object_image, sibling, across[1], probe, amplitudes, left, right, term
    )
    part_1 = lax.all_to_all(grad_1, "pat", split_axis=0, concat_axis=0, tiled=True)

    own, away = sum_pieces(pos_pat, me, part_0, part_1, owners, width)
    from_sibling_far = flip(away[0], 1)
    from_sibling = flip(away[1], 1)
    from_across = flip(
        (own[0] + from_sibling_far.astype(jnp.float32)).astype(jnp.bfloat16), 2
    )
    total = own[1] + from_sibling.astype(jnp.float32) + from_across.astype(jnp.float32)
    mine = lax.dynamic_slice_in_dim(object_image, my_class * height, height, 1)
    updated = (mine.astype(jnp.float32) - OBJECT_RATE * total).astype(jnp.bfloat16)
    object_next = lax.all_gather(updated, "pat", axis=1, tiled=True)

    core = my_owner % 2
    line = my_owner // 2
    plane = lax.dynamic_index_in_dim(term, core, 0, False) + flip(
        lax.dynamic_index_in_dim(term, 1 - core, 0, False), 1
    )
    rows = plane.shape[0] // 2
    quarter = lax.dynamic_slice_in_dim(plane, line * rows, rows, 0) + flip(
        lax.dynamic_slice_in_dim(plane, (1 - line) * rows, rows, 0), 2
    )
    quarter = lax.psum(quarter, "pat")
    quarters = lax.all_gather(quarter, "obj", axis=0)
    probe_total = quarters.reshape(2, 2, rows, PATCH).transpose(1, 0, 2, 3).reshape(2, PATCH, PATCH)
    probe_next = probe - PROBE_RATE * probe_total
    return (object_next, probe_next)


def solution(mesh):
    return jax.shard_map(
        shards,
        mesh=mesh,
        in_specs=(
            P(None, "obj", None),
            P(),
            P(("pat", "obj"), None, None),
            P(("pat", "obj"), None),
            P(("pat", "obj"), None),
        ),
        out_specs=(P(None, "obj", None), P()),
        check_vma=False,
    )
```

```python
import functools
import math

import jax
import jax.numpy as jnp
from jax import lax
from jax.experimental import pallas as pl
from jax.experimental.pallas import tpu as pltpu
from jax.sharding import PartitionSpec as P

PATCH = 512
TILE = 256
LANES = 128
WIDE = PATCH + LANES

OBJECT_RATE = 0.1
PROBE_RATE = 0.05
MAGNITUDE_FLOOR = 0.5
CUT_VMEM = 14 * 1024 * 1024
WAVE_VMEM = 32 * 1024 * 1024
SUM_VMEM = 24 * 1024 * 1024


def dft_tables(length):
    counter = jnp.arange(length, dtype=jnp.int32)
    phase_angle = (counter[:, None] * counter[None, :] % length).astype(jnp.float32) * (
        2.0 * math.pi / length
    )
    factor = 1.0 / math.sqrt(length)
    cosine = (jnp.cos(phase_angle) * factor).astype(jnp.bfloat16)
    sine_part = (-jnp.sin(phase_angle) * factor).astype(jnp.bfloat16)
    return cosine, sine_part, -sine_part


def first_row(pos, index):
    return pos[index, 0] * TILE + pos[index, 2]


def first_col(pos, index):
    return pos[index, 1] * TILE + pos[index, 3]


def shifted_left(blocks, amount):
    turned = [pltpu.roll(b, lax.rem(LANES - amount, LANES), axis=1) for b in blocks]
    lane = lax.broadcasted_iota(jnp.int32, turned[0].shape, 1)
    stay = lane < LANES - amount
    return jnp.concatenate([jnp.where(stay, a, b) for a, b in zip(turned, turned[1:])], 1)


def shifted_right(data, amount):
    count = data.shape[1] // LANES
    turned = [pltpu.roll(data[:, LANES * k : LANES * (k + 1)], amount, axis=1) for k in range(count)]
    lane = lax.broadcasted_iota(jnp.int32, turned[0].shape, 1)
    stay = lane >= amount
    before = [jnp.zeros_like(turned[0])] + turned
    after = turned + [jnp.zeros_like(turned[0])]
    return jnp.concatenate([jnp.where(stay, a, b) for a, b in zip(after, before)], 1)


def band_of_rows(row_at, start, count):
    rows = lax.broadcasted_iota(jnp.int32, (count, PATCH), 0) + start
    return row_at // PATCH + (rows < lax.rem(row_at, PATCH)).astype(jnp.int32)


CHUNK = 64
SUBLANES = 8


def rows_from(ref, plane, start, count):
    aligned = pl.multiple_of(start // SUBLANES * SUBLANES, SUBLANES)
    amount = lax.rem(start, SUBLANES)
    data = ref[plane, pl.ds(aligned, count + SUBLANES), :]
    data = data.reshape(count // SUBLANES + 1, SUBLANES, data.shape[1])
    turned = pltpu.roll(data, lax.rem(SUBLANES - amount, SUBLANES), axis=1)
    row = lax.broadcasted_iota(jnp.int32, turned[1:].shape, 1)
    data = jnp.where(row < SUBLANES - amount, turned[:-1], turned[1:])
    return data.reshape(count, data.shape[2])


def cut_rows(blocks, plane, rows, amount):
    return shifted_left([b[plane, rows, :].astype(jnp.float32) for b in blocks], amount)


def cut_kernel(flip, first, pos, me, *refs):
    blocks, out = refs[:-1], refs[-1]
    target = lax.bitwise_xor(me[0], flip)
    amount = lax.rem(first_col(pos, 2 * target + first + pl.program_id(0)), LANES)

    def body(i, carry):
        rows = pl.ds(pl.multiple_of(i * CHUNK, CHUNK), CHUNK)
        for plane in range(2):
            out[0, plane, rows, :] = cut_rows(blocks, plane, rows, amount).astype(jnp.bfloat16)
        return carry

    lax.fori_loop(0, PATCH // CHUNK, body, 0)


def cut(band, pos, me, flip, first, count):
    def block(k):
        def index(i, pos, me):
            return (0, 0, first_col(pos, 2 * lax.bitwise_xor(me[0], flip) + first + i) // LANES + k)

        return pl.BlockSpec((2, PATCH, LANES), index)

    return pl.pallas_call(
        functools.partial(cut_kernel, flip, first),
        grid_spec=pltpu.PrefetchScalarGridSpec(
            num_scalar_prefetch=2,
            grid=(count,),
            in_specs=[block(k) for k in range(WIDE // LANES)],
            out_specs=pl.BlockSpec((1, 2, PATCH, PATCH), lambda i, pos, me: (i, 0, 0, 0)),
        ),
        out_shape=jax.ShapeDtypeStruct((count, 2, PATCH, PATCH), jnp.bfloat16),
        compiler_params=pltpu.CompilerParams(vmem_limit_bytes=CUT_VMEM),
        cost_estimate=pl.CostEstimate(
            flops=count * 2 * PATCH * WIDE, bytes_accessed=count * 2300000, transcendentals=0
        ),
    )(pos, me, *([band] * (WIDE // LANES)))


def merge_kernel(which, pos, me, *refs):
    blocks, sibling, out = refs[:-2], refs[-2], refs[-1]
    index = 2 * lax.bitwise_xor(me[0], 2) + which
    amount = lax.rem(first_col(pos, index), LANES)
    row_at = first_row(pos, index)

    def body(i, carry):
        rows = pl.ds(pl.multiple_of(i * CHUNK, CHUNK), CHUNK)
        mine = band_of_rows(row_at, i * CHUNK, CHUNK) == me[0]
        for plane in range(2):
            own = cut_rows(blocks, plane, rows, amount)
            other = sibling[0, plane, rows, :].astype(jnp.float32)
            out[plane, rows, :] = jnp.where(mine, own, other).astype(jnp.bfloat16)
        return carry

    lax.fori_loop(0, PATCH // CHUNK, body, 0)


def cut_and_merge(band, sibling, pos, me, which):
    def block(k):
        def index(i, pos, me):
            return (0, 0, first_col(pos, 2 * lax.bitwise_xor(me[0], 2) + which) // LANES + k)

        return pl.BlockSpec((2, PATCH, LANES), index)

    return pl.pallas_call(
        functools.partial(merge_kernel, which),
        grid_spec=pltpu.PrefetchScalarGridSpec(
            num_scalar_prefetch=2,
            grid=(1,),
            in_specs=[block(k) for k in range(WIDE // LANES)]
            + [pl.BlockSpec((1, 2, PATCH, PATCH), lambda i, pos, me: (0, 0, 0, 0))],
            out_specs=pl.BlockSpec((2, PATCH, PATCH), lambda i, pos, me: (0, 0, 0)),
        ),
        out_shape=jax.ShapeDtypeStruct((2, PATCH, PATCH), jnp.bfloat16),
        compiler_params=pltpu.CompilerParams(vmem_limit_bytes=CUT_VMEM),
        cost_estimate=pl.CostEstimate(
            flops=2 * PATCH * WIDE, bytes_accessed=3300000, transcendentals=0
        ),
    )(pos, me, *([band] * (WIDE // LANES)), sibling)


def wave_kernel(which, pos, me, spare, band, sibling, across, probe, amplitudes, *refs):
    tables, refs = refs[:3], refs[3:]
    last = which == 1
    if last:
        term_in, grad, keep_term, give_term, *scratch = refs
    else:
        grad, term_out, *scratch = refs
    window, sib_v, far_v, probe_v, amp_v, left_v, right_v, term_v, patch_v, twice, field, half, sems = scratch
    index = 2 * me[0] + which
    col_at = first_col(pos, index)
    row_at = first_row(pos, index)
    start = pl.multiple_of(col_at // LANES * LANES, LANES)
    pairs = [
        (band.at[:, :, pl.ds(start, WIDE)], window),
        (sibling.at[which], sib_v),
        (across, far_v),
        (probe, probe_v),
    ]
    cosine, sine, minus = tables
    quarters = [(slice(0, PATCH), slice(0, PATCH)), (slice(0, PATCH), slice(PATCH, 2 * PATCH))]
    quarters += [(slice(PATCH, 2 * PATCH), slice(0, PATCH)), (slice(PATCH, 2 * PATCH), slice(PATCH, 2 * PATCH))]
    pairs += [(t, left_v.at[q]) for t, q in zip((cosine, minus, sine, cosine), quarters)]
    pairs.append((amplitudes.at[which], amp_v))
    pairs += [(t, right_v.at[q]) for t, q in zip((cosine, sine, minus, cosine), quarters)]
    if last:
        pairs.append((term_in, term_v))
    copies = [pltpu.make_async_copy(a, b, sems.at[k]) for k, (a, b) in enumerate(pairs)]
    for copy in copies:
        copy.start()
    for copy in copies[:3]:
        copy.wait()
    amount = lax.rem(col_at, LANES)
    down = lax.rem(row_at, PATCH)
    views = [window.at[:, :, LANES * k : LANES * (k + 1)] for k in range(WIDE // LANES)]

    def assemble(i, carry):
        at = pl.multiple_of(i * CHUNK, CHUNK)
        rows = pl.ds(at, CHUNK)
        owner = band_of_rows(row_at, at, CHUNK)
        mine = owner == me[0]
        near = owner == lax.bitwise_xor(me[0], 1)
        for plane in range(2):
            own = cut_rows(views, plane, rows, amount)
            beside = sib_v[plane, rows, :].astype(jnp.float32)
            beyond = far_v[plane, rows, :].astype(jnp.float32)
            patch = jnp.where(mine, own, jnp.where(near, beside, beyond))
            twice[plane, rows, :] = patch
            twice[plane, pl.ds(pl.multiple_of(at + PATCH, CHUNK), CHUNK), :] = patch
        return carry

    lax.fori_loop(0, PATCH // CHUNK, assemble, 0)
    copies[3].wait()

    def illuminate(i, carry):
        at = pl.multiple_of(i * CHUNK, CHUNK)
        rows = pl.ds(at, CHUNK)
        patch_real = rows_from(twice, 0, at + down, CHUNK)
        patch_imag = rows_from(twice, 1, at + down, CHUNK)
        patch_v[0, rows, :] = patch_real.astype(jnp.bfloat16)
        patch_v[1, rows, :] = patch_imag.astype(jnp.bfloat16)
        probe_real = probe_v[0, rows, :]
        probe_imag = probe_v[1, rows, :]
        field[rows, :] = (probe_real * patch_real - probe_imag * patch_imag).astype(jnp.bfloat16)
        field[pl.ds(pl.multiple_of(at + PATCH, CHUNK), CHUNK), :] = (
            probe_real * patch_imag + probe_imag * patch_real
        ).astype(jnp.bfloat16)
        return carry

    lax.fori_loop(0, PATCH // CHUNK, illuminate, 0)
    for copy in copies[4:8]:
        copy.wait()

    def over_rows(table):
        for k in range(4):
            part = jnp.dot(
                table[256 * k : 256 * (k + 1), :], field[...], preferred_element_type=jnp.float32
            ).astype(jnp.bfloat16)
            half[256 * (k % 2) : 256 * (k % 2 + 1), PATCH * (k // 2) : PATCH * (k // 2 + 1)] = part

    over_rows(left_v)
    for copy in copies[8:13]:
        copy.wait()
    for k in range(2):
        rows = slice(256 * k, 256 * (k + 1))
        far = jnp.dot(half[rows, :], right_v[...], preferred_element_type=jnp.float32)
        far_real = far[:, :PATCH]
        far_imag = far[:, PATCH:]
        power = far_real * far_real + far_imag * far_imag
        keep = 1.0 - amp_v[rows, :].astype(jnp.float32) * lax.rsqrt(
            jnp.maximum(power, MAGNITUDE_FLOOR * MAGNITUDE_FLOOR)
        )
        field[rows, :] = (far_real * keep).astype(jnp.bfloat16)
        field[PATCH + 256 * k : PATCH + 256 * (k + 1), :] = (far_imag * keep).astype(jnp.bfloat16)
    over_rows(right_v)
    if last:
        copies[13].wait()
        core = lax.rem(me[0], 2)
    for k in range(2):
        rows = slice(256 * k, 256 * (k + 1))
        back = jnp.dot(half[rows, :], left_v[...], preferred_element_type=jnp.float32)
        back_real = back[:, :PATCH]
        back_imag = back[:, PATCH:]
        patch_real = patch_v[0, rows, :].astype(jnp.float32)
        patch_imag = patch_v[1, rows, :].astype(jnp.float32)
        term_real = patch_real * back_real + patch_imag * back_imag
        term_imag = patch_real * back_imag - patch_imag * back_real
        if last:
            term_real = term_real + term_v[0, rows, :]
            term_imag = term_imag + term_v[1, rows, :]
            keep_term[rows, :] = jnp.where(core == 0, term_real, term_imag)
            give_term[rows, :] = jnp.where(core == 0, term_imag, term_real)
        else:
            term_out[0, rows, :] = term_real
            term_out[1, rows, :] = term_imag
        term_v[0, rows, :] = back_real
        term_v[1, rows, :] = back_imag

    def weigh(i, carry):
        at = pl.multiple_of(i * CHUNK, CHUNK)
        rows = pl.ds(at, CHUNK)
        again = pl.ds(pl.multiple_of(at + PATCH, CHUNK), CHUNK)
        probe_real = probe_v[0, rows, :]
        probe_imag = probe_v[1, rows, :]
        back_real = term_v[0, rows, :]
        back_imag = term_v[1, rows, :]
        grad_real = probe_real * back_real + probe_imag * back_imag
        grad_imag = probe_real * back_imag - probe_imag * back_real
        twice[0, rows, :] = grad_real
        twice[0, again, :] = grad_real
        twice[1, rows, :] = grad_imag
        twice[1, again, :] = grad_imag
        return carry

    lax.fori_loop(0, PATCH // CHUNK, weigh, 0)
    classes, height = grad.shape[0], grad.shape[2]

    def spread(k, carry):
        for plane in range(2):
            grad[k, plane] = rows_from(twice, plane, PATCH - down + k * height, height).astype(
                jnp.bfloat16
            )
        return carry

    lax.fori_loop(0, classes, spread, 0)


def wave(which, classes, pos, me, spare, band, sibling, across, probe, amplitudes, tables, term):
    operands = [band, sibling, across, probe, amplitudes, *tables]
    smem = pl.BlockSpec(memory_space=pltpu.SMEM)
    hbm = pl.BlockSpec(memory_space=pl.ANY)
    vmem = pl.BlockSpec(memory_space=pltpu.VMEM)
    planes = (2, PATCH, PATCH)
    plane = jax.ShapeDtypeStruct((PATCH, PATCH), jnp.float32)
    if term is None:
        terms = [jax.ShapeDtypeStruct(planes, jnp.float32)]
    else:
        operands.append(term)
        terms = [plane, plane]
    return pl.pallas_call(
        functools.partial(wave_kernel, which),
        in_specs=[smem, smem, smem] + [hbm] * len(operands),
        out_specs=[vmem] * (1 + len(terms)),
        out_shape=[
            jax.ShapeDtypeStruct((classes, 2, PATCH // classes, PATCH), jnp.bfloat16),
            *terms,
        ],
        scratch_shapes=[
            pltpu.VMEM((2, PATCH, WIDE), jnp.bfloat16),
            pltpu.VMEM(planes, jnp.bfloat16),
            pltpu.VMEM(planes, jnp.bfloat16),
            pltpu.VMEM(planes, jnp.float32),
            pltpu.VMEM((PATCH, PATCH), jnp.bfloat16),
            pltpu.VMEM((2 * PATCH, 2 * PATCH), jnp.bfloat16),
            pltpu.VMEM((2 * PATCH, 2 * PATCH), jnp.bfloat16),
            pltpu.VMEM(planes, jnp.float32),
            pltpu.VMEM(planes, jnp.bfloat16),
            pltpu.VMEM((2, 2 * PATCH + SUBLANES, PATCH), jnp.float32),
            pltpu.VMEM((2 * PATCH, PATCH), jnp.bfloat16),
            pltpu.VMEM((PATCH, 2 * PATCH), jnp.bfloat16),
            pltpu.SemaphoreType.DMA((14,)),
        ],
        compiler_params=pltpu.CompilerParams(vmem_limit_bytes=WAVE_VMEM),
        cost_estimate=pl.CostEstimate(
            flops=32 * PATCH**3, bytes_accessed=14000000, transcendentals=PATCH * PATCH
        ),
    )(pos, me, spare, *operands)


def sum_kernel(pos, me, first, second, own, away, canvas):
    classes, height = first.shape[0], first.shape[2]
    start = me[1] * height
    canvas[...] = jnp.zeros_like(canvas)
    rows = lax.broadcasted_iota(jnp.int32, (2 * height, WIDE), 0)
    rows = start + jnp.where(rows >= height, rows - height, rows)

    def piece(k, source, which):
        index = 2 * k + which
        row_at = first_row(pos, index)
        col_at = first_col(pos, index)
        down = lax.rem(row_at, PATCH)
        at = pl.ds(pl.multiple_of(col_at // LANES * LANES, LANES), WIDE)
        data = source[k].astype(jnp.float32).reshape(2 * height, PATCH)
        data = shifted_right(data, lax.rem(col_at, LANES))

        @pl.when(down < start + height)
        def _():
            canvas[row_at // PATCH, :, at] += jnp.where(rows >= down, data, 0.0)

        @pl.when(down > start)
        def _():
            canvas[row_at // PATCH + 1, :, at] += jnp.where(rows < down, data, 0.0)

    def body(k, carry):
        piece(k, first, 0)
        piece(k, second, 1)
        return carry

    lax.fori_loop(0, classes, body, 0)
    shape = own.shape[1:]
    for k in range(2):
        keep = lax.bitwise_xor(me[0], 2 - 2 * k)
        give = lax.bitwise_xor(me[0], 3 - 2 * k)
        own[k] = canvas[keep].reshape(shape)
        away[k] = canvas[give].reshape(shape).astype(jnp.bfloat16)


def sum_pieces(pos, me, first, second, bands, width):
    height = first.shape[2]
    smem = pl.BlockSpec(memory_space=pltpu.SMEM)
    vmem = pl.BlockSpec(memory_space=pltpu.VMEM)
    shape = (2, 2, height, width)
    return pl.pallas_call(
        sum_kernel,
        in_specs=[smem, smem, vmem, vmem],
        out_specs=[vmem, vmem],
        out_shape=[
            jax.ShapeDtypeStruct(shape, jnp.float32),
            jax.ShapeDtypeStruct(shape, jnp.bfloat16),
        ],
        scratch_shapes=[pltpu.VMEM((bands, 2 * height, width), jnp.float32)],
        compiler_params=pltpu.CompilerParams(vmem_limit_bytes=SUM_VMEM),
        cost_estimate=pl.CostEstimate(
            flops=8 * first.size, bytes_accessed=4 * first.size + 6 * math.prod(shape), transcendentals=0
        ),
    )(pos, me, first, second)


def shards(object_image, probe, amplitudes, pos_tile, pos_offset):
    owners = lax.axis_size("obj")
    classes = lax.axis_size("pat")
    my_owner = lax.axis_index("obj").astype(jnp.int32)
    my_class = lax.axis_index("pat").astype(jnp.int32)
    me = jnp.stack([my_owner, my_class])
    height = PATCH // classes
    width = object_image.shape[2]
    assert owners == 4 and object_image.shape[1] == PATCH and pos_tile.shape[0] == 2

    def flip(value, bit):
        return lax.ppermute(value, "obj", [(k, k ^ bit) for k in range(owners)])

    own_pos = jnp.concatenate([pos_tile, pos_offset], 1)
    pos = lax.all_gather(own_pos, "obj", axis=0, tiled=True)
    pos_pat = lax.all_gather(own_pos, "pat", axis=0, tiled=True)

    relay = [flip(cut(object_image, pos, me, 3, k, 1), 1) for k in range(2)]
    across = [flip(cut_and_merge(object_image, relay[k], pos, me, k), 2) for k in range(2)]
    sibling = flip(cut(object_image, pos, me, 1, 0, 2), 1)

    tables = dft_tables(PATCH)
    operands = (probe, amplitudes, tables)
    grad_0, term = wave(
        0, classes, pos, me, pos_pat, object_image, sibling, across[0], *operands, None
    )
    part_0 = lax.all_to_all(grad_0, "pat", split_axis=0, concat_axis=0, tiled=True)
    grad_1, keep_term, give_term = wave(
        1, classes, pos, me, pos_pat, object_image, sibling, across[1], *operands, term
    )
    grad_1, part_0 = lax.optimization_barrier((grad_1, part_0))
    part_1 = lax.all_to_all(grad_1, "pat", split_axis=0, concat_axis=0, tiled=True)

    own, away = sum_pieces(pos_pat, me, part_0, part_1, owners, width)
    from_sibling_far = flip(away[0], 1)
    from_sibling = flip(away[1], 1)
    from_across = flip(
        (own[0] + from_sibling_far.astype(jnp.float32)).astype(jnp.bfloat16), 2
    )
    total = own[1] + from_sibling.astype(jnp.float32) + from_across.astype(jnp.float32)
    mine = lax.dynamic_slice_in_dim(object_image, my_class * height, height, 1)
    updated = (mine.astype(jnp.float32) - OBJECT_RATE * total).astype(jnp.bfloat16)
    object_next = lax.all_gather(updated, "pat", axis=1, tiled=True)

    core = my_owner % 2
    line = my_owner // 2
    part = keep_term + flip(give_term, 1)

    def halved(part, bit, other):
        rows = part.shape[0] // 2
        give = lax.dynamic_slice_in_dim(part, (1 - bit) * rows, rows, 0)
        return lax.dynamic_slice_in_dim(part, bit * rows, rows, 0) + other(give)

    def doubled(part, bit, other):
        got = other(part)
        return jnp.where(bit == 0, jnp.concatenate([part, got]), jnp.concatenate([got, part]))

    def pat_flip(bit):
        return lambda value: lax.ppermute(value, "pat", [(k, k ^ bit) for k in range(classes)])

    part = halved(part, line, lambda value: flip(value, 2))
    bits = [1 << k for k in range(classes.bit_length() - 1)]
    for bit in bits:
        part = halved(part, my_class // bit % 2, pat_flip(bit))
    for bit in reversed(bits):
        part = doubled(part, my_class // bit % 2, pat_flip(bit))
    part = doubled(part, line, lambda value: flip(value, 2))
    probe_total = doubled(part[None], core, lambda value: flip(value, 1))
    probe_next = probe - PROBE_RATE * probe_total
    return (object_next, probe_next)


def solution(mesh):
    return jax.shard_map(
        shards,
        mesh=mesh,
        in_specs=(
            P(None, "obj", None),
            P(),
            P(("pat", "obj"), None, None),
            P(("pat", "obj"), None),
            P(("pat", "obj"), None),
        ),
        out_specs=(P(None, "obj", None), P()),
        check_vma=False,
    )
```

```python
import functools
import math

import jax
import jax.numpy as jnp
from jax import lax
from jax.experimental import pallas as pl
from jax.experimental.pallas import tpu as pltpu
from jax.sharding import PartitionSpec as P

PATCH = 512
TILE = 256
LANES = 128
WIDE = PATCH + LANES

OBJECT_RATE = 0.1
PROBE_RATE = 0.05
MAGNITUDE_FLOOR = 0.5
ALL_VMEM = 56 * 1024 * 1024
CUT_VMEM = 14 * 1024 * 1024
WAVE_VMEM = 32 * 1024 * 1024
SUM_VMEM = 24 * 1024 * 1024


def dft_tables(counter):
    length = counter.shape[0]
    phase_angle = (counter[:, None] * counter[None, :] % length).astype(jnp.float32) * (
        2.0 * math.pi / length
    )
    factor = 1.0 / math.sqrt(length)
    cosine = (jnp.cos(phase_angle) * factor).astype(jnp.bfloat16)
    sine_part = (-jnp.sin(phase_angle) * factor).astype(jnp.bfloat16)
    return cosine, sine_part, -sine_part


def first_row(pos, index):
    return pos[index, 0] * TILE + pos[index, 2]


def first_col(pos, index):
    return pos[index, 1] * TILE + pos[index, 3]


def shifted_left(blocks, amount):
    turned = [pltpu.roll(b, lax.rem(LANES - amount, LANES), axis=1) for b in blocks]
    lane = lax.broadcasted_iota(jnp.int32, turned[0].shape, 1)
    stay = lane < LANES - amount
    return jnp.concatenate([jnp.where(stay, a, b) for a, b in zip(turned, turned[1:])], 1)


def shifted_right(data, amount):
    count = data.shape[1] // LANES
    turned = [pltpu.roll(data[:, LANES * k : LANES * (k + 1)], amount, axis=1) for k in range(count)]
    lane = lax.broadcasted_iota(jnp.int32, turned[0].shape, 1)
    stay = lane >= amount
    before = [jnp.zeros_like(turned[0])] + turned
    after = turned + [jnp.zeros_like(turned[0])]
    return jnp.concatenate([jnp.where(stay, a, b) for a, b in zip(after, before)], 1)


def band_of_rows(row_at, start, count):
    rows = lax.broadcasted_iota(jnp.int32, (count, PATCH), 0) + start
    return row_at // PATCH + (rows < lax.rem(row_at, PATCH)).astype(jnp.int32)


CHUNK = 64
SUBLANES = 8


def rows_from(ref, plane, start, count):
    aligned = pl.multiple_of(start // SUBLANES * SUBLANES, SUBLANES)
    amount = lax.rem(start, SUBLANES)
    data = ref[plane, pl.ds(aligned, count + SUBLANES), :]
    data = data.reshape(count // SUBLANES + 1, SUBLANES, data.shape[1])
    turned = pltpu.roll(data, lax.rem(SUBLANES - amount, SUBLANES), axis=1)
    row = lax.broadcasted_iota(jnp.int32, turned[1:].shape, 1)
    data = jnp.where(row < SUBLANES - amount, turned[:-1], turned[1:])
    return data.reshape(count, data.shape[2])


def cut_rows(blocks, plane, rows, amount):
    return shifted_left([b[plane, rows, :].astype(jnp.float32) for b in blocks], amount)


def cut_kernel(flip, first, pos, me, *refs):
    blocks, out = refs[:-1], refs[-1]
    target = lax.bitwise_xor(me[0], flip)
    amount = lax.rem(first_col(pos, 2 * target + first + pl.program_id(0)), LANES)

    def body(i, carry):
        rows = pl.ds(pl.multiple_of(i * CHUNK, CHUNK), CHUNK)
        for plane in range(2):
            out[0, plane, rows, :] = cut_rows(blocks, plane, rows, amount).astype(jnp.bfloat16)
        return carry

    lax.fori_loop(0, PATCH // CHUNK, body, 0)


def cut(band, pos, me, flip, first, count, vmem):
    def block(k):
        def index(i, pos, me):
            return (0, 0, first_col(pos, 2 * lax.bitwise_xor(me[0], flip) + first + i) // LANES + k)

        return pl.BlockSpec((2, PATCH, LANES), index)

    return pl.pallas_call(
        functools.partial(cut_kernel, flip, first),
        grid_spec=pltpu.PrefetchScalarGridSpec(
            num_scalar_prefetch=2,
            grid=(count,),
            in_specs=[block(k) for k in range(WIDE // LANES)],
            out_specs=pl.BlockSpec((1, 2, PATCH, PATCH), lambda i, pos, me: (i, 0, 0, 0)),
        ),
        out_shape=jax.ShapeDtypeStruct((count, 2, PATCH, PATCH), jnp.bfloat16),
        compiler_params=pltpu.CompilerParams(vmem_limit_bytes=vmem),
        cost_estimate=pl.CostEstimate(
            flops=count * 2 * PATCH * WIDE, bytes_accessed=count * 2300000, transcendentals=0
        ),
    )(pos, me, *([band] * (WIDE // LANES)))


def merge_kernel(which, pos, me, *refs):
    blocks, sibling, out = refs[:-2], refs[-2], refs[-1]
    index = 2 * lax.bitwise_xor(me[0], 2) + which
    amount = lax.rem(first_col(pos, index), LANES)
    row_at = first_row(pos, index)

    def body(i, carry):
        rows = pl.ds(pl.multiple_of(i * CHUNK, CHUNK), CHUNK)
        mine = band_of_rows(row_at, i * CHUNK, CHUNK) == me[0]
        for plane in range(2):
            own = cut_rows(blocks, plane, rows, amount)
            other = sibling[0, plane, rows, :].astype(jnp.float32)
            out[plane, rows, :] = jnp.where(mine, own, other).astype(jnp.bfloat16)
        return carry

    lax.fori_loop(0, PATCH // CHUNK, body, 0)


def cut_and_merge(band, sibling, pos, me, which):
    def block(k):
        def index(i, pos, me):
            return (0, 0, first_col(pos, 2 * lax.bitwise_xor(me[0], 2) + which) // LANES + k)

        return pl.BlockSpec((2, PATCH, LANES), index)

    return pl.pallas_call(
        functools.partial(merge_kernel, which),
        grid_spec=pltpu.PrefetchScalarGridSpec(
            num_scalar_prefetch=2,
            grid=(1,),
            in_specs=[block(k) for k in range(WIDE // LANES)]
            + [pl.BlockSpec((1, 2, PATCH, PATCH), lambda i, pos, me: (0, 0, 0, 0))],
            out_specs=pl.BlockSpec((2, PATCH, PATCH), lambda i, pos, me: (0, 0, 0)),
        ),
        out_shape=jax.ShapeDtypeStruct((2, PATCH, PATCH), jnp.bfloat16),
        compiler_params=pltpu.CompilerParams(vmem_limit_bytes=CUT_VMEM),
        cost_estimate=pl.CostEstimate(
            flops=2 * PATCH * WIDE, bytes_accessed=3300000, transcendentals=0
        ),
    )(pos, me, *([band] * (WIDE // LANES)), sibling)


def wave_kernel(which, pos, me, band, sibling, across, probe, amplitudes, *refs):
    tables, refs = refs[:3], refs[3:]
    last = which == 1
    if last:
        term_in, grad, keep_term, give_term, *scratch = refs
    else:
        grad, term_out, *scratch = refs
    window, sib_v, far_v, probe_v, amp_v, left_v, right_v, term_v, patch_v, twice, field, half, sems = scratch
    index = 2 * me[0] + which
    col_at = first_col(pos, index)
    row_at = first_row(pos, index)
    start = pl.multiple_of(col_at // LANES * LANES, LANES)
    pairs = [
        (band.at[:, :, pl.ds(start, WIDE)], window),
        (sibling.at[which], sib_v),
        (across, far_v),
        (probe, probe_v),
    ]
    cosine, sine, minus = tables
    quarters = [(slice(0, PATCH), slice(0, PATCH)), (slice(0, PATCH), slice(PATCH, 2 * PATCH))]
    quarters += [(slice(PATCH, 2 * PATCH), slice(0, PATCH)), (slice(PATCH, 2 * PATCH), slice(PATCH, 2 * PATCH))]
    pairs += [(t, left_v.at[q]) for t, q in zip((cosine, minus, sine, cosine), quarters)]
    pairs.append((amplitudes.at[which], amp_v))
    pairs += [(t, right_v.at[q]) for t, q in zip((cosine, sine, minus, cosine), quarters)]
    if last:
        pairs.append((term_in, term_v))
    copies = [pltpu.make_async_copy(a, b, sems.at[k]) for k, (a, b) in enumerate(pairs)]
    for copy in copies:
        copy.start()
    for copy in copies[:3]:
        copy.wait()
    amount = lax.rem(col_at, LANES)
    down = lax.rem(row_at, PATCH)
    views = [window.at[:, :, LANES * k : LANES * (k + 1)] for k in range(WIDE // LANES)]

    def assemble(i, carry):
        at = pl.multiple_of(i * CHUNK, CHUNK)
        rows = pl.ds(at, CHUNK)
        owner = band_of_rows(row_at, at, CHUNK)
        mine = owner == me[0]
        near = owner == lax.bitwise_xor(me[0], 1)
        for plane in range(2):
            own = cut_rows(views, plane, rows, amount)
            beside = sib_v[plane, rows, :].astype(jnp.float32)
            beyond = far_v[plane, rows, :].astype(jnp.float32)
            patch = jnp.where(mine, own, jnp.where(near, beside, beyond))
            twice[plane, rows, :] = patch
            twice[plane, pl.ds(pl.multiple_of(at + PATCH, CHUNK), CHUNK), :] = patch
        return carry

    lax.fori_loop(0, PATCH // CHUNK, assemble, 0)
    copies[3].wait()

    def illuminate(i, carry):
        at = pl.multiple_of(i * CHUNK, CHUNK)
        rows = pl.ds(at, CHUNK)
        patch_real = rows_from(twice, 0, at + down, CHUNK)
        patch_imag = rows_from(twice, 1, at + down, CHUNK)
        patch_v[0, rows, :] = patch_real.astype(jnp.bfloat16)
        patch_v[1, rows, :] = patch_imag.astype(jnp.bfloat16)
        probe_real = probe_v[0, rows, :]
        probe_imag = probe_v[1, rows, :]
        field[rows, :] = (probe_real * patch_real - probe_imag * patch_imag).astype(jnp.bfloat16)
        field[pl.ds(pl.multiple_of(at + PATCH, CHUNK), CHUNK), :] = (
            probe_real * patch_imag + probe_imag * patch_real
        ).astype(jnp.bfloat16)
        return carry

    lax.fori_loop(0, PATCH // CHUNK, illuminate, 0)
    for copy in copies[4:8]:
        copy.wait()

    def over_rows(table):
        for k in range(4):
            part = jnp.dot(
                table[256 * k : 256 * (k + 1), :], field[...], preferred_element_type=jnp.float32
            ).astype(jnp.bfloat16)
            half[256 * (k % 2) : 256 * (k % 2 + 1), PATCH * (k // 2) : PATCH * (k // 2 + 1)] = part

    over_rows(left_v)
    for copy in copies[8:13]:
        copy.wait()
    for k in range(2):
        rows = slice(256 * k, 256 * (k + 1))
        far = jnp.dot(half[rows, :], right_v[...], preferred_element_type=jnp.float32)
        far_real = far[:, :PATCH]
        far_imag = far[:, PATCH:]
        power = far_real * far_real + far_imag * far_imag
        keep = 1.0 - amp_v[rows, :].astype(jnp.float32) * lax.rsqrt(
            jnp.maximum(power, MAGNITUDE_FLOOR * MAGNITUDE_FLOOR)
        )
        field[rows, :] = (far_real * keep).astype(jnp.bfloat16)
        field[PATCH + 256 * k : PATCH + 256 * (k + 1), :] = (far_imag * keep).astype(jnp.bfloat16)
    over_rows(right_v)
    if last:
        copies[13].wait()
        core = lax.rem(me[0], 2)
    for k in range(2):
        rows = slice(256 * k, 256 * (k + 1))
        back = jnp.dot(half[rows, :], left_v[...], preferred_element_type=jnp.float32)
        back_real = back[:, :PATCH]
        back_imag = back[:, PATCH:]
        patch_real = patch_v[0, rows, :].astype(jnp.float32)
        patch_imag = patch_v[1, rows, :].astype(jnp.float32)
        term_real = patch_real * back_real + patch_imag * back_imag
        term_imag = patch_real * back_imag - patch_imag * back_real
        if last:
            term_real = term_real + term_v[0, rows, :]
            term_imag = term_imag + term_v[1, rows, :]
            keep_term[rows, :] = jnp.where(core == 0, term_real, term_imag)
            give_term[rows, :] = jnp.where(core == 0, term_imag, term_real).astype(jnp.bfloat16)
        else:
            term_out[0, rows, :] = term_real
            term_out[1, rows, :] = term_imag
        term_v[0, rows, :] = back_real
        term_v[1, rows, :] = back_imag

    def weigh(i, carry):
        at = pl.multiple_of(i * CHUNK, CHUNK)
        rows = pl.ds(at, CHUNK)
        again = pl.ds(pl.multiple_of(at + PATCH, CHUNK), CHUNK)
        probe_real = probe_v[0, rows, :]
        probe_imag = probe_v[1, rows, :]
        back_real = term_v[0, rows, :]
        back_imag = term_v[1, rows, :]
        grad_real = probe_real * back_real + probe_imag * back_imag
        grad_imag = probe_real * back_imag - probe_imag * back_real
        twice[0, rows, :] = grad_real
        twice[0, again, :] = grad_real
        twice[1, rows, :] = grad_imag
        twice[1, again, :] = grad_imag
        return carry

    lax.fori_loop(0, PATCH // CHUNK, weigh, 0)
    classes, height = grad.shape[0], grad.shape[2]

    def spread(k, carry):
        for plane in range(2):
            grad[k, plane] = rows_from(twice, plane, PATCH - down + k * height, height).astype(
                jnp.bfloat16
            )
        return carry

    lax.fori_loop(0, classes, spread, 0)


def wave(which, classes, pos, me, band, sibling, across, probe, amplitudes, tables, term):
    operands = [band, sibling, across, probe, amplitudes, *tables]
    smem = pl.BlockSpec(memory_space=pltpu.SMEM)
    hbm = pl.BlockSpec(memory_space=pl.ANY)
    vmem = pl.BlockSpec(memory_space=pltpu.VMEM)
    planes = (2, PATCH, PATCH)
    plane = (PATCH, PATCH)
    if term is None:
        terms = [jax.ShapeDtypeStruct(planes, jnp.float32)]
    else:
        operands.append(term)
        terms = [jax.ShapeDtypeStruct(plane, t) for t in (jnp.float32, jnp.bfloat16)]
    return pl.pallas_call(
        functools.partial(wave_kernel, which),
        in_specs=[smem, smem] + [hbm] * len(operands),
        out_specs=[vmem] * (1 + len(terms)),
        out_shape=[
            jax.ShapeDtypeStruct((classes, 2, PATCH // classes, PATCH), jnp.bfloat16),
            *terms,
        ],
        scratch_shapes=[
            pltpu.VMEM((2, PATCH, WIDE), jnp.bfloat16),
            pltpu.VMEM(planes, jnp.bfloat16),
            pltpu.VMEM(planes, jnp.bfloat16),
            pltpu.VMEM(planes, jnp.float32),
            pltpu.VMEM((PATCH, PATCH), jnp.bfloat16),
            pltpu.VMEM((2 * PATCH, 2 * PATCH), jnp.bfloat16),
            pltpu.VMEM((2 * PATCH, 2 * PATCH), jnp.bfloat16),
            pltpu.VMEM(planes, jnp.float32),
            pltpu.VMEM(planes, jnp.bfloat16),
            pltpu.VMEM((2, 2 * PATCH + SUBLANES, PATCH), jnp.float32),
            pltpu.VMEM((2 * PATCH, PATCH), jnp.bfloat16),
            pltpu.VMEM((PATCH, 2 * PATCH), jnp.bfloat16),
            pltpu.SemaphoreType.DMA((14,)),
        ],
        compiler_params=pltpu.CompilerParams(vmem_limit_bytes=WAVE_VMEM),
        cost_estimate=pl.CostEstimate(
            flops=PATCH**2, bytes_accessed=PATCH**2, transcendentals=0
        ),
    )(pos, me, *operands)


def sum_kernel(pos, me, first, second, own, away, canvas):
    classes, height = first.shape[0], first.shape[2]
    start = me[1] * height
    canvas[...] = jnp.zeros_like(canvas)
    rows = lax.broadcasted_iota(jnp.int32, (2 * height, WIDE), 0)
    rows = start + jnp.where(rows >= height, rows - height, rows)

    def piece(k, source, which):
        index = 2 * k + which
        row_at = first_row(pos, index)
        col_at = first_col(pos, index)
        down = lax.rem(row_at, PATCH)
        at = pl.ds(pl.multiple_of(col_at // LANES * LANES, LANES), WIDE)
        data = source[k].astype(jnp.float32).reshape(2 * height, PATCH)
        data = shifted_right(data, lax.rem(col_at, LANES))

        @pl.when(down < start + height)
        def _():
            canvas[row_at // PATCH, :, at] += jnp.where(rows >= down, data, 0.0)

        @pl.when(down > start)
        def _():
            canvas[row_at // PATCH + 1, :, at] += jnp.where(rows < down, data, 0.0)

    def body(k, carry):
        piece(k, first, 0)
        piece(k, second, 1)
        return carry

    lax.fori_loop(0, classes, body, 0)
    shape = own.shape[1:]
    for k in range(2):
        keep = lax.bitwise_xor(me[0], 2 - 2 * k)
        give = lax.bitwise_xor(me[0], 3 - 2 * k)
        own[k] = canvas[keep].reshape(shape)
        away[k] = canvas[give].reshape(shape).astype(jnp.bfloat16)


def sum_pieces(pos, me, first, second, bands, width):
    height = first.shape[2]
    smem = pl.BlockSpec(memory_space=pltpu.SMEM)
    vmem = pl.BlockSpec(memory_space=pltpu.VMEM)
    shape = (2, 2, height, width)
    return pl.pallas_call(
        sum_kernel,
        in_specs=[smem, smem, vmem, vmem],
        out_specs=[vmem, vmem],
        out_shape=[
            jax.ShapeDtypeStruct(shape, jnp.float32),
            jax.ShapeDtypeStruct(shape, jnp.bfloat16),
        ],
        scratch_shapes=[pltpu.VMEM((bands, 2 * height, width), jnp.float32)],
        compiler_params=pltpu.CompilerParams(vmem_limit_bytes=SUM_VMEM),
        cost_estimate=pl.CostEstimate(
            flops=8 * first.size, bytes_accessed=4 * first.size + 6 * math.prod(shape), transcendentals=0
        ),
    )(pos, me, first, second)


def shards(object_image, probe, amplitudes, pos_tile, pos_offset):
    owners = lax.axis_size("obj")
    classes = lax.axis_size("pat")
    my_owner = lax.axis_index("obj").astype(jnp.int32)
    my_class = lax.axis_index("pat").astype(jnp.int32)
    me = jnp.stack([my_owner, my_class])
    height = PATCH // classes
    width = object_image.shape[2]
    assert owners == 4 and object_image.shape[1] == PATCH and pos_tile.shape[0] == 2

    def flip(value, bit):
        return lax.ppermute(value, "obj", [(k, k ^ bit) for k in range(owners)])

    def pat_flip(bit):
        return lambda value: lax.ppermute(value, "pat", [(k, k ^ bit) for k in range(classes)])

    def halved(part, bit, other):
        rows = part.shape[0] // 2
        give = lax.dynamic_slice_in_dim(part, (1 - bit) * rows, rows, 0).astype(jnp.bfloat16)
        return lax.dynamic_slice_in_dim(part, bit * rows, rows, 0) + other(give).astype(jnp.float32)

    def doubled(part, bit, other):
        got = other(part)
        return jnp.where(bit == 0, jnp.concatenate([part, got]), jnp.concatenate([got, part]))

    bits = [1 << k for k in range(classes.bit_length() - 1)]
    own_pos = jnp.concatenate([pos_tile, pos_offset], 1)
    pos = lax.all_gather(own_pos, "obj", axis=0, tiled=True)

    relay = [flip(cut(object_image, pos, me, 3, k, 1, ALL_VMEM), 1) for k in range(2)]
    merged = [cut_and_merge(object_image, relay[k], pos, me, k) for k in range(2)]
    counter = jnp.arange(PATCH, dtype=jnp.int32)
    merged[1], counter, pos_pat = lax.optimization_barrier((merged[1], counter, own_pos))
    across = [flip(m, 2) for m in merged]
    sibling = flip(cut(object_image, pos, me, 1, 0, 2, CUT_VMEM), 1)
    for bit in bits:
        pos_pat = doubled(pos_pat, my_class // bit % 2, pat_flip(bit))

    operands = (probe, amplitudes, dft_tables(counter))
    grad_0, term = wave(0, classes, pos, me, object_image, sibling, across[0], *operands, None)
    part_0 = lax.all_to_all(grad_0, "pat", split_axis=0, concat_axis=0, tiled=True)
    grad_1, keep_term, give_term = wave(
        1, classes, pos, me, object_image, sibling, across[1], *operands, term
    )
    grad_1, part_0 = lax.optimization_barrier((grad_1, part_0))
    part_1 = lax.all_to_all(grad_1, "pat", split_axis=0, concat_axis=0, tiled=True)

    own, away = sum_pieces(pos_pat, me, part_0, part_1, owners, width)
    from_sibling_far = flip(away[0], 1)
    from_sibling = flip(away[1], 1)
    from_across = flip(
        (own[0] + from_sibling_far.astype(jnp.float32)).astype(jnp.bfloat16), 2
    )
    total = own[1] + from_sibling.astype(jnp.float32) + from_across.astype(jnp.float32)
    mine = lax.dynamic_slice_in_dim(object_image, my_class * height, height, 1)
    updated = (mine.astype(jnp.float32) - OBJECT_RATE * total).astype(jnp.bfloat16)
    object_next = lax.all_gather(updated, "pat", axis=1, tiled=True)

    core = my_owner % 2
    line = my_owner // 2
    part = keep_term + flip(give_term, 1).astype(jnp.float32)
    part = halved(part, line, lambda value: flip(value, 2))
    for bit in bits:
        part = halved(part, my_class // bit % 2, pat_flip(bit))
    part = part.astype(jnp.bfloat16)
    for bit in reversed(bits):
        part = doubled(part, my_class // bit % 2, pat_flip(bit))
    part = doubled(part, line, lambda value: flip(value, 2))
    probe_total = doubled(part[None], core, lambda value: flip(value, 1)).astype(jnp.float32)
    probe_next = probe - PROBE_RATE * probe_total
    return (object_next, probe_next)


def solution(mesh):
    return jax.shard_map(
        shards,
        mesh=mesh,
        in_specs=(
            P(None, "obj", None),
            P(),
            P(("pat", "obj"), None, None),
            P(("pat", "obj"), None),
            P(("pat", "obj"), None),
        ),
        out_specs=(P(None, "obj", None), P()),
        check_vma=False,
    )
```

```python
import functools
import math

import jax
import jax.numpy as jnp
import numpy as np
from jax import lax
from jax.experimental import pallas as pl
from jax.experimental.pallas import tpu as pltpu
from jax.sharding import PartitionSpec as P

PATCH = 512
TILE = 256
LANES = 128
WIDE = PATCH + LANES

OBJECT_RATE = 0.1
PROBE_RATE = 0.05
MAGNITUDE_FLOOR = 0.5
CUT_VMEM = 14 * 1024 * 1024
WAVE_VMEM = 32 * 1024 * 1024
SUM_VMEM = 24 * 1024 * 1024
BY_PERMUTE = (4, 8)


def dft_tables(length):
    counter = np.arange(length, dtype=np.int32)
    phase_angle = (counter[:, None] * counter[None, :] % length).astype(np.float32) * np.float32(
        2.0 * math.pi / length
    )
    factor = np.float32(1.0 / math.sqrt(length))
    cosine = (np.cos(phase_angle) * factor).astype(jnp.bfloat16)
    sine_part = (-np.sin(phase_angle) * factor).astype(jnp.bfloat16)
    return jnp.asarray(cosine), jnp.asarray(sine_part), jnp.asarray(-sine_part)


def first_row(pos, index):
    return pos[index, 0] * TILE + pos[index, 2]


def first_col(pos, index):
    return pos[index, 1] * TILE + pos[index, 3]


def shifted_left(blocks, amount):
    turned = [pltpu.roll(b, lax.rem(LANES - amount, LANES), axis=1) for b in blocks]
    lane = lax.broadcasted_iota(jnp.int32, turned[0].shape, 1)
    stay = lane < LANES - amount
    return jnp.concatenate([jnp.where(stay, a, b) for a, b in zip(turned, turned[1:])], 1)


def shifted_right(data, amount):
    count = data.shape[1] // LANES
    turned = [pltpu.roll(data[:, LANES * k : LANES * (k + 1)], amount, axis=1) for k in range(count)]
    lane = lax.broadcasted_iota(jnp.int32, turned[0].shape, 1)
    stay = lane >= amount
    before = [jnp.zeros_like(turned[0])] + turned
    after = turned + [jnp.zeros_like(turned[0])]
    return jnp.concatenate([jnp.where(stay, a, b) for a, b in zip(after, before)], 1)


def band_of_rows(row_at, start, count):
    rows = lax.broadcasted_iota(jnp.int32, (count, PATCH), 0) + start
    return row_at // PATCH + (rows < lax.rem(row_at, PATCH)).astype(jnp.int32)


CHUNK = 64
SUBLANES = 8


def rows_from(ref, plane, start, count):
    aligned = pl.multiple_of(start // SUBLANES * SUBLANES, SUBLANES)
    amount = lax.rem(start, SUBLANES)
    data = ref[plane, pl.ds(aligned, count + SUBLANES), :]
    data = data.reshape(count // SUBLANES + 1, SUBLANES, data.shape[1])
    turned = pltpu.roll(data, lax.rem(SUBLANES - amount, SUBLANES), axis=1)
    row = lax.broadcasted_iota(jnp.int32, turned[1:].shape, 1)
    data = jnp.where(row < SUBLANES - amount, turned[:-1], turned[1:])
    return data.reshape(count, data.shape[2])


def cut_rows(blocks, plane, rows, amount):
    return shifted_left([b[plane, rows, :].astype(jnp.float32) for b in blocks], amount)


def cut_kernel(flip, first, pos, me, *refs):
    blocks, out = refs[:-1], refs[-1]
    target = lax.bitwise_xor(me[0], flip)
    amount = lax.rem(first_col(pos, 2 * target + first + pl.program_id(0)), LANES)

    def body(i, carry):
        rows = pl.ds(pl.multiple_of(i * CHUNK, CHUNK), CHUNK)
        for plane in range(2):
            out[0, plane, rows, :] = cut_rows(blocks, plane, rows, amount).astype(jnp.bfloat16)
        return carry

    lax.fori_loop(0, PATCH // CHUNK, body, 0)


def cut(band, pos, me, flip, first, count):
    def block(k):
        def index(i, pos, me):
            return (0, 0, first_col(pos, 2 * lax.bitwise_xor(me[0], flip) + first + i) // LANES + k)

        return pl.BlockSpec((2, PATCH, LANES), index)

    return pl.pallas_call(
        functools.partial(cut_kernel, flip, first),
        grid_spec=pltpu.PrefetchScalarGridSpec(
            num_scalar_prefetch=2,
            grid=(count,),
            in_specs=[block(k) for k in range(WIDE // LANES)],
            out_specs=pl.BlockSpec((1, 2, PATCH, PATCH), lambda i, pos, me: (i, 0, 0, 0)),
        ),
        out_shape=jax.ShapeDtypeStruct((count, 2, PATCH, PATCH), jnp.bfloat16),
        compiler_params=pltpu.CompilerParams(vmem_limit_bytes=CUT_VMEM),
        cost_estimate=pl.CostEstimate(
            flops=count * 2 * PATCH * WIDE, bytes_accessed=count * 2300000, transcendentals=0
        ),
    )(pos, me, *([band] * (WIDE // LANES)))


def merge_kernel(which, pos, me, *refs):
    blocks, sibling, out = refs[:-2], refs[-2], refs[-1]
    index = 2 * lax.bitwise_xor(me[0], 2) + which
    amount = lax.rem(first_col(pos, index), LANES)
    row_at = first_row(pos, index)

    def body(i, carry):
        rows = pl.ds(pl.multiple_of(i * CHUNK, CHUNK), CHUNK)
        mine = band_of_rows(row_at, i * CHUNK, CHUNK) == me[0]
        for plane in range(2):
            own = cut_rows(blocks, plane, rows, amount)
            other = sibling[0, plane, rows, :].astype(jnp.float32)
            out[plane, rows, :] = jnp.where(mine, own, other).astype(jnp.bfloat16)
        return carry

    lax.fori_loop(0, PATCH // CHUNK, body, 0)


def cut_and_merge(band, sibling, pos, me, which):
    def block(k):
        def index(i, pos, me):
            return (0, 0, first_col(pos, 2 * lax.bitwise_xor(me[0], 2) + which) // LANES + k)

        return pl.BlockSpec((2, PATCH, LANES), index)

    return pl.pallas_call(
        functools.partial(merge_kernel, which),
        grid_spec=pltpu.PrefetchScalarGridSpec(
            num_scalar_prefetch=2,
            grid=(1,),
            in_specs=[block(k) for k in range(WIDE // LANES)]
            + [pl.BlockSpec((1, 2, PATCH, PATCH), lambda i, pos, me: (0, 0, 0, 0))],
            out_specs=pl.BlockSpec((2, PATCH, PATCH), lambda i, pos, me: (0, 0, 0)),
        ),
        out_shape=jax.ShapeDtypeStruct((2, PATCH, PATCH), jnp.bfloat16),
        compiler_params=pltpu.CompilerParams(vmem_limit_bytes=CUT_VMEM),
        cost_estimate=pl.CostEstimate(
            flops=2 * PATCH * WIDE, bytes_accessed=3300000, transcendentals=0
        ),
    )(pos, me, *([band] * (WIDE // LANES)), sibling)


def rest_index(step, pos, me):
    return jnp.where(step == 0, 2 * lax.bitwise_xor(me[0], 3) + 1, 2 * lax.bitwise_xor(me[0], 1) + step - 1)


def rest_kernel(pos, me, *refs):
    blocks, second, pieces = refs[:-2], refs[-2], refs[-1]
    step = pl.program_id(0)
    amount = lax.rem(first_col(pos, rest_index(step, pos, me)), LANES)

    def take(out):
        def body(i, carry):
            rows = pl.ds(pl.multiple_of(i * CHUNK, CHUNK), CHUNK)
            for plane in range(2):
                out[0, plane, rows, :] = cut_rows(blocks, plane, rows, amount).astype(jnp.bfloat16)
            return carry

        lax.fori_loop(0, PATCH // CHUNK, body, 0)

    pl.when(step == 0)(lambda: take(second))
    pl.when(step > 0)(lambda: take(pieces))


def cut_rest(band, pos, me):
    def block(k):
        def index(i, pos, me):
            return (0, 0, first_col(pos, rest_index(i, pos, me)) // LANES + k)

        return pl.BlockSpec((2, PATCH, LANES), index)

    shape = (2, PATCH, PATCH)
    return pl.pallas_call(
        rest_kernel,
        grid_spec=pltpu.PrefetchScalarGridSpec(
            num_scalar_prefetch=2,
            grid=(3,),
            in_specs=[block(k) for k in range(WIDE // LANES)],
            out_specs=[
                pl.BlockSpec((1, *shape), lambda i, pos, me: (0, 0, 0, 0)),
                pl.BlockSpec((1, *shape), lambda i, pos, me: (jnp.maximum(i - 1, 0), 0, 0, 0)),
            ],
        ),
        out_shape=[
            jax.ShapeDtypeStruct((1, *shape), jnp.bfloat16),
            jax.ShapeDtypeStruct((2, *shape), jnp.bfloat16),
        ],
        compiler_params=pltpu.CompilerParams(vmem_limit_bytes=CUT_VMEM),
        cost_estimate=pl.CostEstimate(
            flops=6 * PATCH * WIDE, bytes_accessed=7000000, transcendentals=0
        ),
    )(pos, me, *([band] * (WIDE // LANES)))


def wave_kernel(which, pos, me, spare, band, sibling, across, probe, amplitudes, *refs):
    tables, refs = refs[:3], refs[3:]
    last = which == 1
    if last:
        term_in, grad, keep_term, give_term, *scratch = refs
    else:
        grad, term_out, *scratch = refs
    window, sib_v, far_v, probe_v, amp_v, left_v, right_v, term_v, patch_v, twice, field, half, sems = scratch
    index = 2 * me[0] + which
    col_at = first_col(pos, index)
    row_at = first_row(pos, index)
    start = pl.multiple_of(col_at // LANES * LANES, LANES)
    pairs = [
        (band.at[:, :, pl.ds(start, WIDE)], window),
        (sibling.at[which], sib_v),
        (across, far_v),
        (probe, probe_v),
    ]
    cosine, sine, minus = tables
    quarters = [(slice(0, PATCH), slice(0, PATCH)), (slice(0, PATCH), slice(PATCH, 2 * PATCH))]
    quarters += [(slice(PATCH, 2 * PATCH), slice(0, PATCH)), (slice(PATCH, 2 * PATCH), slice(PATCH, 2 * PATCH))]
    pairs += [(t, left_v.at[q]) for t, q in zip((cosine, minus, sine, cosine), quarters)]
    pairs.append((amplitudes.at[which], amp_v))
    pairs += [(t, right_v.at[q]) for t, q in zip((cosine, sine, minus, cosine), quarters)]
    if last:
        pairs.append((term_in, term_v))
    copies = [pltpu.make_async_copy(a, b, sems.at[k]) for k, (a, b) in enumerate(pairs)]
    for copy in copies:
        copy.start()
    for copy in copies[:3]:
        copy.wait()
    amount = lax.rem(col_at, LANES)
    down = lax.rem(row_at, PATCH)
    views = [window.at[:, :, LANES * k : LANES * (k + 1)] for k in range(WIDE // LANES)]

    def assemble(i, carry):
        at = pl.multiple_of(i * CHUNK, CHUNK)
        rows = pl.ds(at, CHUNK)
        owner = band_of_rows(row_at, at, CHUNK)
        mine = owner == me[0]
        near = owner == lax.bitwise_xor(me[0], 1)
        for plane in range(2):
            own = cut_rows(views, plane, rows, amount)
            beside = sib_v[plane, rows, :].astype(jnp.float32)
            beyond = far_v[plane, rows, :].astype(jnp.float32)
            patch = jnp.where(mine, own, jnp.where(near, beside, beyond))
            twice[plane, rows, :] = patch
            twice[plane, pl.ds(pl.multiple_of(at + PATCH, CHUNK), CHUNK), :] = patch
        return carry

    lax.fori_loop(0, PATCH // CHUNK, assemble, 0)
    copies[3].wait()

    def illuminate(i, carry):
        at = pl.multiple_of(i * CHUNK, CHUNK)
        rows = pl.ds(at, CHUNK)
        patch_real = rows_from(twice, 0, at + down, CHUNK)
        patch_imag = rows_from(twice, 1, at + down, CHUNK)
        patch_v[0, rows, :] = patch_real.astype(jnp.bfloat16)
        patch_v[1, rows, :] = patch_imag.astype(jnp.bfloat16)
        probe_real = probe_v[0, rows, :]
        probe_imag = probe_v[1, rows, :]
        field[rows, :] = (probe_real * patch_real - probe_imag * patch_imag).astype(jnp.bfloat16)
        field[pl.ds(pl.multiple_of(at + PATCH, CHUNK), CHUNK), :] = (
            probe_real * patch_imag + probe_imag * patch_real
        ).astype(jnp.bfloat16)
        return carry

    lax.fori_loop(0, PATCH // CHUNK, illuminate, 0)
    for copy in copies[4:8]:
        copy.wait()

    def over_rows(table):
        for k in range(4):
            part = jnp.dot(
                table[256 * k : 256 * (k + 1), :], field[...], preferred_element_type=jnp.float32
            ).astype(jnp.bfloat16)
            half[256 * (k % 2) : 256 * (k % 2 + 1), PATCH * (k // 2) : PATCH * (k // 2 + 1)] = part

    over_rows(left_v)
    for copy in copies[8:13]:
        copy.wait()
    for k in range(2):
        rows = slice(256 * k, 256 * (k + 1))
        far = jnp.dot(half[rows, :], right_v[...], preferred_element_type=jnp.float32)
        far_real = far[:, :PATCH]
        far_imag = far[:, PATCH:]
        power = far_real * far_real + far_imag * far_imag
        keep = 1.0 - amp_v[rows, :].astype(jnp.float32) * lax.rsqrt(
            jnp.maximum(power, MAGNITUDE_FLOOR * MAGNITUDE_FLOOR)
        )
        field[rows, :] = (far_real * keep).astype(jnp.bfloat16)
        field[PATCH + 256 * k : PATCH + 256 * (k + 1), :] = (far_imag * keep).astype(jnp.bfloat16)
    over_rows(right_v)
    if last:
        copies[13].wait()
        core = lax.rem(me[0], 2)
    for k in range(2):
        rows = slice(256 * k, 256 * (k + 1))
        back = jnp.dot(half[rows, :], left_v[...], preferred_element_type=jnp.float32)
        back_real = back[:, :PATCH]
        back_imag = back[:, PATCH:]
        patch_real = patch_v[0, rows, :].astype(jnp.float32)
        patch_imag = patch_v[1, rows, :].astype(jnp.float32)
        term_real = patch_real * back_real + patch_imag * back_imag
        term_imag = patch_real * back_imag - patch_imag * back_real
        if last:
            term_real = term_real + term_v[0, rows, :]
            term_imag = term_imag + term_v[1, rows, :]
            keep_term[rows, :] = jnp.where(core == 0, term_real, term_imag)
            give_term[rows, :] = jnp.where(core == 0, term_imag, term_real).astype(jnp.bfloat16)
        else:
            term_out[0, rows, :] = term_real
            term_out[1, rows, :] = term_imag
        term_v[0, rows, :] = back_real
        term_v[1, rows, :] = back_imag

    def weigh(i, carry):
        at = pl.multiple_of(i * CHUNK, CHUNK)
        rows = pl.ds(at, CHUNK)
        again = pl.ds(pl.multiple_of(at + PATCH, CHUNK), CHUNK)
        probe_real = probe_v[0, rows, :]
        probe_imag = probe_v[1, rows, :]
        back_real = term_v[0, rows, :]
        back_imag = term_v[1, rows, :]
        grad_real = probe_real * back_real + probe_imag * back_imag
        grad_imag = probe_real * back_imag - probe_imag * back_real
        twice[0, rows, :] = grad_real
        twice[0, again, :] = grad_real
        twice[1, rows, :] = grad_imag
        twice[1, again, :] = grad_imag
        return carry

    lax.fori_loop(0, PATCH // CHUNK, weigh, 0)
    classes, height = grad.shape[0], grad.shape[2]

    def spread(k, carry):
        for plane in range(2):
            grad[k, plane] = rows_from(twice, plane, PATCH - down + k * height, height).astype(
                jnp.bfloat16
            )
        return carry

    lax.fori_loop(0, classes, spread, 0)


def wave(which, classes, pos, me, spare, band, sibling, across, probe, amplitudes, tables, term):
    operands = [band, sibling, across, probe, amplitudes, *tables]
    smem = pl.BlockSpec(memory_space=pltpu.SMEM)
    hbm = pl.BlockSpec(memory_space=pl.ANY)
    vmem = pl.BlockSpec(memory_space=pltpu.VMEM)
    planes = (2, PATCH, PATCH)
    plane = (PATCH, PATCH)
    if term is None:
        terms = [jax.ShapeDtypeStruct(planes, jnp.float32)]
    else:
        operands.append(term)
        terms = [jax.ShapeDtypeStruct(plane, t) for t in (jnp.float32, jnp.bfloat16)]
    return pl.pallas_call(
        functools.partial(wave_kernel, which),
        in_specs=[smem, smem, smem] + [hbm] * len(operands),
        out_specs=[vmem] * (1 + len(terms)),
        out_shape=[
            jax.ShapeDtypeStruct((classes, 2, PATCH // classes, PATCH), jnp.bfloat16),
            *terms,
        ],
        scratch_shapes=[
            pltpu.VMEM((2, PATCH, WIDE), jnp.bfloat16),
            pltpu.VMEM(planes, jnp.bfloat16),
            pltpu.VMEM(planes, jnp.bfloat16),
            pltpu.VMEM(planes, jnp.float32),
            pltpu.VMEM((PATCH, PATCH), jnp.bfloat16),
            pltpu.VMEM((2 * PATCH, 2 * PATCH), jnp.bfloat16),
            pltpu.VMEM((2 * PATCH, 2 * PATCH), jnp.bfloat16),
            pltpu.VMEM(planes, jnp.float32),
            pltpu.VMEM(planes, jnp.bfloat16),
            pltpu.VMEM((2, 2 * PATCH + SUBLANES, PATCH), jnp.float32),
            pltpu.VMEM((2 * PATCH, PATCH), jnp.bfloat16),
            pltpu.VMEM((PATCH, 2 * PATCH), jnp.bfloat16),
            pltpu.SemaphoreType.DMA((14,)),
        ],
        compiler_params=pltpu.CompilerParams(vmem_limit_bytes=WAVE_VMEM),
        cost_estimate=pl.CostEstimate(
            flops=32 * PATCH**3, bytes_accessed=100_000_000, transcendentals=0
        ),
    )(pos, me, spare, *operands)


def sum_kernel(pos, me, first, second, own, away, canvas):
    classes, height = first.shape[0], first.shape[2]
    start = me[1] * height
    canvas[...] = jnp.zeros_like(canvas)
    rows = lax.broadcasted_iota(jnp.int32, (2 * height, WIDE), 0)
    rows = start + jnp.where(rows >= height, rows - height, rows)

    def piece(k, source, which):
        index = 2 * k + which
        row_at = first_row(pos, index)
        col_at = first_col(pos, index)
        down = lax.rem(row_at, PATCH)
        at = pl.ds(pl.multiple_of(col_at // LANES * LANES, LANES), WIDE)
        data = source[k].astype(jnp.float32).reshape(2 * height, PATCH)
        data = shifted_right(data, lax.rem(col_at, LANES))

        @pl.when(down < start + height)
        def _():
            canvas[row_at // PATCH, :, at] += jnp.where(rows >= down, data, 0.0)

        @pl.when(down > start)
        def _():
            canvas[row_at // PATCH + 1, :, at] += jnp.where(rows < down, data, 0.0)

    def body(k, carry):
        piece(k, first, 0)
        piece(k, second, 1)
        return carry

    lax.fori_loop(0, classes, body, 0)
    shape = own.shape[1:]
    for k in range(2):
        keep = lax.bitwise_xor(me[0], 2 - 2 * k)
        give = lax.bitwise_xor(me[0], 3 - 2 * k)
        own[k] = canvas[keep].reshape(shape)
        away[k] = canvas[give].reshape(shape).astype(jnp.bfloat16)


def sum_pieces(pos, me, first, second, bands, width):
    height = first.shape[2]
    smem = pl.BlockSpec(memory_space=pltpu.SMEM)
    vmem = pl.BlockSpec(memory_space=pltpu.VMEM)
    shape = (2, 2, height, width)
    return pl.pallas_call(
        sum_kernel,
        in_specs=[smem, smem, vmem, vmem],
        out_specs=[vmem, vmem],
        out_shape=[
            jax.ShapeDtypeStruct(shape, jnp.float32),
            jax.ShapeDtypeStruct(shape, jnp.bfloat16),
        ],
        scratch_shapes=[pltpu.VMEM((bands, 2 * height, width), jnp.float32)],
        compiler_params=pltpu.CompilerParams(vmem_limit_bytes=SUM_VMEM),
        cost_estimate=pl.CostEstimate(
            flops=8 * first.size, bytes_accessed=4 * first.size + 6 * math.prod(shape), transcendentals=0
        ),
    )(pos, me, first, second)


def assemble_kernel(length, me, *refs):
    steps = length - 1
    own, refs = refs[0], refs[1:]
    ups, downs, overs = refs[:steps], refs[steps : 2 * steps], refs[2 * steps : 3 * steps + 1]
    out, sems = refs[3 * steps + 1 :]
    height = own.shape[1]
    place = me[1] // 2
    side = lax.rem(me[1], 2)

    def copy(source, at, column, k):
        rows = pl.ds(pl.multiple_of((2 * at + column) * height, height), height)
        return pltpu.make_async_copy(source, out.at[:, rows, :], sems.at[k])

    always = [copy(own, place, side, 0)]
    for k in range(length):
        always.append(copy(overs[k], sent_over(place, k, length), 1 - side, k + 1))
    some = []
    for k in range(1, length):
        below, above = place - k, place + k
        held = length + 2 * k - 1
        some.append((below >= 0, copy(ups[k - 1], below, side, held)))
        some.append((above < length, copy(downs[k - 1], above, side, held + 1)))
    for part in always:
        part.start()
    for has, part in some:
        pl.when(has)(part.start)
    for part in always:
        part.wait()
    for has, part in some:
        pl.when(has)(part.wait)


def sent_over(place, k, length):
    low = jnp.where(place >= k, place - k, place + k)
    if k == length - 1:
        high = jnp.where(place == 0, length - 1, jnp.where(place == length - 1, 0, place + 1))
        return high
    return low


def gather_classes(own, me, classes, term, term_steps):
    length = classes // 2
    place = me[1] // 2

    def along(value, held, step):
        pairs = [(2 * z + x, 2 * (z + step) + x) for z in held if 0 <= z + step < length for x in range(2)]
        return lax.ppermute(value, "pat", pairs)

    def over(value):
        return lax.ppermute(value, "pat", [(k, k ^ 1) for k in range(classes)])

    ups, downs, overs = [own], [own], []
    for k in range(length - 1):
        overs.append(over(jnp.where(place >= k, ups[k], downs[k]) if k else own))
        ups.append(along(ups[k], range(k, length), 1))
        downs.append(along(downs[k], range(length - k), -1))
        for step in term_steps[k : k + 1] if k < length - 2 else term_steps[k:-1]:
            term = step(term)
        overs[k], ups[k + 1], downs[k + 1], term = lax.optimization_barrier(
            (overs[k], ups[k + 1], downs[k + 1], term)
        )
    end = jnp.where(place == 0, downs[-1], ups[-1])
    if length > 2:
        middle = (place > 0) & (place < length - 1)
        end = jnp.where(middle, downs[1], end)
    last, term = lax.optimization_barrier((over(end), term_steps[-1](term)))
    overs.append(last)
    operands = [own, *ups[1:], *downs[1:], *overs]
    hbm = pl.BlockSpec(memory_space=pl.ANY)
    object_next = pl.pallas_call(
        functools.partial(assemble_kernel, length),
        in_specs=[pl.BlockSpec(memory_space=pltpu.SMEM)] + [hbm] * len(operands),
        out_specs=hbm,
        out_shape=jax.ShapeDtypeStruct((2, classes * own.shape[1], own.shape[2]), own.dtype),
        scratch_shapes=[pltpu.SemaphoreType.DMA((3 * length - 1,))],
        compiler_params=pltpu.CompilerParams(vmem_limit_bytes=CUT_VMEM),
        cost_estimate=pl.CostEstimate(
            flops=0, bytes_accessed=4 * own.size * classes, transcendentals=0
        ),
    )(me, *operands)
    return object_next, term


def shards(object_image, probe, amplitudes, pos_tile, pos_offset):
    owners = lax.axis_size("obj")
    classes = lax.axis_size("pat")
    my_owner = lax.axis_index("obj").astype(jnp.int32)
    my_class = lax.axis_index("pat").astype(jnp.int32)
    me = jnp.stack([my_owner, my_class])
    height = PATCH // classes
    width = object_image.shape[2]
    assert owners == 4 and object_image.shape[1] == PATCH and pos_tile.shape[0] == 2

    def flip(value, bit):
        return lax.ppermute(value, "obj", [(k, k ^ bit) for k in range(owners)])

    def pat_flip(bit):
        return lambda value: lax.ppermute(value, "pat", [(k, k ^ bit) for k in range(classes)])

    def halved(part, bit, other):
        rows = part.shape[0] // 2
        give = lax.dynamic_slice_in_dim(part, (1 - bit) * rows, rows, 0).astype(jnp.bfloat16)
        return lax.dynamic_slice_in_dim(part, bit * rows, rows, 0) + other(give).astype(jnp.float32)

    def doubled(part, bit, other):
        got = other(part)
        return jnp.where(bit == 0, jnp.concatenate([part, got]), jnp.concatenate([got, part]))

    bits = [1 << k for k in range(classes.bit_length() - 1)]
    own_pos = jnp.concatenate([pos_tile, pos_offset], 1)
    pos = lax.all_gather(own_pos, "obj", axis=0, tiled=True)

    first = cut(object_image, pos, me, 3, 0, 1)
    second, pieces = cut_rest(object_image, pos, me)
    second, pieces, then = lax.optimization_barrier((second, pieces, me))
    relay = [flip(first, 1), flip(second, 1)]
    sibling = flip(pieces, 1)
    merged = [cut_and_merge(object_image, relay[k], pos, then, k) for k in range(2)]
    merged[1], pos_pat = lax.optimization_barrier((merged[1], own_pos))
    across = [flip(m, 2) for m in merged]
    for bit in bits:
        pos_pat = doubled(pos_pat, my_class // bit % 2, pat_flip(bit))

    operands = (probe, amplitudes, dft_tables(PATCH))
    grad_0, term = wave(0, classes, pos, me, me, object_image, sibling, across[0], *operands, None)
    part_0 = lax.all_to_all(grad_0, "pat", split_axis=0, concat_axis=0, tiled=True)
    grad_1, keep_term, give_term = wave(
        1, classes, pos, me, pos_pat, object_image, sibling, across[1], *operands, term
    )
    grad_1, part_0 = lax.optimization_barrier((grad_1, part_0))
    part_1 = lax.all_to_all(grad_1, "pat", split_axis=0, concat_axis=0, tiled=True)

    core = my_owner % 2
    line = my_owner // 2
    term = keep_term + flip(give_term, 1).astype(jnp.float32)
    term = halved(term, line, lambda value: flip(value, 2))
    term, then = lax.optimization_barrier((term, me))
    own, away = sum_pieces(pos_pat, then, part_0, part_1, owners, width)
    from_sibling_far = flip(away[0], 1)
    from_sibling = flip(away[1], 1)
    from_across = flip(
        (own[0] + from_sibling_far.astype(jnp.float32)).astype(jnp.bfloat16), 2
    )
    for bit in bits:
        term = halved(term, my_class // bit % 2, pat_flip(bit))
    total = own[1] + from_sibling.astype(jnp.float32) + from_across.astype(jnp.float32)
    mine = lax.dynamic_slice_in_dim(object_image, my_class * height, height, 1)
    updated = (mine.astype(jnp.float32) - OBJECT_RATE * total).astype(jnp.bfloat16)
    updated, term = lax.optimization_barrier((updated, term.astype(jnp.bfloat16)))
    steps = [
        functools.partial(doubled, bit=my_class // bit % 2, other=pat_flip(bit)) for bit in reversed(bits)
    ]
    steps.append(functools.partial(doubled, bit=line, other=lambda value: flip(value, 2)))
    steps.append(lambda part: doubled(part[None], core, lambda value: flip(value, 1)))
    if classes in BY_PERMUTE:
        object_next, term = gather_classes(updated, me, classes, term, steps)
    else:
        object_next = lax.all_gather(updated, "pat", axis=1, tiled=True)
        for step in steps:
            term = step(term)
    probe_total = term.astype(jnp.float32)
    probe_next = probe - PROBE_RATE * probe_total
    return (object_next, probe_next)


def solution(mesh):
    return jax.shard_map(
        shards,
        mesh=mesh,
        in_specs=(
            P(None, "obj", None),
            P(),
            P(("pat", "obj"), None, None),
            P(("pat", "obj"), None),
            P(("pat", "obj"), None),
        ),
        out_specs=(P(None, "obj", None), P()),
        check_vma=False,
    )
```

```python
import functools
import math

import jax
import jax.numpy as jnp
import numpy as np
from jax import lax
from jax.experimental import pallas as pl
from jax.experimental.pallas import tpu as pltpu
from jax.sharding import PartitionSpec as P

PATCH = 512
TILE = 256
LANES = 128
WIDE = PATCH + LANES

OBJECT_RATE = 0.1
PROBE_RATE = 0.05
MAGNITUDE_FLOOR = 0.5
CUT_VMEM = 14 * 1024 * 1024
WAVE_VMEM = 56 * 1024 * 1024
SUM_VMEM = 24 * 1024 * 1024


def dft_tables(length):
    counter = np.arange(length, dtype=np.int32)
    phase_angle = (counter[:, None] * counter[None, :] % length).astype(np.float32) * np.float32(
        2.0 * math.pi / length
    )
    factor = np.float32(1.0 / math.sqrt(length))
    cosine = (np.cos(phase_angle) * factor).astype(jnp.bfloat16)
    sine_part = (-np.sin(phase_angle) * factor).astype(jnp.bfloat16)
    return jnp.asarray(cosine), jnp.asarray(sine_part), jnp.asarray(-sine_part)


def first_row(pos, index):
    return pos[index, 0] * TILE + pos[index, 2]


def first_col(pos, index):
    return pos[index, 1] * TILE + pos[index, 3]


def shifted_left(blocks, amount):
    turned = [pltpu.roll(b, lax.rem(LANES - amount, LANES), axis=1) for b in blocks]
    lane = lax.broadcasted_iota(jnp.int32, turned[0].shape, 1)
    stay = lane < LANES - amount
    return jnp.concatenate([jnp.where(stay, a, b) for a, b in zip(turned, turned[1:])], 1)


def shifted_right(data, amount):
    count = data.shape[1] // LANES
    turned = [pltpu.roll(data[:, LANES * k : LANES * (k + 1)], amount, axis=1) for k in range(count)]
    lane = lax.broadcasted_iota(jnp.int32, turned[0].shape, 1)
    stay = lane >= amount
    before = [jnp.zeros_like(turned[0])] + turned
    after = turned + [jnp.zeros_like(turned[0])]
    return jnp.concatenate([jnp.where(stay, a, b) for a, b in zip(after, before)], 1)


def band_of_rows(row_at, start, count):
    rows = lax.broadcasted_iota(jnp.int32, (count, PATCH), 0) + start
    return row_at // PATCH + (rows < lax.rem(row_at, PATCH)).astype(jnp.int32)


CHUNK = 64
SUBLANES = 8


def rows_from(ref, plane, start, count):
    aligned = pl.multiple_of(start // SUBLANES * SUBLANES, SUBLANES)
    amount = lax.rem(start, SUBLANES)
    data = ref[plane, pl.ds(aligned, count + SUBLANES), :]
    data = data.reshape(count // SUBLANES + 1, SUBLANES, data.shape[1])
    turned = pltpu.roll(data, lax.rem(SUBLANES - amount, SUBLANES), axis=1)
    row = lax.broadcasted_iota(jnp.int32, turned[1:].shape, 1)
    data = jnp.where(row < SUBLANES - amount, turned[:-1], turned[1:])
    return data.reshape(count, data.shape[2])


def cut_rows(blocks, plane, rows, amount):
    return shifted_left([b[plane, rows, :].astype(jnp.float32) for b in blocks], amount)


def cut_kernel(flip, first, pos, me, *refs):
    blocks, out = refs[:-1], refs[-1]
    target = lax.bitwise_xor(me[0], flip)
    amount = lax.rem(first_col(pos, 2 * target + first + pl.program_id(0)), LANES)

    def body(i, carry):
        rows = pl.ds(pl.multiple_of(i * CHUNK, CHUNK), CHUNK)
        for plane in range(2):
            out[0, plane, rows, :] = cut_rows(blocks, plane, rows, amount).astype(jnp.bfloat16)
        return carry

    lax.fori_loop(0, PATCH // CHUNK, body, 0)


def cut(band, pos, me, flip, first, count):
    def block(k):
        def index(i, pos, me):
            return (0, 0, first_col(pos, 2 * lax.bitwise_xor(me[0], flip) + first + i) // LANES + k)

        return pl.BlockSpec((2, PATCH, LANES), index)

    return pl.pallas_call(
        functools.partial(cut_kernel, flip, first),
        grid_spec=pltpu.PrefetchScalarGridSpec(
            num_scalar_prefetch=2,
            grid=(count,),
            in_specs=[block(k) for k in range(WIDE // LANES)],
            out_specs=pl.BlockSpec((1, 2, PATCH, PATCH), lambda i, pos, me: (i, 0, 0, 0)),
        ),
        out_shape=jax.ShapeDtypeStruct((count, 2, PATCH, PATCH), jnp.bfloat16),
        compiler_params=pltpu.CompilerParams(vmem_limit_bytes=CUT_VMEM),
        cost_estimate=pl.CostEstimate(
            flops=count * 2 * PATCH * WIDE, bytes_accessed=count * 2300000, transcendentals=0
        ),
    )(pos, me, *([band] * (WIDE // LANES)))


def merge_kernel(which, pos, me, *refs):
    blocks, sibling, out = refs[:-2], refs[-2], refs[-1]
    index = 2 * lax.bitwise_xor(me[0], 2) + which
    amount = lax.rem(first_col(pos, index), LANES)
    row_at = first_row(pos, index)

    def body(i, carry):
        rows = pl.ds(pl.multiple_of(i * CHUNK, CHUNK), CHUNK)
        mine = band_of_rows(row_at, i * CHUNK, CHUNK) == me[0]
        for plane in range(2):
            own = cut_rows(blocks, plane, rows, amount)
            other = sibling[0, plane, rows, :].astype(jnp.float32)
            out[plane, rows, :] = jnp.where(mine, own, other).astype(jnp.bfloat16)
        return carry

    lax.fori_loop(0, PATCH // CHUNK, body, 0)


def cut_and_merge(band, sibling, pos, me, which):
    def block(k):
        def index(i, pos, me):
            return (0, 0, first_col(pos, 2 * lax.bitwise_xor(me[0], 2) + which) // LANES + k)

        return pl.BlockSpec((2, PATCH, LANES), index)

    return pl.pallas_call(
        functools.partial(merge_kernel, which),
        grid_spec=pltpu.PrefetchScalarGridSpec(
            num_scalar_prefetch=2,
            grid=(1,),
            in_specs=[block(k) for k in range(WIDE // LANES)]
            + [pl.BlockSpec((1, 2, PATCH, PATCH), lambda i, pos, me: (0, 0, 0, 0))],
            out_specs=pl.BlockSpec((2, PATCH, PATCH), lambda i, pos, me: (0, 0, 0)),
        ),
        out_shape=jax.ShapeDtypeStruct((2, PATCH, PATCH), jnp.bfloat16),
        compiler_params=pltpu.CompilerParams(vmem_limit_bytes=CUT_VMEM),
        cost_estimate=pl.CostEstimate(
            flops=2 * PATCH * WIDE, bytes_accessed=3300000, transcendentals=0
        ),
    )(pos, me, *([band] * (WIDE // LANES)), sibling)


def rest_index(step, pos, me):
    return jnp.where(step == 0, 2 * lax.bitwise_xor(me[0], 3) + 1, 2 * lax.bitwise_xor(me[0], 1) + step - 1)


def rest_kernel(pos, me, *refs):
    blocks, second, pieces = refs[:-2], refs[-2], refs[-1]
    step = pl.program_id(0)
    amount = lax.rem(first_col(pos, rest_index(step, pos, me)), LANES)

    def take(out):
        def body(i, carry):
            rows = pl.ds(pl.multiple_of(i * CHUNK, CHUNK), CHUNK)
            for plane in range(2):
                out[0, plane, rows, :] = cut_rows(blocks, plane, rows, amount).astype(jnp.bfloat16)
            return carry

        lax.fori_loop(0, PATCH // CHUNK, body, 0)

    pl.when(step == 0)(lambda: take(second))
    pl.when(step > 0)(lambda: take(pieces))


def cut_rest(band, pos, me):
    def block(k):
        def index(i, pos, me):
            return (0, 0, first_col(pos, rest_index(i, pos, me)) // LANES + k)

        return pl.BlockSpec((2, PATCH, LANES), index)

    shape = (2, PATCH, PATCH)
    return pl.pallas_call(
        rest_kernel,
        grid_spec=pltpu.PrefetchScalarGridSpec(
            num_scalar_prefetch=2,
            grid=(3,),
            in_specs=[block(k) for k in range(WIDE // LANES)],
            out_specs=[
                pl.BlockSpec((1, *shape), lambda i, pos, me: (0, 0, 0, 0)),
                pl.BlockSpec((1, *shape), lambda i, pos, me: (jnp.maximum(i - 1, 0), 0, 0, 0)),
            ],
        ),
        out_shape=[
            jax.ShapeDtypeStruct((1, *shape), jnp.bfloat16),
            jax.ShapeDtypeStruct((2, *shape), jnp.bfloat16),
        ],
        compiler_params=pltpu.CompilerParams(vmem_limit_bytes=CUT_VMEM),
        cost_estimate=pl.CostEstimate(
            flops=6 * PATCH * WIDE, bytes_accessed=7000000, transcendentals=0
        ),
    )(pos, me, *([band] * (WIDE // LANES)))


def wave_kernel(which, pos, me, spare, band, sibling, across, probe, amplitudes, *refs):
    tables, refs = refs[:3], refs[3:]
    last = which == 1
    if last:
        term_in, grad, keep_term, give_term, *scratch = refs
    else:
        grad, term_out, *scratch = refs
    window, sib_v, far_v, probe_v, amp_v, left_v, right_v, term_v, patch_v, twice, field, half, sems = scratch
    index = 2 * me[0] + which
    col_at = first_col(pos, index)
    row_at = first_row(pos, index)
    start = pl.multiple_of(col_at // LANES * LANES, LANES)
    pairs = [
        (band.at[:, :, pl.ds(start, WIDE)], window),
        (sibling.at[which], sib_v),
        (across, far_v),
        (probe, probe_v),
    ]
    cosine, sine, minus = tables
    quarters = [(slice(0, PATCH), slice(0, PATCH)), (slice(0, PATCH), slice(PATCH, 2 * PATCH))]
    quarters += [(slice(PATCH, 2 * PATCH), slice(0, PATCH)), (slice(PATCH, 2 * PATCH), slice(PATCH, 2 * PATCH))]
    pairs += [(t, left_v.at[q]) for t, q in zip((cosine, minus, sine, cosine), quarters)]
    pairs.append((amplitudes.at[which], amp_v))
    pairs += [(t, right_v.at[q]) for t, q in zip((cosine, sine, minus, cosine), quarters)]
    if last:
        pairs.append((term_in, term_v))
    copies = [pltpu.make_async_copy(a, b, sems.at[k]) for k, (a, b) in enumerate(pairs)]
    for copy in copies:
        copy.start()
    for copy in copies[:3]:
        copy.wait()
    amount = lax.rem(col_at, LANES)
    down = lax.rem(row_at, PATCH)
    views = [window.at[:, :, LANES * k : LANES * (k + 1)] for k in range(WIDE // LANES)]

    def assemble(i, carry):
        at = pl.multiple_of(i * CHUNK, CHUNK)
        rows = pl.ds(at, CHUNK)
        owner = band_of_rows(row_at, at, CHUNK)
        mine = owner == me[0]
        near = owner == lax.bitwise_xor(me[0], 1)
        for plane in range(2):
            own = cut_rows(views, plane, rows, amount)
            beside = sib_v[plane, rows, :].astype(jnp.float32)
            beyond = far_v[plane, rows, :].astype(jnp.float32)
            patch = jnp.where(mine, own, jnp.where(near, beside, beyond))
            twice[plane, rows, :] = patch
            twice[plane, pl.ds(pl.multiple_of(at + PATCH, CHUNK), CHUNK), :] = patch
        return carry

    lax.fori_loop(0, PATCH // CHUNK, assemble, 0)
    copies[3].wait()

    def illuminate(i, carry):
        at = pl.multiple_of(i * CHUNK, CHUNK)
        rows = pl.ds(at, CHUNK)
        patch_real = rows_from(twice, 0, at + down, CHUNK)
        patch_imag = rows_from(twice, 1, at + down, CHUNK)
        patch_v[0, rows, :] = patch_real.astype(jnp.bfloat16)
        patch_v[1, rows, :] = patch_imag.astype(jnp.bfloat16)
        probe_real = probe_v[0, rows, :]
        probe_imag = probe_v[1, rows, :]
        field[rows, :] = (probe_real * patch_real - probe_imag * patch_imag).astype(jnp.bfloat16)
        field[pl.ds(pl.multiple_of(at + PATCH, CHUNK), CHUNK), :] = (
            probe_real * patch_imag + probe_imag * patch_real
        ).astype(jnp.bfloat16)
        return carry

    lax.fori_loop(0, PATCH // CHUNK, illuminate, 0)
    for copy in copies[4:8]:
        copy.wait()

    def over_rows(table):
        for k in range(4):
            part = jnp.dot(
                table[256 * k : 256 * (k + 1), :], field[...], preferred_element_type=jnp.float32
            ).astype(jnp.bfloat16)
            half[256 * (k % 2) : 256 * (k % 2 + 1), PATCH * (k // 2) : PATCH * (k // 2 + 1)] = part

    over_rows(left_v)
    for copy in copies[8:13]:
        copy.wait()
    for k in range(2):
        rows = slice(256 * k, 256 * (k + 1))
        far = jnp.dot(half[rows, :], right_v[...], preferred_element_type=jnp.float32)
        far_real = far[:, :PATCH]
        far_imag = far[:, PATCH:]
        power = far_real * far_real + far_imag * far_imag
        keep = 1.0 - amp_v[rows, :].astype(jnp.float32) * lax.rsqrt(
            jnp.maximum(power, MAGNITUDE_FLOOR * MAGNITUDE_FLOOR)
        )
        field[rows, :] = (far_real * keep).astype(jnp.bfloat16)
        field[PATCH + 256 * k : PATCH + 256 * (k + 1), :] = (far_imag * keep).astype(jnp.bfloat16)
    over_rows(right_v)
    if last:
        copies[13].wait()
        core = lax.rem(me[0], 2)
    for k in range(2):
        rows = slice(256 * k, 256 * (k + 1))
        back = jnp.dot(half[rows, :], left_v[...], preferred_element_type=jnp.float32)
        back_real = back[:, :PATCH]
        back_imag = back[:, PATCH:]
        patch_real = patch_v[0, rows, :].astype(jnp.float32)
        patch_imag = patch_v[1, rows, :].astype(jnp.float32)
        term_real = patch_real * back_real + patch_imag * back_imag
        term_imag = patch_real * back_imag - patch_imag * back_real
        if last:
            term_real = term_real + term_v[0, rows, :]
            term_imag = term_imag + term_v[1, rows, :]
            keep_term[rows, :] = jnp.where(core == 0, term_real, term_imag)
            give_term[rows, :] = jnp.where(core == 0, term_imag, term_real).astype(jnp.bfloat16)
        else:
            term_out[0, rows, :] = term_real
            term_out[1, rows, :] = term_imag
        term_v[0, rows, :] = back_real
        term_v[1, rows, :] = back_imag

    def weigh(i, carry):
        at = pl.multiple_of(i * CHUNK, CHUNK)
        rows = pl.ds(at, CHUNK)
        again = pl.ds(pl.multiple_of(at + PATCH, CHUNK), CHUNK)
        probe_real = probe_v[0, rows, :]
        probe_imag = probe_v[1, rows, :]
        back_real = term_v[0, rows, :]
        back_imag = term_v[1, rows, :]
        grad_real = probe_real * back_real + probe_imag * back_imag
        grad_imag = probe_real * back_imag - probe_imag * back_real
        twice[0, rows, :] = grad_real
        twice[0, again, :] = grad_real
        twice[1, rows, :] = grad_imag
        twice[1, again, :] = grad_imag
        return carry

    lax.fori_loop(0, PATCH // CHUNK, weigh, 0)
    classes, height = grad.shape[0], grad.shape[2]

    def spread(k, carry):
        for plane in range(2):
            grad[k, plane] = rows_from(twice, plane, PATCH - down + k * height, height).astype(
                jnp.bfloat16
            )
        return carry

    lax.fori_loop(0, classes, spread, 0)


def wave(which, classes, pos, me, spare, band, sibling, across, probe, amplitudes, tables, term):
    operands = [band, sibling, across, probe, amplitudes, *tables]
    smem = pl.BlockSpec(memory_space=pltpu.SMEM)
    hbm = pl.BlockSpec(memory_space=pl.ANY)
    vmem = pl.BlockSpec(memory_space=pltpu.VMEM)
    planes = (2, PATCH, PATCH)
    plane = (PATCH, PATCH)
    if term is None:
        terms = [jax.ShapeDtypeStruct(planes, jnp.float32)]
    else:
        operands.append(term)
        terms = [jax.ShapeDtypeStruct(plane, t) for t in (jnp.float32, jnp.bfloat16)]
    return pl.pallas_call(
        functools.partial(wave_kernel, which),
        in_specs=[smem, smem, smem] + [hbm] * len(operands),
        out_specs=[vmem] * (1 + len(terms)),
        out_shape=[
            jax.ShapeDtypeStruct((classes, 2, PATCH // classes, PATCH), jnp.bfloat16),
            *terms,
        ],
        scratch_shapes=[
            pltpu.VMEM((2, PATCH, WIDE), jnp.bfloat16),
            pltpu.VMEM(planes, jnp.bfloat16),
            pltpu.VMEM(planes, jnp.bfloat16),
            pltpu.VMEM(planes, jnp.float32),
            pltpu.VMEM((PATCH, PATCH), jnp.bfloat16),
            pltpu.VMEM((2 * PATCH, 2 * PATCH), jnp.bfloat16),
            pltpu.VMEM((2 * PATCH, 2 * PATCH), jnp.bfloat16),
            pltpu.VMEM(planes, jnp.float32),
            pltpu.VMEM(planes, jnp.bfloat16),
            pltpu.VMEM((2, 2 * PATCH + SUBLANES, PATCH), jnp.float32),
            pltpu.VMEM((2 * PATCH, PATCH), jnp.bfloat16),
            pltpu.VMEM((PATCH, 2 * PATCH), jnp.bfloat16),
            pltpu.SemaphoreType.DMA((14,)),
        ],
        compiler_params=pltpu.CompilerParams(vmem_limit_bytes=WAVE_VMEM),
        cost_estimate=pl.CostEstimate(
            flops=32 * PATCH**3, bytes_accessed=100_000_000, transcendentals=0
        ),
    )(pos, me, spare, *operands)


def sum_kernel(pos, me, first, second, own, away, canvas):
    classes, height = first.shape[0], first.shape[2]
    start = me[1] * height
    canvas[...] = jnp.zeros_like(canvas)
    rows = lax.broadcasted_iota(jnp.int32, (2 * height, WIDE), 0)
    rows = start + jnp.where(rows >= height, rows - height, rows)

    def piece(k, source, which):
        index = 2 * k + which
        row_at = first_row(pos, index)
        col_at = first_col(pos, index)
        down = lax.rem(row_at, PATCH)
        at = pl.ds(pl.multiple_of(col_at // LANES * LANES, LANES), WIDE)
        data = source[k].astype(jnp.float32).reshape(2 * height, PATCH)
        data = shifted_right(data, lax.rem(col_at, LANES))

        @pl.when(down < start + height)
        def _():
            canvas[row_at // PATCH, :, at] += jnp.where(rows >= down, data, 0.0)

        @pl.when(down > start)
        def _():
            canvas[row_at // PATCH + 1, :, at] += jnp.where(rows < down, data, 0.0)

    def body(k, carry):
        piece(k, first, 0)
        piece(k, second, 1)
        return carry

    lax.fori_loop(0, classes, body, 0)
    shape = own.shape[1:]
    for k in range(2):
        keep = lax.bitwise_xor(me[0], 2 - 2 * k)
        give = lax.bitwise_xor(me[0], 3 - 2 * k)
        own[k] = canvas[keep].reshape(shape)
        away[k] = canvas[give].reshape(shape).astype(jnp.bfloat16)


def sum_pieces(pos, me, first, second, bands, width):
    height = first.shape[2]
    smem = pl.BlockSpec(memory_space=pltpu.SMEM)
    vmem = pl.BlockSpec(memory_space=pltpu.VMEM)
    shape = (2, 2, height, width)
    return pl.pallas_call(
        sum_kernel,
        in_specs=[smem, smem, vmem, vmem],
        out_specs=[vmem, vmem],
        out_shape=[
            jax.ShapeDtypeStruct(shape, jnp.float32),
            jax.ShapeDtypeStruct(shape, jnp.bfloat16),
        ],
        scratch_shapes=[pltpu.VMEM((bands, 2 * height, width), jnp.float32)],
        compiler_params=pltpu.CompilerParams(vmem_limit_bytes=SUM_VMEM),
        cost_estimate=pl.CostEstimate(
            flops=8 * first.size, bytes_accessed=4 * first.size + 6 * math.prod(shape), transcendentals=0
        ),
    )(pos, me, first, second)


def shards(object_image, probe, amplitudes, pos_tile, pos_offset):
    owners = lax.axis_size("obj")
    classes = lax.axis_size("pat")
    my_owner = lax.axis_index("obj").astype(jnp.int32)
    my_class = lax.axis_index("pat").astype(jnp.int32)
    me = jnp.stack([my_owner, my_class])
    height = PATCH // classes
    width = object_image.shape[2]
    assert owners == 4 and object_image.shape[1] == PATCH and pos_tile.shape[0] == 2

    def flip(value, bit):
        return lax.ppermute(value, "obj", [(k, k ^ bit) for k in range(owners)])

    def pat_flip(bit):
        return lambda value: lax.ppermute(value, "pat", [(k, k ^ bit) for k in range(classes)])

    def halved(part, bit, other):
        rows = part.shape[0] // 2
        give = lax.dynamic_slice_in_dim(part, (1 - bit) * rows, rows, 0).astype(jnp.bfloat16)
        return lax.dynamic_slice_in_dim(part, bit * rows, rows, 0) + other(give).astype(jnp.float32)

    def doubled(part, bit, other):
        got = other(part)
        return jnp.where(bit == 0, jnp.concatenate([part, got]), jnp.concatenate([got, part]))

    bits = [1 << k for k in range(classes.bit_length() - 1)]
    own_pos = jnp.concatenate([pos_tile, pos_offset], 1)
    pos = lax.all_gather(own_pos, "obj", axis=0, tiled=True)

    first = cut(object_image, pos, me, 3, 0, 1)
    second, pieces = cut_rest(object_image, pos, me)
    second, pieces, then = lax.optimization_barrier((second, pieces, me))
    relay = [flip(first, 1), flip(second, 1)]
    sibling = flip(pieces, 1)
    merged = [cut_and_merge(object_image, relay[k], pos, then, k) for k in range(2)]
    merged[1], pos_pat = lax.optimization_barrier((merged[1], own_pos))
    across = [flip(m, 2) for m in merged]
    for bit in bits:
        pos_pat = doubled(pos_pat, my_class // bit % 2, pat_flip(bit))

    operands = (probe, amplitudes, dft_tables(PATCH))
    grad_0, term = wave(0, classes, pos, me, me, object_image, sibling, across[0], *operands, None)
    grad_0, across[1] = lax.optimization_barrier((grad_0, across[1]))
    part_0 = lax.all_to_all(grad_0, "pat", split_axis=0, concat_axis=0, tiled=True)
    grad_1, keep_term, give_term = wave(
        1, classes, pos, me, pos_pat, object_image, sibling, across[1], *operands, term
    )
    grad_1, part_0 = lax.optimization_barrier((grad_1, part_0))
    part_1 = lax.all_to_all(grad_1, "pat", split_axis=0, concat_axis=0, tiled=True)

    core = my_owner % 2
    line = my_owner // 2
    term = keep_term + flip(give_term, 1).astype(jnp.float32)
    term = halved(term, line, lambda value: flip(value, 2))
    term, then = lax.optimization_barrier((term, me))
    own, away = sum_pieces(pos_pat, then, part_0, part_1, owners, width)
    from_sibling_far = flip(away[0], 1)
    from_sibling = flip(away[1], 1)
    from_across = flip(
        (own[0] + from_sibling_far.astype(jnp.float32)).astype(jnp.bfloat16), 2
    )
    for bit in bits:
        term = halved(term, my_class // bit % 2, pat_flip(bit))
    total = own[1] + from_sibling.astype(jnp.float32) + from_across.astype(jnp.float32)
    mine = lax.dynamic_slice_in_dim(object_image, my_class * height, height, 1)
    updated = (mine.astype(jnp.float32) - OBJECT_RATE * total).astype(jnp.bfloat16)
    updated, term = lax.optimization_barrier((updated, term.astype(jnp.bfloat16)))
    steps = [
        functools.partial(doubled, bit=my_class // bit % 2, other=pat_flip(bit)) for bit in reversed(bits)
    ]
    steps.append(functools.partial(doubled, bit=line, other=lambda value: flip(value, 2)))
    steps.append(lambda part: doubled(part[None], core, lambda value: flip(value, 1)))
    object_next = lax.all_gather(updated, "pat", axis=1, tiled=True)
    for step in steps:
        term = step(term)
    probe_total = term.astype(jnp.float32)
    probe_next = probe - PROBE_RATE * probe_total
    return (object_next, probe_next)


def solution(mesh):
    return jax.shard_map(
        shards,
        mesh=mesh,
        in_specs=(
            P(None, "obj", None),
            P(),
            P(("pat", "obj"), None, None),
            P(("pat", "obj"), None),
            P(("pat", "obj"), None),
        ),
        out_specs=(P(None, "obj", None), P()),
        check_vma=False,
    )
```

```python
import functools
import math

import jax
import jax.numpy as jnp
import numpy as np
from jax import lax
from jax.experimental import pallas as pl
from jax.experimental.pallas import tpu as pltpu
from jax.sharding import PartitionSpec as P

PATCH = 512
TILE = 256
LANES = 128
WIDE = PATCH + LANES

OBJECT_RATE = 0.1
PROBE_RATE = 0.05
MAGNITUDE_FLOOR = 0.5
CUT_VMEM = 14 * 1024 * 1024
WAVE_VMEM = 56 * 1024 * 1024
SUM_VMEM = 24 * 1024 * 1024


def dft_tables(length):
    counter = np.arange(length, dtype=np.int32)
    phase_angle = (counter[:, None] * counter[None, :] % length).astype(np.float32) * np.float32(
        2.0 * math.pi / length
    )
    factor = np.float32(1.0 / math.sqrt(length))
    cosine = (np.cos(phase_angle) * factor).astype(jnp.bfloat16)
    sine_part = (-np.sin(phase_angle) * factor).astype(jnp.bfloat16)
    return jnp.asarray(cosine), jnp.asarray(sine_part), jnp.asarray(-sine_part)


def first_row(pos, index):
    return pos[index, 0] * TILE + pos[index, 2]


def first_col(pos, index):
    return pos[index, 1] * TILE + pos[index, 3]


def shifted_left(blocks, amount):
    turned = [pltpu.roll(b, lax.rem(LANES - amount, LANES), axis=1) for b in blocks]
    lane = lax.broadcasted_iota(jnp.int32, turned[0].shape, 1)
    stay = lane < LANES - amount
    return jnp.concatenate([jnp.where(stay, a, b) for a, b in zip(turned, turned[1:])], 1)


def shifted_right(data, amount):
    count = data.shape[1] // LANES
    turned = [pltpu.roll(data[:, LANES * k : LANES * (k + 1)], amount, axis=1) for k in range(count)]
    lane = lax.broadcasted_iota(jnp.int32, turned[0].shape, 1)
    stay = lane >= amount
    before = [jnp.zeros_like(turned[0])] + turned
    after = turned + [jnp.zeros_like(turned[0])]
    return jnp.concatenate([jnp.where(stay, a, b) for a, b in zip(after, before)], 1)


def band_of_rows(row_at, start, count):
    rows = lax.broadcasted_iota(jnp.int32, (count, PATCH), 0) + start
    return row_at // PATCH + (rows < lax.rem(row_at, PATCH)).astype(jnp.int32)


CHUNK = 64
SUBLANES = 8


def rows_from(ref, plane, start, count):
    aligned = pl.multiple_of(start // SUBLANES * SUBLANES, SUBLANES)
    amount = lax.rem(start, SUBLANES)
    data = ref[plane, pl.ds(aligned, count + SUBLANES), :]
    data = data.reshape(count // SUBLANES + 1, SUBLANES, data.shape[1])
    turned = pltpu.roll(data, lax.rem(SUBLANES - amount, SUBLANES), axis=1)
    row = lax.broadcasted_iota(jnp.int32, turned[1:].shape, 1)
    data = jnp.where(row < SUBLANES - amount, turned[:-1], turned[1:])
    return data.reshape(count, data.shape[2])


def cut_rows(blocks, plane, rows, amount):
    return shifted_left([b[plane, rows, :].astype(jnp.float32) for b in blocks], amount)


def cut_kernel(flip, first, pos, me, *refs):
    blocks, out = refs[:-1], refs[-1]
    target = lax.bitwise_xor(me[0], flip)
    amount = lax.rem(first_col(pos, 2 * target + first + pl.program_id(0)), LANES)

    def body(i, carry):
        rows = pl.ds(pl.multiple_of(i * CHUNK, CHUNK), CHUNK)
        for plane in range(2):
            out[0, plane, rows, :] = cut_rows(blocks, plane, rows, amount).astype(jnp.bfloat16)
        return carry

    lax.fori_loop(0, PATCH // CHUNK, body, 0)


def cut(band, pos, me, flip, first, count):
    def block(k):
        def index(i, pos, me):
            return (0, 0, first_col(pos, 2 * lax.bitwise_xor(me[0], flip) + first + i) // LANES + k)

        return pl.BlockSpec((2, PATCH, LANES), index)

    return pl.pallas_call(
        functools.partial(cut_kernel, flip, first),
        grid_spec=pltpu.PrefetchScalarGridSpec(
            num_scalar_prefetch=2,
            grid=(count,),
            in_specs=[block(k) for k in range(WIDE // LANES)],
            out_specs=pl.BlockSpec((1, 2, PATCH, PATCH), lambda i, pos, me: (i, 0, 0, 0)),
        ),
        out_shape=jax.ShapeDtypeStruct((count, 2, PATCH, PATCH), jnp.bfloat16),
        compiler_params=pltpu.CompilerParams(vmem_limit_bytes=CUT_VMEM),
        cost_estimate=pl.CostEstimate(
            flops=count * 2 * PATCH * WIDE, bytes_accessed=count * 2300000, transcendentals=0
        ),
    )(pos, me, *([band] * (WIDE // LANES)))


def merge_kernel(which, pos, me, *refs):
    blocks, sibling, out = refs[:-2], refs[-2], refs[-1]
    index = 2 * lax.bitwise_xor(me[0], 2) + which
    amount = lax.rem(first_col(pos, index), LANES)
    row_at = first_row(pos, index)

    def body(i, carry):
        rows = pl.ds(pl.multiple_of(i * CHUNK, CHUNK), CHUNK)
        mine = band_of_rows(row_at, i * CHUNK, CHUNK) == me[0]
        for plane in range(2):
            own = cut_rows(blocks, plane, rows, amount)
            other = sibling[0, plane, rows, :].astype(jnp.float32)
            out[plane, rows, :] = jnp.where(mine, own, other).astype(jnp.bfloat16)
        return carry

    lax.fori_loop(0, PATCH // CHUNK, body, 0)


def cut_and_merge(band, sibling, pos, me, which):
    def block(k):
        def index(i, pos, me):
            return (0, 0, first_col(pos, 2 * lax.bitwise_xor(me[0], 2) + which) // LANES + k)

        return pl.BlockSpec((2, PATCH, LANES), index)

    return pl.pallas_call(
        functools.partial(merge_kernel, which),
        grid_spec=pltpu.PrefetchScalarGridSpec(
            num_scalar_prefetch=2,
            grid=(1,),
            in_specs=[block(k) for k in range(WIDE // LANES)]
            + [pl.BlockSpec((1, 2, PATCH, PATCH), lambda i, pos, me: (0, 0, 0, 0))],
            out_specs=pl.BlockSpec((2, PATCH, PATCH), lambda i, pos, me: (0, 0, 0)),
        ),
        out_shape=jax.ShapeDtypeStruct((2, PATCH, PATCH), jnp.bfloat16),
        compiler_params=pltpu.CompilerParams(vmem_limit_bytes=CUT_VMEM),
        cost_estimate=pl.CostEstimate(
            flops=2 * PATCH * WIDE, bytes_accessed=3300000, transcendentals=0
        ),
    )(pos, me, *([band] * (WIDE // LANES)), sibling)


def rest_index(step, pos, me):
    return jnp.where(step == 0, 2 * lax.bitwise_xor(me[0], 3) + 1, 2 * lax.bitwise_xor(me[0], 1) + step - 1)


def rest_kernel(pos, me, *refs):
    blocks, second, pieces = refs[:-2], refs[-2], refs[-1]
    step = pl.program_id(0)
    amount = lax.rem(first_col(pos, rest_index(step, pos, me)), LANES)

    def take(out):
        def body(i, carry):
            rows = pl.ds(pl.multiple_of(i * CHUNK, CHUNK), CHUNK)
            for plane in range(2):
                out[0, plane, rows, :] = cut_rows(blocks, plane, rows, amount).astype(jnp.bfloat16)
            return carry

        lax.fori_loop(0, PATCH // CHUNK, body, 0)

    pl.when(step == 0)(lambda: take(second))
    pl.when(step > 0)(lambda: take(pieces))


def cut_rest(band, pos, me):
    def block(k):
        def index(i, pos, me):
            return (0, 0, first_col(pos, rest_index(i, pos, me)) // LANES + k)

        return pl.BlockSpec((2, PATCH, LANES), index)

    shape = (2, PATCH, PATCH)
    return pl.pallas_call(
        rest_kernel,
        grid_spec=pltpu.PrefetchScalarGridSpec(
            num_scalar_prefetch=2,
            grid=(3,),
            in_specs=[block(k) for k in range(WIDE // LANES)],
            out_specs=[
                pl.BlockSpec((1, *shape), lambda i, pos, me: (0, 0, 0, 0)),
                pl.BlockSpec((1, *shape), lambda i, pos, me: (jnp.maximum(i - 1, 0), 0, 0, 0)),
            ],
        ),
        out_shape=[
            jax.ShapeDtypeStruct((1, *shape), jnp.bfloat16),
            jax.ShapeDtypeStruct((2, *shape), jnp.bfloat16),
        ],
        compiler_params=pltpu.CompilerParams(vmem_limit_bytes=CUT_VMEM),
        cost_estimate=pl.CostEstimate(
            flops=6 * PATCH * WIDE, bytes_accessed=7000000, transcendentals=0
        ),
    )(pos, me, *([band] * (WIDE // LANES)))


def wave_kernel(which, pos, me, spare, band, sibling, across, probe, amplitudes, *refs):
    tables, refs = refs[:3], refs[3:]
    last = which == 1
    if last:
        term_in, grad, keep_term, give_term, *scratch = refs
    else:
        grad, term_out, *scratch = refs
    window, sib_v, far_v, probe_v, amp_v, matrix, term_v, patch_v, twice, field, half, sems = scratch
    index = 2 * me[0] + which
    col_at = first_col(pos, index)
    row_at = first_row(pos, index)
    start = pl.multiple_of(col_at // LANES * LANES, LANES)
    pairs = [
        (band.at[:, :, pl.ds(start, WIDE)], window),
        (sibling.at[which], sib_v),
        (across, far_v),
        (probe, probe_v),
    ]
    cosine, sine, minus = tables
    quarters = [(slice(0, PATCH), slice(0, PATCH)), (slice(0, PATCH), slice(PATCH, 2 * PATCH))]
    quarters += [(slice(PATCH, 2 * PATCH), slice(0, PATCH)), (slice(PATCH, 2 * PATCH), slice(PATCH, 2 * PATCH))]
    pairs += [(t, matrix.at[q]) for t, q in zip((cosine, minus, sine, cosine), quarters)]
    pairs.append((amplitudes.at[which], amp_v))
    if last:
        pairs.append((term_in, term_v))
    copies = [pltpu.make_async_copy(a, b, sems.at[k]) for k, (a, b) in enumerate(pairs)]
    for copy in copies:
        copy.start()
    for copy in copies[:3]:
        copy.wait()
    amount = lax.rem(col_at, LANES)
    down = lax.rem(row_at, PATCH)
    views = [window.at[:, :, LANES * k : LANES * (k + 1)] for k in range(WIDE // LANES)]

    def assemble(i, carry):
        at = pl.multiple_of(i * CHUNK, CHUNK)
        rows = pl.ds(at, CHUNK)
        owner = band_of_rows(row_at, at, CHUNK)
        mine = owner == me[0]
        near = owner == lax.bitwise_xor(me[0], 1)
        for plane in range(2):
            own = cut_rows(views, plane, rows, amount)
            beside = sib_v[plane, rows, :].astype(jnp.float32)
            beyond = far_v[plane, rows, :].astype(jnp.float32)
            patch = jnp.where(mine, own, jnp.where(near, beside, beyond))
            twice[plane, rows, :] = patch
            twice[plane, pl.ds(pl.multiple_of(at + PATCH, CHUNK), CHUNK), :] = patch
        return carry

    lax.fori_loop(0, PATCH // CHUNK, assemble, 0)
    copies[3].wait()

    def illuminate(i, carry):
        at = pl.multiple_of(i * CHUNK, CHUNK)
        rows = pl.ds(at, CHUNK)
        patch_real = rows_from(twice, 0, at + down, CHUNK)
        patch_imag = rows_from(twice, 1, at + down, CHUNK)
        patch_v[0, rows, :] = patch_real.astype(jnp.bfloat16)
        patch_v[1, rows, :] = patch_imag.astype(jnp.bfloat16)
        probe_real = probe_v[0, rows, :]
        probe_imag = probe_v[1, rows, :]
        field[rows, :] = (probe_real * patch_real - probe_imag * patch_imag).astype(jnp.bfloat16)
        field[pl.ds(pl.multiple_of(at + PATCH, CHUNK), CHUNK), :] = (
            probe_real * patch_imag + probe_imag * patch_real
        ).astype(jnp.bfloat16)
        return carry

    lax.fori_loop(0, PATCH // CHUNK, illuminate, 0)
    for copy in copies[4:8]:
        copy.wait()

    def over_rows():
        for k in range(4):
            part = jnp.dot(
                matrix[256 * k : 256 * (k + 1), :], field[...], preferred_element_type=jnp.float32
            ).astype(jnp.bfloat16)
            at = PATCH * (1 - k // 2)
            half[256 * (k % 2) : 256 * (k % 2 + 1), at : at + PATCH] = part

    over_rows()
    copies[8].wait()
    for k in range(2):
        rows = slice(256 * k, 256 * (k + 1))
        far = jnp.dot(half[rows, :], matrix[...], preferred_element_type=jnp.float32)
        far_imag = far[:, :PATCH]
        far_real = far[:, PATCH:]
        power = far_real * far_real + far_imag * far_imag
        keep = 1.0 - amp_v[rows, :].astype(jnp.float32) * lax.rsqrt(
            jnp.maximum(power, MAGNITUDE_FLOOR * MAGNITUDE_FLOOR)
        )
        field[rows, :] = (far_imag * keep).astype(jnp.bfloat16)
        field[PATCH + 256 * k : PATCH + 256 * (k + 1), :] = (far_real * keep).astype(jnp.bfloat16)
    over_rows()
    if last:
        copies[9].wait()
        core = lax.rem(me[0], 2)
    for k in range(2):
        rows = slice(256 * k, 256 * (k + 1))
        back = jnp.dot(half[rows, :], matrix[...], preferred_element_type=jnp.float32)
        back_real = back[:, :PATCH]
        back_imag = back[:, PATCH:]
        patch_real = patch_v[0, rows, :].astype(jnp.float32)
        patch_imag = patch_v[1, rows, :].astype(jnp.float32)
        term_real = patch_real * back_real + patch_imag * back_imag
        term_imag = patch_real * back_imag - patch_imag * back_real
        if last:
            term_real = term_real + term_v[0, rows, :]
            term_imag = term_imag + term_v[1, rows, :]
            keep_term[rows, :] = jnp.where(core == 0, term_real, term_imag)
            give_term[rows, :] = jnp.where(core == 0, term_imag, term_real).astype(jnp.bfloat16)
        else:
            term_out[0, rows, :] = term_real
            term_out[1, rows, :] = term_imag
        term_v[0, rows, :] = back_real
        term_v[1, rows, :] = back_imag

    def weigh(i, carry):
        at = pl.multiple_of(i * CHUNK, CHUNK)
        rows = pl.ds(at, CHUNK)
        again = pl.ds(pl.multiple_of(at + PATCH, CHUNK), CHUNK)
        probe_real = probe_v[0, rows, :]
        probe_imag = probe_v[1, rows, :]
        back_real = term_v[0, rows, :]
        back_imag = term_v[1, rows, :]
        grad_real = probe_real * back_real + probe_imag * back_imag
        grad_imag = probe_real * back_imag - probe_imag * back_real
        twice[0, rows, :] = grad_real
        twice[0, again, :] = grad_real
        twice[1, rows, :] = grad_imag
        twice[1, again, :] = grad_imag
        return carry

    lax.fori_loop(0, PATCH // CHUNK, weigh, 0)
    classes, height = grad.shape[0], grad.shape[2]

    def spread(k, carry):
        for plane in range(2):
            grad[k, plane] = rows_from(twice, plane, PATCH - down + k * height, height).astype(
                jnp.bfloat16
            )
        return carry

    lax.fori_loop(0, classes, spread, 0)


def wave(which, classes, pos, me, spare, band, sibling, across, probe, amplitudes, tables, term):
    operands = [band, sibling, across, probe, amplitudes, *tables]
    smem = pl.BlockSpec(memory_space=pltpu.SMEM)
    hbm = pl.BlockSpec(memory_space=pl.ANY)
    vmem = pl.BlockSpec(memory_space=pltpu.VMEM)
    planes = (2, PATCH, PATCH)
    plane = (PATCH, PATCH)
    if term is None:
        terms = [jax.ShapeDtypeStruct(planes, jnp.float32)]
    else:
        operands.append(term)
        terms = [jax.ShapeDtypeStruct(plane, t) for t in (jnp.float32, jnp.bfloat16)]
    return pl.pallas_call(
        functools.partial(wave_kernel, which),
        in_specs=[smem, smem, smem] + [hbm] * len(operands),
        out_specs=[vmem] * (1 + len(terms)),
        out_shape=[
            jax.ShapeDtypeStruct((classes, 2, PATCH // classes, PATCH), jnp.bfloat16),
            *terms,
        ],
        scratch_shapes=[
            pltpu.VMEM((2, PATCH, WIDE), jnp.bfloat16),
            pltpu.VMEM(planes, jnp.bfloat16),
            pltpu.VMEM(planes, jnp.bfloat16),
            pltpu.VMEM(planes, jnp.float32),
            pltpu.VMEM((PATCH, PATCH), jnp.bfloat16),
            pltpu.VMEM((2 * PATCH, 2 * PATCH), jnp.bfloat16),
            pltpu.VMEM(planes, jnp.float32),
            pltpu.VMEM(planes, jnp.bfloat16),
            pltpu.VMEM((2, 2 * PATCH + SUBLANES, PATCH), jnp.float32),
            pltpu.VMEM((2 * PATCH, PATCH), jnp.bfloat16),
            pltpu.VMEM((PATCH, 2 * PATCH), jnp.bfloat16),
            pltpu.SemaphoreType.DMA((10,)),
        ],
        compiler_params=pltpu.CompilerParams(vmem_limit_bytes=WAVE_VMEM),
        cost_estimate=pl.CostEstimate(
            flops=32 * PATCH**3, bytes_accessed=100_000_000, transcendentals=0
        ),
    )(pos, me, spare, *operands)


def sum_kernel(pos, me, first, second, own_far, own_near, away_far, away_near, canvas):
    classes, height = first.shape[0], first.shape[2]
    start = me[1] * height
    canvas[...] = jnp.zeros_like(canvas)
    rows = lax.broadcasted_iota(jnp.int32, (2 * height, WIDE), 0)
    rows = start + jnp.where(rows >= height, rows - height, rows)

    def piece(k, source, which):
        index = 2 * k + which
        row_at = first_row(pos, index)
        col_at = first_col(pos, index)
        down = lax.rem(row_at, PATCH)
        at = pl.ds(pl.multiple_of(col_at // LANES * LANES, LANES), WIDE)
        data = source[k].astype(jnp.float32).reshape(2 * height, PATCH)
        data = shifted_right(data, lax.rem(col_at, LANES))

        @pl.when(down < start + height)
        def _():
            canvas[row_at // PATCH, :, at] += jnp.where(rows >= down, data, 0.0)

        @pl.when(down > start)
        def _():
            canvas[row_at // PATCH + 1, :, at] += jnp.where(rows < down, data, 0.0)

    def body(k, carry):
        piece(k, first, 0)
        piece(k, second, 1)
        return carry

    lax.fori_loop(0, classes, body, 0)
    shape = own_far.shape
    for k, (own, away) in enumerate([(own_far, away_far), (own_near, away_near)]):
        keep = lax.bitwise_xor(me[0], 2 - 2 * k)
        give = lax.bitwise_xor(me[0], 3 - 2 * k)
        own[...] = canvas[keep].reshape(shape)
        away[...] = canvas[give].reshape(shape).astype(jnp.bfloat16)


def sum_pieces(pos, me, first, second, bands, width):
    height = first.shape[2]
    smem = pl.BlockSpec(memory_space=pltpu.SMEM)
    vmem = pl.BlockSpec(memory_space=pltpu.VMEM)
    shape = (2, height, width)
    return pl.pallas_call(
        sum_kernel,
        in_specs=[smem, smem, vmem, vmem],
        out_specs=[vmem] * 4,
        out_shape=[
            jax.ShapeDtypeStruct(shape, kind)
            for kind in (jnp.float32, jnp.float32, jnp.bfloat16, jnp.bfloat16)
        ],
        scratch_shapes=[pltpu.VMEM((bands, 2 * height, width), jnp.float32)],
        compiler_params=pltpu.CompilerParams(vmem_limit_bytes=SUM_VMEM),
        cost_estimate=pl.CostEstimate(
            flops=8 * first.size, bytes_accessed=4 * first.size + 12 * math.prod(shape), transcendentals=0
        ),
    )(pos, me, first, second)


def shards(object_image, probe, amplitudes, pos_tile, pos_offset):
    owners = lax.axis_size("obj")
    classes = lax.axis_size("pat")
    my_owner = lax.axis_index("obj").astype(jnp.int32)
    my_class = lax.axis_index("pat").astype(jnp.int32)
    me = jnp.stack([my_owner, my_class])
    height = PATCH // classes
    width = object_image.shape[2]
    assert owners == 4 and object_image.shape[1] == PATCH and pos_tile.shape[0] == 2

    def flip(value, bit):
        return lax.ppermute(value, "obj", [(k, k ^ bit) for k in range(owners)])

    def pat_flip(bit):
        return lambda value: lax.ppermute(value, "pat", [(k, k ^ bit) for k in range(classes)])

    def halved(part, bit, other):
        rows = part.shape[0] // 2
        give = lax.dynamic_slice_in_dim(part, (1 - bit) * rows, rows, 0).astype(jnp.bfloat16)
        return lax.dynamic_slice_in_dim(part, bit * rows, rows, 0) + other(give).astype(jnp.float32)

    def doubled(part, bit, other):
        got = other(part)
        return jnp.where(bit == 0, jnp.concatenate([part, got]), jnp.concatenate([got, part]))

    bits = [1 << k for k in range(classes.bit_length() - 1)]
    own_pos = jnp.concatenate([pos_tile, pos_offset], 1)
    pos = lax.all_gather(own_pos, "obj", axis=0, tiled=True)

    first = cut(object_image, pos, me, 3, 0, 1)
    second, pieces = cut_rest(object_image, pos, me)
    second, pieces, then = lax.optimization_barrier((second, pieces, me))
    relay = [flip(first, 1), flip(second, 1)]
    sibling = flip(pieces, 1)
    merged = [cut_and_merge(object_image, relay[k], pos, then, k) for k in range(2)]
    merged[1], pos_pat = lax.optimization_barrier((merged[1], own_pos))
    across = [flip(m, 2) for m in merged]
    for bit in bits:
        pos_pat = doubled(pos_pat, my_class // bit % 2, pat_flip(bit))

    operands = (probe, amplitudes, dft_tables(PATCH))
    grad_0, term = wave(0, classes, pos, me, pos_pat, object_image, sibling, across[0], *operands, None)
    grad_0, across[1] = lax.optimization_barrier((grad_0, across[1]))
    part_0 = lax.all_to_all(grad_0, "pat", split_axis=0, concat_axis=0, tiled=True)
    grad_1, keep_term, give_term = wave(
        1, classes, pos, me, me, object_image, sibling, across[1], *operands, term
    )
    grad_1, part_0 = lax.optimization_barrier((grad_1, part_0))
    part_1 = lax.all_to_all(grad_1, "pat", split_axis=0, concat_axis=0, tiled=True)

    core = my_owner % 2
    line = my_owner // 2
    term = keep_term + flip(give_term, 1).astype(jnp.float32)
    term = halved(term, line, lambda value: flip(value, 2))
    term, then = lax.optimization_barrier((term, me))
    own_far, own_near, away_far, away_near = sum_pieces(
        pos_pat, then, part_0, part_1, owners, width
    )
    from_sibling_far = flip(away_far, 1)
    from_sibling = flip(away_near, 1)
    from_across = flip(
        (own_far + from_sibling_far.astype(jnp.float32)).astype(jnp.bfloat16), 2
    )
    for bit in bits:
        term = halved(term, my_class // bit % 2, pat_flip(bit))
    total = own_near + from_sibling.astype(jnp.float32) + from_across.astype(jnp.float32)
    mine = lax.dynamic_slice_in_dim(object_image, my_class * height, height, 1)
    updated = (mine.astype(jnp.float32) - OBJECT_RATE * total).astype(jnp.bfloat16)
    updated, term = lax.optimization_barrier((updated, term.astype(jnp.bfloat16)))
    steps = [
        functools.partial(doubled, bit=my_class // bit % 2, other=pat_flip(bit)) for bit in reversed(bits)
    ]
    steps.append(functools.partial(doubled, bit=line, other=lambda value: flip(value, 2)))
    steps.append(lambda part: doubled(part[None], core, lambda value: flip(value, 1)))
    object_next = lax.all_gather(updated, "pat", axis=1, tiled=True)
    for step in steps:
        term = step(term)
    probe_total = term.astype(jnp.float32)
    probe_next = probe - PROBE_RATE * probe_total
    return (object_next, probe_next)


def solution(mesh):
    return jax.shard_map(
        shards,
        mesh=mesh,
        in_specs=(
            P(None, "obj", None),
            P(),
            P(("pat", "obj"), None, None),
            P(("pat", "obj"), None),
            P(("pat", "obj"), None),
        ),
        out_specs=(P(None, "obj", None), P()),
        check_vma=False,
    )
```

```python
import functools
import math

import jax
import jax.numpy as jnp
import numpy as np
from jax import lax
from jax.experimental import pallas as pl
from jax.experimental.pallas import tpu as pltpu
from jax.sharding import PartitionSpec as P

PATCH = 512
TILE = 256
LANES = 128
WIDE = PATCH + LANES

OBJECT_RATE = 0.1
PROBE_RATE = 0.05
MAGNITUDE_FLOOR = 0.5
CUT_VMEM = 14 * 1024 * 1024
WAVE_VMEM = 56 * 1024 * 1024
SUM_VMEM = 24 * 1024 * 1024


def dft_tables(length):
    counter = np.arange(length, dtype=np.int32)
    phase_angle = (counter[:, None] * counter[None, :] % length).astype(np.float32) * np.float32(
        2.0 * math.pi / length
    )
    factor = np.float32(1.0 / math.sqrt(length))
    cosine = (np.cos(phase_angle) * factor).astype(jnp.bfloat16)
    sine_part = (-np.sin(phase_angle) * factor).astype(jnp.bfloat16)
    return jnp.asarray(cosine), jnp.asarray(sine_part), jnp.asarray(-sine_part)


def first_row(pos, index):
    return pos[index, 0] * TILE + pos[index, 2]


def first_col(pos, index):
    return pos[index, 1] * TILE + pos[index, 3]


def shifted_left(blocks, amount):
    turned = [pltpu.roll(b, lax.rem(LANES - amount, LANES), axis=1) for b in blocks]
    lane = lax.broadcasted_iota(jnp.int32, turned[0].shape, 1)
    stay = lane < LANES - amount
    return jnp.concatenate([jnp.where(stay, a, b) for a, b in zip(turned, turned[1:])], 1)


def shifted_right(data, amount):
    count = data.shape[1] // LANES
    turned = [pltpu.roll(data[:, LANES * k : LANES * (k + 1)], amount, axis=1) for k in range(count)]
    lane = lax.broadcasted_iota(jnp.int32, turned[0].shape, 1)
    stay = lane >= amount
    before = [jnp.zeros_like(turned[0])] + turned
    after = turned + [jnp.zeros_like(turned[0])]
    return jnp.concatenate([jnp.where(stay, a, b) for a, b in zip(after, before)], 1)


def band_of_rows(row_at, start, count):
    rows = lax.broadcasted_iota(jnp.int32, (count, PATCH), 0) + start
    return row_at // PATCH + (rows < lax.rem(row_at, PATCH)).astype(jnp.int32)


CHUNK = 64
SUBLANES = 8


def rows_from(ref, plane, start, count):
    aligned = pl.multiple_of(start // SUBLANES * SUBLANES, SUBLANES)
    amount = lax.rem(start, SUBLANES)
    data = ref[plane, pl.ds(aligned, count + SUBLANES), :]
    data = data.reshape(count // SUBLANES + 1, SUBLANES, data.shape[1])
    turned = pltpu.roll(data, lax.rem(SUBLANES - amount, SUBLANES), axis=1)
    row = lax.broadcasted_iota(jnp.int32, turned[1:].shape, 1)
    data = jnp.where(row < SUBLANES - amount, turned[:-1], turned[1:])
    return data.reshape(count, data.shape[2])


def cut_rows(blocks, plane, rows, amount):
    return shifted_left([b[plane, rows, :].astype(jnp.float32) for b in blocks], amount)


def cut_kernel(flip, first, pos, me, *refs):
    blocks, out = refs[:-1], refs[-1]
    target = lax.bitwise_xor(me[0], flip)
    amount = lax.rem(first_col(pos, 2 * target + first + pl.program_id(0)), LANES)

    def body(i, carry):
        rows = pl.ds(pl.multiple_of(i * CHUNK, CHUNK), CHUNK)
        for plane in range(2):
            out[0, plane, rows, :] = cut_rows(blocks, plane, rows, amount).astype(jnp.bfloat16)
        return carry

    lax.fori_loop(0, PATCH // CHUNK, body, 0)


def cut(band, pos, me, flip, first, count):
    def block(k):
        def index(i, pos, me):
            return (0, 0, first_col(pos, 2 * lax.bitwise_xor(me[0], flip) + first + i) // LANES + k)

        return pl.BlockSpec((2, PATCH, LANES), index)

    return pl.pallas_call(
        functools.partial(cut_kernel, flip, first),
        grid_spec=pltpu.PrefetchScalarGridSpec(
            num_scalar_prefetch=2,
            grid=(count,),
            in_specs=[block(k) for k in range(WIDE // LANES)],
            out_specs=pl.BlockSpec((1, 2, PATCH, PATCH), lambda i, pos, me: (i, 0, 0, 0)),
        ),
        out_shape=jax.ShapeDtypeStruct((count, 2, PATCH, PATCH), jnp.bfloat16),
        compiler_params=pltpu.CompilerParams(vmem_limit_bytes=CUT_VMEM),
        cost_estimate=pl.CostEstimate(
            flops=count * 2 * PATCH * WIDE, bytes_accessed=count * 2300000, transcendentals=0
        ),
    )(pos, me, *([band] * (WIDE // LANES)))


def merge_kernel(which, pos, me, *refs):
    blocks, sibling, out = refs[:-2], refs[-2], refs[-1]
    index = 2 * lax.bitwise_xor(me[0], 2) + which
    amount = lax.rem(first_col(pos, index), LANES)
    row_at = first_row(pos, index)

    def body(i, carry):
        rows = pl.ds(pl.multiple_of(i * CHUNK, CHUNK), CHUNK)
        mine = band_of_rows(row_at, i * CHUNK, CHUNK) == me[0]
        for plane in range(2):
            own = cut_rows(blocks, plane, rows, amount)
            other = sibling[0, plane, rows, :].astype(jnp.float32)
            out[plane, rows, :] = jnp.where(mine, own, other).astype(jnp.bfloat16)
        return carry

    lax.fori_loop(0, PATCH // CHUNK, body, 0)


def cut_and_merge(band, sibling, pos, me, which):
    def block(k):
        def index(i, pos, me):
            return (0, 0, first_col(pos, 2 * lax.bitwise_xor(me[0], 2) + which) // LANES + k)

        return pl.BlockSpec((2, PATCH, LANES), index)

    return pl.pallas_call(
        functools.partial(merge_kernel, which),
        grid_spec=pltpu.PrefetchScalarGridSpec(
            num_scalar_prefetch=2,
            grid=(1,),
            in_specs=[block(k) for k in range(WIDE // LANES)]
            + [pl.BlockSpec((1, 2, PATCH, PATCH), lambda i, pos, me: (0, 0, 0, 0))],
            out_specs=pl.BlockSpec((2, PATCH, PATCH), lambda i, pos, me: (0, 0, 0)),
        ),
        out_shape=jax.ShapeDtypeStruct((2, PATCH, PATCH), jnp.bfloat16),
        compiler_params=pltpu.CompilerParams(vmem_limit_bytes=CUT_VMEM),
        cost_estimate=pl.CostEstimate(
            flops=2 * PATCH * WIDE, bytes_accessed=3300000, transcendentals=0
        ),
    )(pos, me, *([band] * (WIDE // LANES)), sibling)


def rest_index(step, pos, me):
    return jnp.where(step == 0, 2 * lax.bitwise_xor(me[0], 3) + 1, 2 * lax.bitwise_xor(me[0], 1) + step - 1)


def rest_kernel(pos, me, *refs):
    blocks, second, pieces = refs[:-2], refs[-2], refs[-1]
    step = pl.program_id(0)
    amount = lax.rem(first_col(pos, rest_index(step, pos, me)), LANES)

    def take(out):
        def body(i, carry):
            rows = pl.ds(pl.multiple_of(i * CHUNK, CHUNK), CHUNK)
            for plane in range(2):
                out[0, plane, rows, :] = cut_rows(blocks, plane, rows, amount).astype(jnp.bfloat16)
            return carry

        lax.fori_loop(0, PATCH // CHUNK, body, 0)

    pl.when(step == 0)(lambda: take(second))
    pl.when(step > 0)(lambda: take(pieces))


def cut_rest(band, pos, me):
    def block(k):
        def index(i, pos, me):
            return (0, 0, first_col(pos, rest_index(i, pos, me)) // LANES + k)

        return pl.BlockSpec((2, PATCH, LANES), index)

    shape = (2, PATCH, PATCH)
    return pl.pallas_call(
        rest_kernel,
        grid_spec=pltpu.PrefetchScalarGridSpec(
            num_scalar_prefetch=2,
            grid=(3,),
            in_specs=[block(k) for k in range(WIDE // LANES)],
            out_specs=[
                pl.BlockSpec((1, *shape), lambda i, pos, me: (0, 0, 0, 0)),
                pl.BlockSpec((1, *shape), lambda i, pos, me: (jnp.maximum(i - 1, 0), 0, 0, 0)),
            ],
        ),
        out_shape=[
            jax.ShapeDtypeStruct((1, *shape), jnp.bfloat16),
            jax.ShapeDtypeStruct((2, *shape), jnp.bfloat16),
        ],
        compiler_params=pltpu.CompilerParams(vmem_limit_bytes=CUT_VMEM),
        cost_estimate=pl.CostEstimate(
            flops=6 * PATCH * WIDE, bytes_accessed=7000000, transcendentals=0
        ),
    )(pos, me, *([band] * (WIDE // LANES)))


def wave_kernel(which, pos, me, spare, band, sibling, across, probe, amplitudes, *refs):
    tables, refs = refs[:3], refs[3:]
    last = which == 1
    if last:
        term_in, real_grad, imag_grad, keep_term, give_term, *scratch = refs
        grads = [real_grad, imag_grad]
    else:
        both, term_out, *scratch = refs
        grads = [both.at[:, plane] for plane in range(2)]
    window, sib_v, far_v, probe_v, amp_v, matrix, term_v, patch_v, twice, field, half, sems = scratch
    index = 2 * me[0] + which
    col_at = first_col(pos, index)
    row_at = first_row(pos, index)
    start = pl.multiple_of(col_at // LANES * LANES, LANES)
    pairs = [
        (band.at[:, :, pl.ds(start, WIDE)], window),
        (sibling.at[which], sib_v),
        (across, far_v),
        (probe, probe_v),
    ]
    cosine, sine, minus = tables
    quarters = [(slice(0, PATCH), slice(0, PATCH)), (slice(0, PATCH), slice(PATCH, 2 * PATCH))]
    quarters += [(slice(PATCH, 2 * PATCH), slice(0, PATCH)), (slice(PATCH, 2 * PATCH), slice(PATCH, 2 * PATCH))]
    pairs += [(t, matrix.at[q]) for t, q in zip((cosine, minus, sine, cosine), quarters)]
    pairs.append((amplitudes.at[which], amp_v))
    if last:
        pairs.append((term_in, term_v))
    copies = [pltpu.make_async_copy(a, b, sems.at[k]) for k, (a, b) in enumerate(pairs)]
    for copy in copies:
        copy.start()
    for copy in copies[:3]:
        copy.wait()
    amount = lax.rem(col_at, LANES)
    down = lax.rem(row_at, PATCH)
    views = [window.at[:, :, LANES * k : LANES * (k + 1)] for k in range(WIDE // LANES)]

    def assemble(i, carry):
        at = pl.multiple_of(i * CHUNK, CHUNK)
        rows = pl.ds(at, CHUNK)
        owner = band_of_rows(row_at, at, CHUNK)
        mine = owner == me[0]
        near = owner == lax.bitwise_xor(me[0], 1)
        for plane in range(2):
            own = cut_rows(views, plane, rows, amount)
            beside = sib_v[plane, rows, :].astype(jnp.float32)
            beyond = far_v[plane, rows, :].astype(jnp.float32)
            patch = jnp.where(mine, own, jnp.where(near, beside, beyond))
            twice[plane, rows, :] = patch
            twice[plane, pl.ds(pl.multiple_of(at + PATCH, CHUNK), CHUNK), :] = patch
        return carry

    lax.fori_loop(0, PATCH // CHUNK, assemble, 0)
    copies[3].wait()

    def illuminate(i, carry):
        at = pl.multiple_of(i * CHUNK, CHUNK)
        rows = pl.ds(at, CHUNK)
        patch_real = rows_from(twice, 0, at + down, CHUNK)
        patch_imag = rows_from(twice, 1, at + down, CHUNK)
        patch_v[0, rows, :] = patch_real.astype(jnp.bfloat16)
        patch_v[1, rows, :] = patch_imag.astype(jnp.bfloat16)
        probe_real = probe_v[0, rows, :]
        probe_imag = probe_v[1, rows, :]
        field[rows, :] = (probe_real * patch_real - probe_imag * patch_imag).astype(jnp.bfloat16)
        field[pl.ds(pl.multiple_of(at + PATCH, CHUNK), CHUNK), :] = (
            probe_real * patch_imag + probe_imag * patch_real
        ).astype(jnp.bfloat16)
        return carry

    lax.fori_loop(0, PATCH // CHUNK, illuminate, 0)
    for copy in copies[4:8]:
        copy.wait()

    def over_rows():
        for k in range(4):
            part = jnp.dot(
                matrix[256 * k : 256 * (k + 1), :], field[...], preferred_element_type=jnp.float32
            ).astype(jnp.bfloat16)
            at = PATCH * (1 - k // 2)
            half[256 * (k % 2) : 256 * (k % 2 + 1), at : at + PATCH] = part

    over_rows()
    copies[8].wait()
    for k in range(2):
        rows = slice(256 * k, 256 * (k + 1))
        far = jnp.dot(half[rows, :], matrix[...], preferred_element_type=jnp.float32)
        far_imag = far[:, :PATCH]
        far_real = far[:, PATCH:]
        power = far_real * far_real + far_imag * far_imag
        keep = 1.0 - amp_v[rows, :].astype(jnp.float32) * lax.rsqrt(
            jnp.maximum(power, MAGNITUDE_FLOOR * MAGNITUDE_FLOOR)
        )
        field[rows, :] = (far_imag * keep).astype(jnp.bfloat16)
        field[PATCH + 256 * k : PATCH + 256 * (k + 1), :] = (far_real * keep).astype(jnp.bfloat16)
    over_rows()
    if last:
        copies[9].wait()
        core = lax.rem(me[0], 2)
    for k in range(2):
        rows = slice(256 * k, 256 * (k + 1))
        back = jnp.dot(half[rows, :], matrix[...], preferred_element_type=jnp.float32)
        back_real = back[:, :PATCH]
        back_imag = back[:, PATCH:]
        patch_real = patch_v[0, rows, :].astype(jnp.float32)
        patch_imag = patch_v[1, rows, :].astype(jnp.float32)
        term_real = patch_real * back_real + patch_imag * back_imag
        term_imag = patch_real * back_imag - patch_imag * back_real
        if last:
            term_real = term_real + term_v[0, rows, :]
            term_imag = term_imag + term_v[1, rows, :]
            keep_term[rows, :] = jnp.where(core == 0, term_real, term_imag)
            give_term[rows, :] = jnp.where(core == 0, term_imag, term_real).astype(jnp.bfloat16)
        else:
            term_out[0, rows, :] = term_real
            term_out[1, rows, :] = term_imag
        term_v[0, rows, :] = back_real
        term_v[1, rows, :] = back_imag

    def weigh(i, carry):
        at = pl.multiple_of(i * CHUNK, CHUNK)
        rows = pl.ds(at, CHUNK)
        again = pl.ds(pl.multiple_of(at + PATCH, CHUNK), CHUNK)
        probe_real = probe_v[0, rows, :]
        probe_imag = probe_v[1, rows, :]
        back_real = term_v[0, rows, :]
        back_imag = term_v[1, rows, :]
        grad_real = probe_real * back_real + probe_imag * back_imag
        grad_imag = probe_real * back_imag - probe_imag * back_real
        twice[0, rows, :] = grad_real
        twice[0, again, :] = grad_real
        twice[1, rows, :] = grad_imag
        twice[1, again, :] = grad_imag
        return carry

    lax.fori_loop(0, PATCH // CHUNK, weigh, 0)
    classes, height = grads[0].shape[0], grads[0].shape[1]

    def spread(k, carry):
        for plane in range(2):
            grads[plane][k] = rows_from(twice, plane, PATCH - down + k * height, height).astype(
                jnp.bfloat16
            )
        return carry

    lax.fori_loop(0, classes, spread, 0)


def wave(which, classes, pos, me, spare, band, sibling, across, probe, amplitudes, tables, term):
    operands = [band, sibling, across, probe, amplitudes, *tables]
    smem = pl.BlockSpec(memory_space=pltpu.SMEM)
    hbm = pl.BlockSpec(memory_space=pl.ANY)
    vmem = pl.BlockSpec(memory_space=pltpu.VMEM)
    planes = (2, PATCH, PATCH)
    plane = (PATCH, PATCH)
    height = PATCH // classes
    if term is None:
        grads = [jax.ShapeDtypeStruct((classes, 2, height, PATCH), jnp.bfloat16)]
        terms = [jax.ShapeDtypeStruct(planes, jnp.float32)]
    else:
        operands.append(term)
        grads = [jax.ShapeDtypeStruct((classes, height, PATCH), jnp.bfloat16)] * 2
        terms = [jax.ShapeDtypeStruct(plane, t) for t in (jnp.float32, jnp.bfloat16)]
    return pl.pallas_call(
        functools.partial(wave_kernel, which),
        in_specs=[smem, smem, smem] + [hbm] * len(operands),
        out_specs=[vmem] * len(grads + terms),
        out_shape=grads + terms,
        scratch_shapes=[
            pltpu.VMEM((2, PATCH, WIDE), jnp.bfloat16),
            pltpu.VMEM(planes, jnp.bfloat16),
            pltpu.VMEM(planes, jnp.bfloat16),
            pltpu.VMEM(planes, jnp.float32),
            pltpu.VMEM((PATCH, PATCH), jnp.bfloat16),
            pltpu.VMEM((2 * PATCH, 2 * PATCH), jnp.bfloat16),
            pltpu.VMEM(planes, jnp.float32),
            pltpu.VMEM(planes, jnp.bfloat16),
            pltpu.VMEM((2, 2 * PATCH + SUBLANES, PATCH), jnp.float32),
            pltpu.VMEM((2 * PATCH, PATCH), jnp.bfloat16),
            pltpu.VMEM((PATCH, 2 * PATCH), jnp.bfloat16),
            pltpu.SemaphoreType.DMA((10,)),
        ],
        compiler_params=pltpu.CompilerParams(vmem_limit_bytes=WAVE_VMEM),
        cost_estimate=pl.CostEstimate(
            flops=32 * PATCH**3, bytes_accessed=300_000_000, transcendentals=0
        ),
    )(pos, me, spare, *operands)


def sum_kernel(pos, me, first, second, own_far, own_near, away_far, away_near, canvas):
    classes, height = second.shape[0], second.shape[1]
    start = me[1] * height
    canvas[...] = jnp.zeros_like(canvas)
    rows = start + lax.broadcasted_iota(jnp.int32, (height, WIDE), 0)

    def piece(data, index):
        row_at = first_row(pos, index)
        col_at = first_col(pos, index)
        down = lax.rem(row_at, PATCH)
        at = pl.ds(pl.multiple_of(col_at // LANES * LANES, LANES), WIDE)
        data = shifted_right(data.astype(jnp.float32), lax.rem(col_at, LANES))

        @pl.when(down < start + height)
        def _():
            canvas[row_at // PATCH, :, at] += jnp.where(rows >= down, data, 0.0)

        @pl.when(down > start)
        def _():
            canvas[row_at // PATCH + 1, :, at] += jnp.where(rows < down, data, 0.0)

    def body(k, carry):
        piece(first[k, 0], 2 * k)
        piece(second[k], 2 * k + 1)
        return carry

    lax.fori_loop(0, classes, body, 0)
    for k, (own, away) in enumerate([(own_far, away_far), (own_near, away_near)]):
        own[...] = canvas[lax.bitwise_xor(me[0], 2 - 2 * k)]
        away[...] = canvas[lax.bitwise_xor(me[0], 3 - 2 * k)].astype(jnp.bfloat16)


def sum_pieces(plane, pos, me, first, second, bands, width):
    classes, height = second.shape[0], second.shape[1]
    smem = pl.BlockSpec(memory_space=pltpu.SMEM)
    shape = (height, width)
    return pl.pallas_call(
        sum_kernel,
        grid=(1,),
        in_specs=[
            smem,
            smem,
            pl.BlockSpec((classes, 1, height, PATCH), lambda i: (0, plane, 0, 0)),
            pl.BlockSpec((classes, height, PATCH), lambda i: (0, 0, 0)),
        ],
        out_specs=[pl.BlockSpec(shape, lambda i: (0, 0))] * 4,
        out_shape=[
            jax.ShapeDtypeStruct(shape, kind)
            for kind in (jnp.float32, jnp.float32, jnp.bfloat16, jnp.bfloat16)
        ],
        scratch_shapes=[pltpu.VMEM((bands, height, width), jnp.float32)],
        compiler_params=pltpu.CompilerParams(vmem_limit_bytes=SUM_VMEM),
        cost_estimate=pl.CostEstimate(
            flops=8 * second.size, bytes_accessed=4 * second.size + 12 * math.prod(shape), transcendentals=0
        ),
    )(pos, me, first, second)


def put_kernel(source, *refs):
    refs[-1][0] = source[...]


def put_plane(plane, source, buffer):
    parts = 4
    height, width = source.shape
    operands = [source] if buffer is None else [source, buffer]
    return pl.pallas_call(
        put_kernel,
        grid=(parts,),
        in_specs=[pl.BlockSpec((height // parts, width), lambda i: (i, 0))]
        + [pl.BlockSpec(memory_space=pl.ANY)] * (len(operands) - 1),
        out_specs=pl.BlockSpec((1, height // parts, width), lambda i: (plane, i, 0)),
        out_shape=jax.ShapeDtypeStruct((2, height, width), source.dtype),
        input_output_aliases={} if buffer is None else {1: 0},
        compiler_params=pltpu.CompilerParams(vmem_limit_bytes=SUM_VMEM),
        cost_estimate=pl.CostEstimate(flops=0, bytes_accessed=4 * source.size, transcendentals=0),
    )(*operands)


def shards(object_image, probe, amplitudes, pos_tile, pos_offset):
    owners = lax.axis_size("obj")
    classes = lax.axis_size("pat")
    my_owner = lax.axis_index("obj").astype(jnp.int32)
    my_class = lax.axis_index("pat").astype(jnp.int32)
    me = jnp.stack([my_owner, my_class])
    height = PATCH // classes
    width = object_image.shape[2]
    assert owners == 4 and object_image.shape[1] == PATCH and pos_tile.shape[0] == 2

    def flip(value, bit):
        return lax.ppermute(value, "obj", [(k, k ^ bit) for k in range(owners)])

    def pat_flip(bit):
        return lambda value: lax.ppermute(value, "pat", [(k, k ^ bit) for k in range(classes)])

    def halved(part, bit, other):
        rows = part.shape[0] // 2
        give = lax.dynamic_slice_in_dim(part, (1 - bit) * rows, rows, 0).astype(jnp.bfloat16)
        return lax.dynamic_slice_in_dim(part, bit * rows, rows, 0) + other(give).astype(jnp.float32)

    def doubled(part, bit, other):
        got = other(part)
        return jnp.where(bit == 0, jnp.concatenate([part, got]), jnp.concatenate([got, part]))

    bits = [1 << k for k in range(classes.bit_length() - 1)]
    own_pos = jnp.concatenate([pos_tile, pos_offset], 1)
    pos = lax.all_gather(own_pos, "obj", axis=0, tiled=True)

    first = cut(object_image, pos, me, 3, 0, 1)
    second, pieces = cut_rest(object_image, pos, me)
    second, pieces, then = lax.optimization_barrier((second, pieces, me))
    relay = [flip(first, 1), flip(second, 1)]
    sibling = flip(pieces, 1)
    merged = [cut_and_merge(object_image, relay[k], pos, then, k) for k in range(2)]
    merged[1], pos_pat = lax.optimization_barrier((merged[1], own_pos))
    across = [flip(m, 2) for m in merged]
    for bit in bits:
        pos_pat = doubled(pos_pat, my_class // bit % 2, pat_flip(bit))

    operands = (probe, amplitudes, dft_tables(PATCH))
    grad_0, term = wave(0, classes, pos, me, pos_pat, object_image, sibling, across[0], *operands, None)
    part_0 = lax.all_to_all(grad_0, "pat", split_axis=0, concat_axis=0, tiled=True)
    real_grad, imag_grad, keep_term, give_term = wave(
        1, classes, pos, me, me, object_image, sibling, across[1], *operands, term
    )
    real_grad, part_0 = lax.optimization_barrier((real_grad, part_0))
    real_part = lax.all_to_all(real_grad, "pat", split_axis=0, concat_axis=0, tiled=True)
    imag_grad, real_part = lax.optimization_barrier((imag_grad, real_part))
    imag_part = lax.all_to_all(imag_grad, "pat", split_axis=0, concat_axis=0, tiled=True)

    core = my_owner % 2
    line = my_owner // 2
    term = keep_term + flip(give_term, 1).astype(jnp.float32)
    term = halved(term, line, lambda value: flip(value, 2))

    def return_plane(plane, part, then, wait):
        own_far, own_near, away_far, away_near = sum_pieces(
            plane, pos_pat, then, part_0, part, owners, width
        )
        from_sibling_far = flip(away_far, 1)
        from_sibling = flip(away_near, 1)
        send = (own_far + from_sibling_far.astype(jnp.float32)).astype(jnp.bfloat16)
        send, wait = lax.optimization_barrier((send, wait))
        from_across = flip(send, 2)
        total = own_near + from_sibling.astype(jnp.float32) + from_across.astype(jnp.float32)
        mine = lax.dynamic_slice_in_dim(object_image[plane], my_class * height, height, 0)
        return (mine.astype(jnp.float32) - OBJECT_RATE * total).astype(jnp.bfloat16), wait

    real_rows, then = return_plane(0, real_part, me, me)
    term, then = lax.optimization_barrier((term, then))
    imag_rows, then = return_plane(1, imag_part, then, then)
    real_rows, term = lax.optimization_barrier((real_rows, term))
    for bit in bits:
        term = halved(term, my_class // bit % 2, pat_flip(bit))
    term = term.astype(jnp.bfloat16)
    steps = [
        functools.partial(doubled, bit=my_class // bit % 2, other=pat_flip(bit)) for bit in reversed(bits)
    ]
    steps.append(functools.partial(doubled, bit=line, other=lambda value: flip(value, 2)))
    steps.append(lambda part: doubled(part[None], core, lambda value: flip(value, 1)))
    object_next = put_plane(0, lax.all_gather(real_rows, "pat", axis=0, tiled=True), None)
    object_next = put_plane(1, lax.all_gather(imag_rows, "pat", axis=0, tiled=True), object_next)
    for step in steps:
        term = step(term)
    probe_total = term.astype(jnp.float32)
    probe_next = probe - PROBE_RATE * probe_total
    return (object_next, probe_next)


def solution(mesh):
    return jax.shard_map(
        shards,
        mesh=mesh,
        in_specs=(
            P(None, "obj", None),
            P(),
            P(("pat", "obj"), None, None),
            P(("pat", "obj"), None),
            P(("pat", "obj"), None),
        ),
        out_specs=(P(None, "obj", None), P()),
        check_vma=False,
    )
```

```python
import functools
import math

import jax
import jax.numpy as jnp
import numpy as np
from jax import lax
from jax.experimental import pallas as pl
from jax.experimental.pallas import tpu as pltpu
from jax.sharding import PartitionSpec as P

PATCH = 512
TILE = 256
LANES = 128
WIDE = PATCH + LANES

OBJECT_RATE = 0.1
PROBE_RATE = 0.05
MAGNITUDE_FLOOR = 0.5
CUT_VMEM = 14 * 1024 * 1024
WAVE_VMEM = 56 * 1024 * 1024
SUM_VMEM = 24 * 1024 * 1024


def dft_tables(length):
    counter = np.arange(length, dtype=np.int32)
    phase_angle = (counter[:, None] * counter[None, :] % length).astype(np.float32) * np.float32(
        2.0 * math.pi / length
    )
    factor = np.float32(1.0 / math.sqrt(length))
    cosine = (np.cos(phase_angle) * factor).astype(jnp.bfloat16)
    sine_part = (-np.sin(phase_angle) * factor).astype(jnp.bfloat16)
    return jnp.asarray(cosine), jnp.asarray(sine_part), jnp.asarray(-sine_part)


def first_row(pos, index):
    return pos[index, 0] * TILE + pos[index, 2]


def first_col(pos, index):
    return pos[index, 1] * TILE + pos[index, 3]


def shifted_left(blocks, amount):
    turned = [pltpu.roll(b, lax.rem(LANES - amount, LANES), axis=1) for b in blocks]
    lane = lax.broadcasted_iota(jnp.int32, turned[0].shape, 1)
    stay = lane < LANES - amount
    return jnp.concatenate([jnp.where(stay, a, b) for a, b in zip(turned, turned[1:])], 1)


def shifted_right(data, amount):
    count = data.shape[1] // LANES
    turned = [pltpu.roll(data[:, LANES * k : LANES * (k + 1)], amount, axis=1) for k in range(count)]
    lane = lax.broadcasted_iota(jnp.int32, turned[0].shape, 1)
    stay = lane >= amount
    before = [jnp.zeros_like(turned[0])] + turned
    after = turned + [jnp.zeros_like(turned[0])]
    return jnp.concatenate([jnp.where(stay, a, b) for a, b in zip(after, before)], 1)


def band_of_rows(row_at, start, count):
    rows = lax.broadcasted_iota(jnp.int32, (count, PATCH), 0) + start
    return row_at // PATCH + (rows < lax.rem(row_at, PATCH)).astype(jnp.int32)


CHUNK = 64
SUBLANES = 8


def rows_from(ref, plane, start, count):
    aligned = pl.multiple_of(start // SUBLANES * SUBLANES, SUBLANES)
    amount = lax.rem(start, SUBLANES)
    data = ref[plane, pl.ds(aligned, count + SUBLANES), :]
    data = data.reshape(count // SUBLANES + 1, SUBLANES, data.shape[1])
    turned = pltpu.roll(data, lax.rem(SUBLANES - amount, SUBLANES), axis=1)
    row = lax.broadcasted_iota(jnp.int32, turned[1:].shape, 1)
    data = jnp.where(row < SUBLANES - amount, turned[:-1], turned[1:])
    return data.reshape(count, data.shape[2])


def cut_rows(blocks, plane, rows, amount):
    return shifted_left([b[plane, rows, :].astype(jnp.float32) for b in blocks], amount)


def cut_kernel(flip, first, pos, me, *refs):
    blocks, out = refs[:-1], refs[-1]
    target = lax.bitwise_xor(me[0], flip)
    amount = lax.rem(first_col(pos, 2 * target + first + pl.program_id(0)), LANES)

    def body(i, carry):
        rows = pl.ds(pl.multiple_of(i * CHUNK, CHUNK), CHUNK)
        for plane in range(2):
            out[0, plane, rows, :] = cut_rows(blocks, plane, rows, amount).astype(jnp.bfloat16)
        return carry

    lax.fori_loop(0, PATCH // CHUNK, body, 0)


def cut(band, pos, me, flip, first, count):
    def block(k):
        def index(i, pos, me):
            return (0, 0, first_col(pos, 2 * lax.bitwise_xor(me[0], flip) + first + i) // LANES + k)

        return pl.BlockSpec((2, PATCH, LANES), index)

    return pl.pallas_call(
        functools.partial(cut_kernel, flip, first),
        grid_spec=pltpu.PrefetchScalarGridSpec(
            num_scalar_prefetch=2,
            grid=(count,),
            in_specs=[block(k) for k in range(WIDE // LANES)],
            out_specs=pl.BlockSpec((1, 2, PATCH, PATCH), lambda i, pos, me: (i, 0, 0, 0)),
        ),
        out_shape=jax.ShapeDtypeStruct((count, 2, PATCH, PATCH), jnp.bfloat16),
        compiler_params=pltpu.CompilerParams(vmem_limit_bytes=CUT_VMEM),
        cost_estimate=pl.CostEstimate(
            flops=count * 2 * PATCH * WIDE, bytes_accessed=count * 2300000, transcendentals=0
        ),
    )(pos, me, *([band] * (WIDE // LANES)))


def merge_kernel(which, pos, me, *refs):
    blocks, sibling, outs = refs[:-3], refs[-3], refs[-2:]
    index = 2 * lax.bitwise_xor(me[0], 2) + which
    amount = lax.rem(first_col(pos, index), LANES)
    row_at = first_row(pos, index)

    def body(i, carry):
        rows = pl.ds(pl.multiple_of(i * CHUNK, CHUNK), CHUNK)
        mine = band_of_rows(row_at, i * CHUNK, CHUNK) == me[0]
        for plane in range(2):
            own = cut_rows(blocks, plane, rows, amount)
            other = sibling[0, plane, rows, :].astype(jnp.float32)
            outs[plane][rows, :] = jnp.where(mine, own, other).astype(jnp.bfloat16)
        return carry

    lax.fori_loop(0, PATCH // CHUNK, body, 0)


def cut_and_merge(band, sibling, pos, me, which):
    def block(k):
        def index(i, pos, me):
            return (0, 0, first_col(pos, 2 * lax.bitwise_xor(me[0], 2) + which) // LANES + k)

        return pl.BlockSpec((2, PATCH, LANES), index)

    return pl.pallas_call(
        functools.partial(merge_kernel, which),
        grid_spec=pltpu.PrefetchScalarGridSpec(
            num_scalar_prefetch=2,
            grid=(1,),
            in_specs=[block(k) for k in range(WIDE // LANES)]
            + [pl.BlockSpec((1, 2, PATCH, PATCH), lambda i, pos, me: (0, 0, 0, 0))],
            out_specs=[pl.BlockSpec((PATCH, PATCH), lambda i, pos, me: (0, 0))] * 2,
        ),
        out_shape=[jax.ShapeDtypeStruct((PATCH, PATCH), jnp.bfloat16)] * 2,
        compiler_params=pltpu.CompilerParams(vmem_limit_bytes=CUT_VMEM),
        cost_estimate=pl.CostEstimate(
            flops=2 * PATCH * WIDE, bytes_accessed=3300000, transcendentals=0
        ),
    )(pos, me, *([band] * (WIDE // LANES)), sibling)


def rest_index(step, pos, me):
    return jnp.where(step == 0, 2 * lax.bitwise_xor(me[0], 3) + 1, 2 * lax.bitwise_xor(me[0], 1) + step - 1)


def rest_kernel(pos, me, *refs):
    blocks, second, pieces = refs[:-2], refs[-2], refs[-1]
    step = pl.program_id(0)
    amount = lax.rem(first_col(pos, rest_index(step, pos, me)), LANES)

    def take(out):
        def body(i, carry):
            rows = pl.ds(pl.multiple_of(i * CHUNK, CHUNK), CHUNK)
            for plane in range(2):
                out[0, plane, rows, :] = cut_rows(blocks, plane, rows, amount).astype(jnp.bfloat16)
            return carry

        lax.fori_loop(0, PATCH // CHUNK, body, 0)

    pl.when(step == 0)(lambda: take(second))
    pl.when(step > 0)(lambda: take(pieces))


def cut_rest(band, pos, me):
    def block(k):
        def index(i, pos, me):
            return (0, 0, first_col(pos, rest_index(i, pos, me)) // LANES + k)

        return pl.BlockSpec((2, PATCH, LANES), index)

    shape = (2, PATCH, PATCH)
    return pl.pallas_call(
        rest_kernel,
        grid_spec=pltpu.PrefetchScalarGridSpec(
            num_scalar_prefetch=2,
            grid=(3,),
            in_specs=[block(k) for k in range(WIDE // LANES)],
            out_specs=[
                pl.BlockSpec((1, *shape), lambda i, pos, me: (0, 0, 0, 0)),
                pl.BlockSpec((1, *shape), lambda i, pos, me: (jnp.maximum(i - 1, 0), 0, 0, 0)),
            ],
        ),
        out_shape=[
            jax.ShapeDtypeStruct((1, *shape), jnp.bfloat16),
            jax.ShapeDtypeStruct((2, *shape), jnp.bfloat16),
        ],
        compiler_params=pltpu.CompilerParams(vmem_limit_bytes=CUT_VMEM),
        cost_estimate=pl.CostEstimate(
            flops=6 * PATCH * WIDE, bytes_accessed=7000000, transcendentals=0
        ),
    )(pos, me, *([band] * (WIDE // LANES)))


def wave_kernel(which, pos, me, spare, band, sibling, across_real, across_imag, probe, amplitudes, *refs):
    tables, refs = refs[:3], refs[3:]
    last = which == 1
    if last:
        term_in, both, keep_term, give_term, *scratch = refs
    else:
        both, term_out, *scratch = refs
    window, sib_v, far_v, probe_v, amp_v, matrix, term_v, patch_v, twice, field, half, sems = scratch
    index = 2 * me[0] + which
    col_at = first_col(pos, index)
    row_at = first_row(pos, index)
    start = pl.multiple_of(col_at // LANES * LANES, LANES)
    pairs = [
        (band.at[:, :, pl.ds(start, WIDE)], window),
        (sibling.at[which], sib_v),
        (across_real, far_v.at[0]),
        (across_imag, far_v.at[1]),
        (probe, probe_v),
    ]
    cosine, sine, minus = tables
    quarters = [(slice(0, PATCH), slice(0, PATCH)), (slice(0, PATCH), slice(PATCH, 2 * PATCH))]
    quarters += [(slice(PATCH, 2 * PATCH), slice(0, PATCH)), (slice(PATCH, 2 * PATCH), slice(PATCH, 2 * PATCH))]
    pairs += [(t, matrix.at[q]) for t, q in zip((cosine, minus, sine, cosine), quarters)]
    pairs.append((amplitudes.at[which], amp_v))
    if last:
        pairs.append((term_in, term_v))
    copies = [pltpu.make_async_copy(a, b, sems.at[k]) for k, (a, b) in enumerate(pairs)]
    for copy in copies:
        copy.start()
    for copy in copies[:4]:
        copy.wait()
    amount = lax.rem(col_at, LANES)
    down = lax.rem(row_at, PATCH)
    views = [window.at[:, :, LANES * k : LANES * (k + 1)] for k in range(WIDE // LANES)]

    def assemble(i, carry):
        at = pl.multiple_of(i * CHUNK, CHUNK)
        rows = pl.ds(at, CHUNK)
        owner = band_of_rows(row_at, at, CHUNK)
        mine = owner == me[0]
        near = owner == lax.bitwise_xor(me[0], 1)
        for plane in range(2):
            own = cut_rows(views, plane, rows, amount)
            beside = sib_v[plane, rows, :].astype(jnp.float32)
            beyond = far_v[plane, rows, :].astype(jnp.float32)
            patch = jnp.where(mine, own, jnp.where(near, beside, beyond))
            twice[plane, rows, :] = patch
            twice[plane, pl.ds(pl.multiple_of(at + PATCH, CHUNK), CHUNK), :] = patch
        return carry

    lax.fori_loop(0, PATCH // CHUNK, assemble, 0)
    copies[4].wait()

    def illuminate(i, carry):
        at = pl.multiple_of(i * CHUNK, CHUNK)
        rows = pl.ds(at, CHUNK)
        patch_real = rows_from(twice, 0, at + down, CHUNK)
        patch_imag = rows_from(twice, 1, at + down, CHUNK)
        patch_v[0, rows, :] = patch_real.astype(jnp.bfloat16)
        patch_v[1, rows, :] = patch_imag.astype(jnp.bfloat16)
        probe_real = probe_v[0, rows, :]
        probe_imag = probe_v[1, rows, :]
        field[rows, :] = (probe_real * patch_real - probe_imag * patch_imag).astype(jnp.bfloat16)
        field[pl.ds(pl.multiple_of(at + PATCH, CHUNK), CHUNK), :] = (
            probe_real * patch_imag + probe_imag * patch_real
        ).astype(jnp.bfloat16)
        return carry

    lax.fori_loop(0, PATCH // CHUNK, illuminate, 0)
    for copy in copies[5:9]:
        copy.wait()

    def over_rows():
        for k in range(4):
            part = jnp.dot(
                matrix[256 * k : 256 * (k + 1), :], field[...], preferred_element_type=jnp.float32
            ).astype(jnp.bfloat16)
            at = PATCH * (1 - k // 2)
            half[256 * (k % 2) : 256 * (k % 2 + 1), at : at + PATCH] = part

    over_rows()
    copies[9].wait()
    for k in range(2):
        rows = slice(256 * k, 256 * (k + 1))
        far = jnp.dot(half[rows, :], matrix[...], preferred_element_type=jnp.float32)
        far_imag = far[:, :PATCH]
        far_real = far[:, PATCH:]
        power = far_real * far_real + far_imag * far_imag
        keep = 1.0 - amp_v[rows, :].astype(jnp.float32) * lax.rsqrt(
            jnp.maximum(power, MAGNITUDE_FLOOR * MAGNITUDE_FLOOR)
        )
        field[rows, :] = (far_imag * keep).astype(jnp.bfloat16)
        field[PATCH + 256 * k : PATCH + 256 * (k + 1), :] = (far_real * keep).astype(jnp.bfloat16)
    over_rows()
    if last:
        copies[10].wait()
        core = lax.rem(me[0], 2)
    for k in range(2):
        rows = slice(256 * k, 256 * (k + 1))
        back = jnp.dot(half[rows, :], matrix[...], preferred_element_type=jnp.float32)
        back_real = back[:, :PATCH]
        back_imag = back[:, PATCH:]
        patch_real = patch_v[0, rows, :].astype(jnp.float32)
        patch_imag = patch_v[1, rows, :].astype(jnp.float32)
        term_real = patch_real * back_real + patch_imag * back_imag
        term_imag = patch_real * back_imag - patch_imag * back_real
        if last:
            term_real = term_real + term_v[0, rows, :]
            term_imag = term_imag + term_v[1, rows, :]
            keep_term[rows, :] = jnp.where(core == 0, term_real, term_imag)
            give_term[rows, :] = jnp.where(core == 0, term_imag, term_real).astype(jnp.bfloat16)
        else:
            term_out[0, rows, :] = term_real
            term_out[1, rows, :] = term_imag
        term_v[0, rows, :] = back_real
        term_v[1, rows, :] = back_imag

    def weigh(i, carry):
        at = pl.multiple_of(i * CHUNK, CHUNK)
        rows = pl.ds(at, CHUNK)
        again = pl.ds(pl.multiple_of(at + PATCH, CHUNK), CHUNK)
        probe_real = probe_v[0, rows, :]
        probe_imag = probe_v[1, rows, :]
        back_real = term_v[0, rows, :]
        back_imag = term_v[1, rows, :]
        grad_real = probe_real * back_real + probe_imag * back_imag
        grad_imag = probe_real * back_imag - probe_imag * back_real
        twice[0, rows, :] = grad_real
        twice[0, again, :] = grad_real
        twice[1, rows, :] = grad_imag
        twice[1, again, :] = grad_imag
        return carry

    lax.fori_loop(0, PATCH // CHUNK, weigh, 0)
    classes, height = both.shape[0], both.shape[2]

    def spread(k, carry):
        for plane in range(2):
            both[k, plane] = rows_from(twice, plane, PATCH - down + k * height, height).astype(
                jnp.bfloat16
            )
        return carry

    lax.fori_loop(0, classes, spread, 0)


def wave(which, classes, pos, me, spare, band, sibling, across, probe, amplitudes, tables, term):
    operands = [band, sibling, *across, probe, amplitudes, *tables]
    smem = pl.BlockSpec(memory_space=pltpu.SMEM)
    hbm = pl.BlockSpec(memory_space=pl.ANY)
    vmem = pl.BlockSpec(memory_space=pltpu.VMEM)
    planes = (2, PATCH, PATCH)
    plane = (PATCH, PATCH)
    height = PATCH // classes
    grads = [jax.ShapeDtypeStruct((classes, 2, height, PATCH), jnp.bfloat16)]
    if term is None:
        terms = [jax.ShapeDtypeStruct(planes, jnp.float32)]
    else:
        operands.append(term)
        terms = [jax.ShapeDtypeStruct(plane, t) for t in (jnp.float32, jnp.bfloat16)]
    return pl.pallas_call(
        functools.partial(wave_kernel, which),
        in_specs=[smem, smem, smem] + [hbm] * len(operands),
        out_specs=[vmem] * len(grads + terms),
        out_shape=grads + terms,
        scratch_shapes=[
            pltpu.VMEM((2, PATCH, WIDE), jnp.bfloat16),
            pltpu.VMEM(planes, jnp.bfloat16),
            pltpu.VMEM(planes, jnp.bfloat16),
            pltpu.VMEM(planes, jnp.float32),
            pltpu.VMEM((PATCH, PATCH), jnp.bfloat16),
            pltpu.VMEM((2 * PATCH, 2 * PATCH), jnp.bfloat16),
            pltpu.VMEM(planes, jnp.float32),
            pltpu.VMEM(planes, jnp.bfloat16),
            pltpu.VMEM((2, 2 * PATCH + SUBLANES, PATCH), jnp.float32),
            pltpu.VMEM((2 * PATCH, PATCH), jnp.bfloat16),
            pltpu.VMEM((PATCH, 2 * PATCH), jnp.bfloat16),
            pltpu.SemaphoreType.DMA((11,)),
        ],
        compiler_params=pltpu.CompilerParams(vmem_limit_bytes=WAVE_VMEM),
        cost_estimate=pl.CostEstimate(
            flops=32 * PATCH**3, bytes_accessed=300_000_000, transcendentals=0
        ),
    )(pos, me, spare, *operands)


def sum_kernel(pos, me, first, second, own_far, own_near, away_far, away_near, canvas):
    classes, height = second.shape[0], second.shape[2]
    start = me[1] * height
    canvas[...] = jnp.zeros_like(canvas)
    rows = start + lax.broadcasted_iota(jnp.int32, (height, WIDE), 0)

    def piece(data, index):
        row_at = first_row(pos, index)
        col_at = first_col(pos, index)
        down = lax.rem(row_at, PATCH)
        at = pl.ds(pl.multiple_of(col_at // LANES * LANES, LANES), WIDE)
        data = shifted_right(data.astype(jnp.float32), lax.rem(col_at, LANES))

        @pl.when(down < start + height)
        def _():
            canvas[row_at // PATCH, :, at] += jnp.where(rows >= down, data, 0.0)

        @pl.when(down > start)
        def _():
            canvas[row_at // PATCH + 1, :, at] += jnp.where(rows < down, data, 0.0)

    def body(k, carry):
        piece(first[k, 0], 2 * k)
        piece(second[k, 0], 2 * k + 1)
        return carry

    lax.fori_loop(0, classes, body, 0)
    for k, (own, away) in enumerate([(own_far, away_far), (own_near, away_near)]):
        own[...] = canvas[lax.bitwise_xor(me[0], 2 - 2 * k)]
        away[...] = canvas[lax.bitwise_xor(me[0], 3 - 2 * k)].astype(jnp.bfloat16)


def sum_pieces(plane, pos, me, first, second, bands, width):
    classes, height = second.shape[0], second.shape[2]
    smem = pl.BlockSpec(memory_space=pltpu.SMEM)
    shape = (height, width)
    return pl.pallas_call(
        sum_kernel,
        grid=(1,),
        in_specs=[
            smem,
            smem,
            pl.BlockSpec((classes, 1, height, PATCH), lambda i: (0, plane, 0, 0)),
            pl.BlockSpec((classes, 1, height, PATCH), lambda i: (0, plane, 0, 0)),
        ],
        out_specs=[pl.BlockSpec(shape, lambda i: (0, 0))] * 4,
        out_shape=[
            jax.ShapeDtypeStruct(shape, kind)
            for kind in (jnp.float32, jnp.float32, jnp.bfloat16, jnp.bfloat16)
        ],
        scratch_shapes=[pltpu.VMEM((bands, height, width), jnp.float32)],
        compiler_params=pltpu.CompilerParams(vmem_limit_bytes=SUM_VMEM),
        cost_estimate=pl.CostEstimate(
            flops=8 * second.size, bytes_accessed=4 * second.size + 12 * math.prod(shape), transcendentals=0
        ),
    )(pos, me, first, second)


def put_kernel(source, *refs):
    refs[-1][0] = source[...]


def put_plane(plane, source, buffer):
    parts = 4
    height, width = source.shape
    operands = [source] if buffer is None else [source, buffer]
    return pl.pallas_call(
        put_kernel,
        grid=(parts,),
        in_specs=[pl.BlockSpec((height // parts, width), lambda i: (i, 0))]
        + [pl.BlockSpec(memory_space=pl.ANY)] * (len(operands) - 1),
        out_specs=pl.BlockSpec((1, height // parts, width), lambda i: (plane, i, 0)),
        out_shape=jax.ShapeDtypeStruct((2, height, width), source.dtype),
        input_output_aliases={} if buffer is None else {1: 0},
        compiler_params=pltpu.CompilerParams(vmem_limit_bytes=SUM_VMEM),
        cost_estimate=pl.CostEstimate(flops=0, bytes_accessed=4 * source.size, transcendentals=0),
    )(*operands)


def shards(object_image, probe, amplitudes, pos_tile, pos_offset):
    owners = lax.axis_size("obj")
    classes = lax.axis_size("pat")
    my_owner = lax.axis_index("obj").astype(jnp.int32)
    my_class = lax.axis_index("pat").astype(jnp.int32)
    me = jnp.stack([my_owner, my_class])
    height = PATCH // classes
    width = object_image.shape[2]
    assert owners == 4 and object_image.shape[1] == PATCH and pos_tile.shape[0] == 2

    def flip(value, bit):
        return lax.ppermute(value, "obj", [(k, k ^ bit) for k in range(owners)])

    def pat_flip(bit):
        return lambda value: lax.ppermute(value, "pat", [(k, k ^ bit) for k in range(classes)])

    def halved(part, bit, other):
        rows = part.shape[0] // 2
        give = lax.dynamic_slice_in_dim(part, (1 - bit) * rows, rows, 0).astype(jnp.bfloat16)
        return lax.dynamic_slice_in_dim(part, bit * rows, rows, 0) + other(give).astype(jnp.float32)

    def doubled(part, bit, other):
        got = other(part)
        return jnp.where(bit == 0, jnp.concatenate([part, got]), jnp.concatenate([got, part]))

    bits = [1 << k for k in range(classes.bit_length() - 1)]
    own_pos = jnp.concatenate([pos_tile, pos_offset], 1)
    pos = lax.all_gather(own_pos, "obj", axis=0, tiled=True)

    first = cut(object_image, pos, me, 3, 0, 1)
    second, pieces = cut_rest(object_image, pos, me)
    second, pieces, then = lax.optimization_barrier((second, pieces, me))
    relay = [flip(first, 1), flip(second, 1)]
    sibling = flip(pieces, 1)
    merged = [cut_and_merge(object_image, relay[k], pos, then, k) for k in range(2)]
    merged[1], pos_pat = lax.optimization_barrier((merged[1], own_pos))
    across = [[flip(plane, 2) for plane in planes] for planes in merged]
    for bit in bits:
        pos_pat = doubled(pos_pat, my_class // bit % 2, pat_flip(bit))

    operands = (probe, amplitudes, dft_tables(PATCH))
    grad_0, term = wave(0, classes, pos, me, pos_pat, object_image, sibling, across[0], *operands, None)
    grad_0, across[1][0] = lax.optimization_barrier((grad_0, across[1][0]))
    part_0 = lax.all_to_all(grad_0, "pat", split_axis=0, concat_axis=0, tiled=True)
    grad_1, keep_term, give_term = wave(
        1, classes, pos, me, me, object_image, sibling, across[1], *operands, term
    )
    grad_1, part_0 = lax.optimization_barrier((grad_1, part_0))
    part_1 = lax.all_to_all(grad_1, "pat", split_axis=0, concat_axis=0, tiled=True)

    core = my_owner % 2
    line = my_owner // 2
    term = keep_term + flip(give_term, 1).astype(jnp.float32)
    term = halved(term, line, lambda value: flip(value, 2))

    def return_plane(plane, then, wait):
        own_far, own_near, away_far, away_near = sum_pieces(
            plane, pos_pat, then, part_0, part_1, owners, width
        )
        from_sibling_far = flip(away_far, 1)
        from_sibling = flip(away_near, 1)
        send = (own_far + from_sibling_far.astype(jnp.float32)).astype(jnp.bfloat16)
        send, wait = lax.optimization_barrier((send, wait))
        from_across = flip(send, 2)
        total = own_near + from_sibling.astype(jnp.float32) + from_across.astype(jnp.float32)
        mine = lax.dynamic_slice(
            object_image, (plane, my_class * height, 0), (1, height, width)
        ).reshape(height, width)
        return (mine.astype(jnp.float32) - OBJECT_RATE * total).astype(jnp.bfloat16), wait

    term, then = lax.optimization_barrier((term, me))
    real_rows, then = return_plane(0, then, me)
    imag_rows, then = return_plane(1, then, then)
    real_rows, term = lax.optimization_barrier((real_rows, term))
    for bit in bits:
        term = halved(term, my_class // bit % 2, pat_flip(bit))
    term = term.astype(jnp.bfloat16)
    steps = [
        functools.partial(doubled, bit=my_class // bit % 2, other=pat_flip(bit)) for bit in reversed(bits)
    ]
    steps.append(functools.partial(doubled, bit=line, other=lambda value: flip(value, 2)))
    steps.append(lambda part: doubled(part[None], core, lambda value: flip(value, 1)))
    object_next = put_plane(0, lax.all_gather(real_rows, "pat", axis=0, tiled=True), None)
    object_next = put_plane(1, lax.all_gather(imag_rows, "pat", axis=0, tiled=True), object_next)
    for step in steps:
        term = step(term)
    probe_total = term.astype(jnp.float32)
    probe_next = probe - PROBE_RATE * probe_total
    return (object_next, probe_next)


def solution(mesh):
    return jax.shard_map(
        shards,
        mesh=mesh,
        in_specs=(
            P(None, "obj", None),
            P(),
            P(("pat", "obj"), None, None),
            P(("pat", "obj"), None),
            P(("pat", "obj"), None),
        ),
        out_specs=(P(None, "obj", None), P()),
        check_vma=False,
    )
```

```python
import functools
import math

import jax
import jax.numpy as jnp
import numpy as np
from jax import lax
from jax.experimental import pallas as pl
from jax.experimental.pallas import tpu as pltpu
from jax.sharding import PartitionSpec as P

PATCH = 512
TILE = 256
LANES = 128
WIDE = PATCH + LANES

OBJECT_RATE = 0.1
PROBE_RATE = 0.05
MAGNITUDE_FLOOR = 0.5
CUT_VMEM = 14 * 1024 * 1024
WAVE_VMEM = 56 * 1024 * 1024
SUM_VMEM = 24 * 1024 * 1024
BY_PERMUTE = (4, 8)


def dft_tables(length):
    counter = np.arange(length, dtype=np.int32)
    phase_angle = (counter[:, None] * counter[None, :] % length).astype(np.float32) * np.float32(
        2.0 * math.pi / length
    )
    factor = np.float32(1.0 / math.sqrt(length))
    cosine = (np.cos(phase_angle) * factor).astype(jnp.bfloat16)
    sine_part = (-np.sin(phase_angle) * factor).astype(jnp.bfloat16)
    return jnp.asarray(cosine), jnp.asarray(sine_part), jnp.asarray(-sine_part)


def first_row(pos, index):
    return pos[index, 0] * TILE + pos[index, 2]


def first_col(pos, index):
    return pos[index, 1] * TILE + pos[index, 3]


def shifted_left(blocks, amount):
    turned = [pltpu.roll(b, lax.rem(LANES - amount, LANES), axis=1) for b in blocks]
    lane = lax.broadcasted_iota(jnp.int32, turned[0].shape, 1)
    stay = lane < LANES - amount
    return jnp.concatenate([jnp.where(stay, a, b) for a, b in zip(turned, turned[1:])], 1)


def shifted_right(data, amount):
    count = data.shape[1] // LANES
    turned = [pltpu.roll(data[:, LANES * k : LANES * (k + 1)], amount, axis=1) for k in range(count)]
    lane = lax.broadcasted_iota(jnp.int32, turned[0].shape, 1)
    stay = lane >= amount
    before = [jnp.zeros_like(turned[0])] + turned
    after = turned + [jnp.zeros_like(turned[0])]
    return jnp.concatenate([jnp.where(stay, a, b) for a, b in zip(after, before)], 1)


def band_of_rows(row_at, start, count):
    rows = lax.broadcasted_iota(jnp.int32, (count, PATCH), 0) + start
    return row_at // PATCH + (rows < lax.rem(row_at, PATCH)).astype(jnp.int32)


CHUNK = 64
SUBLANES = 8


def rows_from(ref, plane, start, count):
    aligned = pl.multiple_of(start // SUBLANES * SUBLANES, SUBLANES)
    amount = lax.rem(start, SUBLANES)
    data = ref[plane, pl.ds(aligned, count + SUBLANES), :]
    data = data.reshape(count // SUBLANES + 1, SUBLANES, data.shape[1])
    turned = pltpu.roll(data, lax.rem(SUBLANES - amount, SUBLANES), axis=1)
    row = lax.broadcasted_iota(jnp.int32, turned[1:].shape, 1)
    data = jnp.where(row < SUBLANES - amount, turned[:-1], turned[1:])
    return data.reshape(count, data.shape[2])


def cut_rows(blocks, plane, rows, amount):
    return shifted_left([b[plane, rows, :].astype(jnp.float32) for b in blocks], amount)


def cut_kernel(flip, first, pos, me, *refs):
    blocks, out = refs[:-1], refs[-1]
    target = lax.bitwise_xor(me[0], flip)
    amount = lax.rem(first_col(pos, 2 * target + first + pl.program_id(0)), LANES)

    def body(i, carry):
        rows = pl.ds(pl.multiple_of(i * CHUNK, CHUNK), CHUNK)
        for plane in range(2):
            out[0, plane, rows, :] = cut_rows(blocks, plane, rows, amount).astype(jnp.bfloat16)
        return carry

    lax.fori_loop(0, PATCH // CHUNK, body, 0)


def cut(band, pos, me, flip, first, count):
    def block(k):
        def index(i, pos, me):
            return (0, 0, first_col(pos, 2 * lax.bitwise_xor(me[0], flip) + first + i) // LANES + k)

        return pl.BlockSpec((2, PATCH, LANES), index)

    return pl.pallas_call(
        functools.partial(cut_kernel, flip, first),
        grid_spec=pltpu.PrefetchScalarGridSpec(
            num_scalar_prefetch=2,
            grid=(count,),
            in_specs=[block(k) for k in range(WIDE // LANES)],
            out_specs=pl.BlockSpec((1, 2, PATCH, PATCH), lambda i, pos, me: (i, 0, 0, 0)),
        ),
        out_shape=jax.ShapeDtypeStruct((count, 2, PATCH, PATCH), jnp.bfloat16),
        compiler_params=pltpu.CompilerParams(vmem_limit_bytes=CUT_VMEM),
        cost_estimate=pl.CostEstimate(
            flops=count * 2 * PATCH * WIDE, bytes_accessed=count * 2300000, transcendentals=0
        ),
    )(pos, me, *([band] * (WIDE // LANES)))


def merge_kernel(which, pos, me, *refs):
    blocks, sibling, out = refs[:-2], refs[-2], refs[-1]
    index = 2 * lax.bitwise_xor(me[0], 2) + which
    amount = lax.rem(first_col(pos, index), LANES)
    row_at = first_row(pos, index)

    def body(i, carry):
        rows = pl.ds(pl.multiple_of(i * CHUNK, CHUNK), CHUNK)
        mine = band_of_rows(row_at, i * CHUNK, CHUNK) == me[0]
        for plane in range(2):
            own = cut_rows(blocks, plane, rows, amount)
            other = sibling[0, plane, rows, :].astype(jnp.float32)
            out[plane, rows, :] = jnp.where(mine, own, other).astype(jnp.bfloat16)
        return carry

    lax.fori_loop(0, PATCH // CHUNK, body, 0)


def cut_and_merge(band, sibling, pos, me, which):
    def block(k):
        def index(i, pos, me):
            return (0, 0, first_col(pos, 2 * lax.bitwise_xor(me[0], 2) + which) // LANES + k)

        return pl.BlockSpec((2, PATCH, LANES), index)

    return pl.pallas_call(
        functools.partial(merge_kernel, which),
        grid_spec=pltpu.PrefetchScalarGridSpec(
            num_scalar_prefetch=2,
            grid=(1,),
            in_specs=[block(k) for k in range(WIDE // LANES)]
            + [pl.BlockSpec((1, 2, PATCH, PATCH), lambda i, pos, me: (0, 0, 0, 0))],
            out_specs=pl.BlockSpec((2, PATCH, PATCH), lambda i, pos, me: (0, 0, 0)),
        ),
        out_shape=jax.ShapeDtypeStruct((2, PATCH, PATCH), jnp.bfloat16),
        compiler_params=pltpu.CompilerParams(vmem_limit_bytes=CUT_VMEM),
        cost_estimate=pl.CostEstimate(
            flops=2 * PATCH * WIDE, bytes_accessed=3300000, transcendentals=0
        ),
    )(pos, me, *([band] * (WIDE // LANES)), sibling)


def rest_index(step, pos, me):
    return jnp.where(step == 0, 2 * lax.bitwise_xor(me[0], 3) + 1, 2 * lax.bitwise_xor(me[0], 1) + step - 1)


def rest_kernel(pos, me, *refs):
    blocks, second, pieces = refs[:-2], refs[-2], refs[-1]
    step = pl.program_id(0)
    amount = lax.rem(first_col(pos, rest_index(step, pos, me)), LANES)

    def take(out):
        def body(i, carry):
            rows = pl.ds(pl.multiple_of(i * CHUNK, CHUNK), CHUNK)
            for plane in range(2):
                out[0, plane, rows, :] = cut_rows(blocks, plane, rows, amount).astype(jnp.bfloat16)
            return carry

        lax.fori_loop(0, PATCH // CHUNK, body, 0)

    pl.when(step == 0)(lambda: take(second))
    pl.when(step > 0)(lambda: take(pieces))


def cut_rest(band, pos, me):
    def block(k):
        def index(i, pos, me):
            return (0, 0, first_col(pos, rest_index(i, pos, me)) // LANES + k)

        return pl.BlockSpec((2, PATCH, LANES), index)

    shape = (2, PATCH, PATCH)
    return pl.pallas_call(
        rest_kernel,
        grid_spec=pltpu.PrefetchScalarGridSpec(
            num_scalar_prefetch=2,
            grid=(3,),
            in_specs=[block(k) for k in range(WIDE // LANES)],
            out_specs=[
                pl.BlockSpec((1, *shape), lambda i, pos, me: (0, 0, 0, 0)),
                pl.BlockSpec((1, *shape), lambda i, pos, me: (jnp.maximum(i - 1, 0), 0, 0, 0)),
            ],
        ),
        out_shape=[
            jax.ShapeDtypeStruct((1, *shape), jnp.bfloat16),
            jax.ShapeDtypeStruct((2, *shape), jnp.bfloat16),
        ],
        compiler_params=pltpu.CompilerParams(vmem_limit_bytes=CUT_VMEM),
        cost_estimate=pl.CostEstimate(
            flops=6 * PATCH * WIDE, bytes_accessed=7000000, transcendentals=0
        ),
    )(pos, me, *([band] * (WIDE // LANES)))


def wave_kernel(which, pos, me, spare, band, sibling, across, probe, amplitudes, *refs):
    tables, refs = refs[:3], refs[3:]
    last = which == 1
    if last:
        term_in, grad, keep_term, give_term, *scratch = refs
    else:
        grad, term_out, *scratch = refs
    window, sib_v, far_v, probe_v, amp_v, matrix, term_v, patch_v, twice, field, half, sems = scratch
    index = 2 * me[0] + which
    col_at = first_col(pos, index)
    row_at = first_row(pos, index)
    start = pl.multiple_of(col_at // LANES * LANES, LANES)
    pairs = [
        (band.at[:, :, pl.ds(start, WIDE)], window),
        (sibling.at[which], sib_v),
        (across, far_v),
        (probe, probe_v),
    ]
    cosine, sine, minus = tables
    quarters = [(slice(0, PATCH), slice(0, PATCH)), (slice(0, PATCH), slice(PATCH, 2 * PATCH))]
    quarters += [(slice(PATCH, 2 * PATCH), slice(0, PATCH)), (slice(PATCH, 2 * PATCH), slice(PATCH, 2 * PATCH))]
    pairs += [(t, matrix.at[q]) for t, q in zip((cosine, minus, sine, cosine), quarters)]
    pairs.append((amplitudes.at[which], amp_v))
    if last:
        pairs.append((term_in, term_v))
    copies = [pltpu.make_async_copy(a, b, sems.at[k]) for k, (a, b) in enumerate(pairs)]
    for copy in copies:
        copy.start()
    for copy in copies[:3]:
        copy.wait()
    amount = lax.rem(col_at, LANES)
    down = lax.rem(row_at, PATCH)
    views = [window.at[:, :, LANES * k : LANES * (k + 1)] for k in range(WIDE // LANES)]

    def assemble(i, carry):
        at = pl.multiple_of(i * CHUNK, CHUNK)
        rows = pl.ds(at, CHUNK)
        owner = band_of_rows(row_at, at, CHUNK)
        mine = owner == me[0]
        near = owner == lax.bitwise_xor(me[0], 1)
        for plane in range(2):
            own = cut_rows(views, plane, rows, amount)
            beside = sib_v[plane, rows, :].astype(jnp.float32)
            beyond = far_v[plane, rows, :].astype(jnp.float32)
            patch = jnp.where(mine, own, jnp.where(near, beside, beyond))
            twice[plane, rows, :] = patch
            twice[plane, pl.ds(pl.multiple_of(at + PATCH, CHUNK), CHUNK), :] = patch
        return carry

    lax.fori_loop(0, PATCH // CHUNK, assemble, 0)
    copies[3].wait()

    def illuminate(i, carry):
        at = pl.multiple_of(i * CHUNK, CHUNK)
        rows = pl.ds(at, CHUNK)
        patch_real = rows_from(twice, 0, at + down, CHUNK)
        patch_imag = rows_from(twice, 1, at + down, CHUNK)
        patch_v[0, rows, :] = patch_real.astype(jnp.bfloat16)
        patch_v[1, rows, :] = patch_imag.astype(jnp.bfloat16)
        probe_real = probe_v[0, rows, :]
        probe_imag = probe_v[1, rows, :]
        field[rows, :] = (probe_real * patch_real - probe_imag * patch_imag).astype(jnp.bfloat16)
        field[pl.ds(pl.multiple_of(at + PATCH, CHUNK), CHUNK), :] = (
            probe_real * patch_imag + probe_imag * patch_real
        ).astype(jnp.bfloat16)
        return carry

    lax.fori_loop(0, PATCH // CHUNK, illuminate, 0)
    for copy in copies[4:8]:
        copy.wait()

    def over_rows():
        for k in range(4):
            part = jnp.dot(
                matrix[256 * k : 256 * (k + 1), :], field[...], preferred_element_type=jnp.float32
            ).astype(jnp.bfloat16)
            at = PATCH * (1 - k // 2)
            half[256 * (k % 2) : 256 * (k % 2 + 1), at : at + PATCH] = part

    over_rows()
    copies[8].wait()
    for k in range(2):
        rows = slice(256 * k, 256 * (k + 1))
        far = jnp.dot(half[rows, :], matrix[...], preferred_element_type=jnp.float32)
        far_imag = far[:, :PATCH]
        far_real = far[:, PATCH:]
        power = far_real * far_real + far_imag * far_imag
        keep = 1.0 - amp_v[rows, :].astype(jnp.float32) * lax.rsqrt(
            jnp.maximum(power, MAGNITUDE_FLOOR * MAGNITUDE_FLOOR)
        )
        field[rows, :] = (far_imag * keep).astype(jnp.bfloat16)
        field[PATCH + 256 * k : PATCH + 256 * (k + 1), :] = (far_real * keep).astype(jnp.bfloat16)
    over_rows()
    if last:
        copies[9].wait()
        core = lax.rem(me[0], 2)
    for k in range(2):
        rows = slice(256 * k, 256 * (k + 1))
        back = jnp.dot(half[rows, :], matrix[...], preferred_element_type=jnp.float32)
        back_real = back[:, :PATCH]
        back_imag = back[:, PATCH:]
        patch_real = patch_v[0, rows, :].astype(jnp.float32)
        patch_imag = patch_v[1, rows, :].astype(jnp.float32)
        term_real = patch_real * back_real + patch_imag * back_imag
        term_imag = patch_real * back_imag - patch_imag * back_real
        if last:
            term_real = term_real + term_v[0, rows, :]
            term_imag = term_imag + term_v[1, rows, :]
            keep_term[rows, :] = jnp.where(core == 0, term_real, term_imag)
            give_term[rows, :] = jnp.where(core == 0, term_imag, term_real).astype(jnp.bfloat16)
        else:
            term_out[0, rows, :] = term_real
            term_out[1, rows, :] = term_imag
        term_v[0, rows, :] = back_real
        term_v[1, rows, :] = back_imag

    def weigh(i, carry):
        at = pl.multiple_of(i * CHUNK, CHUNK)
        rows = pl.ds(at, CHUNK)
        again = pl.ds(pl.multiple_of(at + PATCH, CHUNK), CHUNK)
        probe_real = probe_v[0, rows, :]
        probe_imag = probe_v[1, rows, :]
        back_real = term_v[0, rows, :]
        back_imag = term_v[1, rows, :]
        grad_real = probe_real * back_real + probe_imag * back_imag
        grad_imag = probe_real * back_imag - probe_imag * back_real
        twice[0, rows, :] = grad_real
        twice[0, again, :] = grad_real
        twice[1, rows, :] = grad_imag
        twice[1, again, :] = grad_imag
        return carry

    lax.fori_loop(0, PATCH // CHUNK, weigh, 0)
    classes, height = grad.shape[0], grad.shape[2]

    def spread(k, carry):
        for plane in range(2):
            grad[k, plane] = rows_from(twice, plane, PATCH - down + k * height, height).astype(
                jnp.bfloat16
            )
        return carry

    lax.fori_loop(0, classes, spread, 0)


def wave(which, classes, pos, me, spare, band, sibling, across, probe, amplitudes, tables, term):
    operands = [band, sibling, across, probe, amplitudes, *tables]
    smem = pl.BlockSpec(memory_space=pltpu.SMEM)
    hbm = pl.BlockSpec(memory_space=pl.ANY)
    vmem = pl.BlockSpec(memory_space=pltpu.VMEM)
    planes = (2, PATCH, PATCH)
    plane = (PATCH, PATCH)
    if term is None:
        terms = [jax.ShapeDtypeStruct(planes, jnp.float32)]
    else:
        operands.append(term)
        terms = [jax.ShapeDtypeStruct(plane, t) for t in (jnp.float32, jnp.bfloat16)]
    return pl.pallas_call(
        functools.partial(wave_kernel, which),
        in_specs=[smem, smem, smem] + [hbm] * len(operands),
        out_specs=[vmem] * (1 + len(terms)),
        out_shape=[
            jax.ShapeDtypeStruct((classes, 2, PATCH // classes, PATCH), jnp.bfloat16),
            *terms,
        ],
        scratch_shapes=[
            pltpu.VMEM((2, PATCH, WIDE), jnp.bfloat16),
            pltpu.VMEM(planes, jnp.bfloat16),
            pltpu.VMEM(planes, jnp.bfloat16),
            pltpu.VMEM(planes, jnp.float32),
            pltpu.VMEM((PATCH, PATCH), jnp.bfloat16),
            pltpu.VMEM((2 * PATCH, 2 * PATCH), jnp.bfloat16),
            pltpu.VMEM(planes, jnp.float32),
            pltpu.VMEM(planes, jnp.bfloat16),
            pltpu.VMEM((2, 2 * PATCH + SUBLANES, PATCH), jnp.float32),
            pltpu.VMEM((2 * PATCH, PATCH), jnp.bfloat16),
            pltpu.VMEM((PATCH, 2 * PATCH), jnp.bfloat16),
            pltpu.SemaphoreType.DMA((10,)),
        ],
        compiler_params=pltpu.CompilerParams(vmem_limit_bytes=WAVE_VMEM),
        cost_estimate=pl.CostEstimate(
            flops=32 * PATCH**3, bytes_accessed=100_000_000, transcendentals=0
        ),
    )(pos, me, spare, *operands)


def sum_kernel(pos, me, first, second, own_far, own_near, away_far, away_near, canvas):
    classes, height = first.shape[0], first.shape[2]
    start = me[1] * height
    canvas[...] = jnp.zeros_like(canvas)
    rows = lax.broadcasted_iota(jnp.int32, (2 * height, WIDE), 0)
    rows = start + jnp.where(rows >= height, rows - height, rows)

    def piece(k, source, which):
        index = 2 * k + which
        row_at = first_row(pos, index)
        col_at = first_col(pos, index)
        down = lax.rem(row_at, PATCH)
        at = pl.ds(pl.multiple_of(col_at // LANES * LANES, LANES), WIDE)
        data = source[k].astype(jnp.float32).reshape(2 * height, PATCH)
        data = shifted_right(data, lax.rem(col_at, LANES))

        @pl.when(down < start + height)
        def _():
            canvas[row_at // PATCH, :, at] += jnp.where(rows >= down, data, 0.0)

        @pl.when(down > start)
        def _():
            canvas[row_at // PATCH + 1, :, at] += jnp.where(rows < down, data, 0.0)

    def body(k, carry):
        piece(k, first, 0)
        piece(k, second, 1)
        return carry

    lax.fori_loop(0, classes, body, 0)
    shape = own_far.shape
    for k, (own, away) in enumerate([(own_far, away_far), (own_near, away_near)]):
        keep = lax.bitwise_xor(me[0], 2 - 2 * k)
        give = lax.bitwise_xor(me[0], 3 - 2 * k)
        own[...] = canvas[keep].reshape(shape)
        away[...] = canvas[give].reshape(shape).astype(jnp.bfloat16)


def sum_pieces(pos, me, first, second, bands, width):
    height = first.shape[2]
    smem = pl.BlockSpec(memory_space=pltpu.SMEM)
    vmem = pl.BlockSpec(memory_space=pltpu.VMEM)
    shape = (2, height, width)
    return pl.pallas_call(
        sum_kernel,
        in_specs=[smem, smem, vmem, vmem],
        out_specs=[vmem] * 4,
        out_shape=[
            jax.ShapeDtypeStruct(shape, kind)
            for kind in (jnp.float32, jnp.float32, jnp.bfloat16, jnp.bfloat16)
        ],
        scratch_shapes=[pltpu.VMEM((bands, 2 * height, width), jnp.float32)],
        compiler_params=pltpu.CompilerParams(vmem_limit_bytes=SUM_VMEM),
        cost_estimate=pl.CostEstimate(
            flops=8 * first.size, bytes_accessed=4 * first.size + 12 * math.prod(shape), transcendentals=0
        ),
    )(pos, me, first, second)


def assemble_kernel(length, me, *refs):
    steps = length - 1
    own, refs = refs[0], refs[1:]
    ups, downs, overs = refs[:steps], refs[steps : 2 * steps], refs[2 * steps : 3 * steps + 1]
    out, sems = refs[3 * steps + 1 :]
    height = own.shape[1]
    place = me[1] // 2
    side = lax.rem(me[1], 2)

    def copy(source, at, column, k):
        rows = pl.ds(pl.multiple_of((2 * at + column) * height, height), height)
        return pltpu.make_async_copy(source, out.at[:, rows, :], sems.at[k])

    always = [copy(own, place, side, 0)]
    for k in range(length):
        always.append(copy(overs[k], sent_over(place, k, length), 1 - side, k + 1))
    some = []
    for k in range(1, length):
        below, above = place - k, place + k
        held = length + 2 * k - 1
        some.append((below >= 0, copy(ups[k - 1], below, side, held)))
        some.append((above < length, copy(downs[k - 1], above, side, held + 1)))
    for part in always:
        part.start()
    for has, part in some:
        pl.when(has)(part.start)
    for part in always:
        part.wait()
    for has, part in some:
        pl.when(has)(part.wait)


def sent_over(place, k, length):
    low = jnp.where(place >= k, place - k, place + k)
    if k == length - 1:
        high = jnp.where(place == 0, length - 1, jnp.where(place == length - 1, 0, place + 1))
        return high
    return low


def gather_classes(own, me, classes, term, term_steps):
    length = classes // 2
    place = me[1] // 2

    def along(value, held, step):
        pairs = [(2 * z + x, 2 * (z + step) + x) for z in held if 0 <= z + step < length for x in range(2)]
        return lax.ppermute(value, "pat", pairs)

    def over(value):
        return lax.ppermute(value, "pat", [(k, k ^ 1) for k in range(classes)])

    ups, downs, overs = [own], [own], []
    for k in range(length - 1):
        overs.append(over(jnp.where(place >= k, ups[k], downs[k]) if k else own))
        ups.append(along(ups[k], range(k, length), 1))
        downs.append(along(downs[k], range(length - k), -1))
        if k == length - 2:
            for step in term_steps[:-1]:
                term = step(term)
        overs[k], ups[k + 1], downs[k + 1], term = lax.optimization_barrier(
            (overs[k], ups[k + 1], downs[k + 1], term)
        )
    end = jnp.where(place == 0, downs[-1], ups[-1])
    if length > 2:
        middle = (place > 0) & (place < length - 1)
        end = jnp.where(middle, downs[1], end)
    last, term = lax.optimization_barrier((over(end), term_steps[-1](term)))
    overs.append(last)
    operands = [own, *ups[1:], *downs[1:], *overs]
    object_next = pl.pallas_call(
        functools.partial(assemble_kernel, length),
        in_specs=[pl.BlockSpec(memory_space=pltpu.SMEM)]
        + [pl.BlockSpec(memory_space=pltpu.VMEM)] * len(operands),
        out_specs=pl.BlockSpec(memory_space=pl.ANY),
        out_shape=jax.ShapeDtypeStruct((2, classes * own.shape[1], own.shape[2]), own.dtype),
        scratch_shapes=[pltpu.SemaphoreType.DMA((3 * length - 1,))],
        compiler_params=pltpu.CompilerParams(vmem_limit_bytes=CUT_VMEM),
        cost_estimate=pl.CostEstimate(
            flops=0, bytes_accessed=4 * own.size * classes, transcendentals=0
        ),
    )(me, *operands)
    return object_next, term


def shards(object_image, probe, amplitudes, pos_tile, pos_offset):
    owners = lax.axis_size("obj")
    classes = lax.axis_size("pat")
    my_owner = lax.axis_index("obj").astype(jnp.int32)
    my_class = lax.axis_index("pat").astype(jnp.int32)
    me = jnp.stack([my_owner, my_class])
    height = PATCH // classes
    width = object_image.shape[2]
    assert owners == 4 and object_image.shape[1] == PATCH and pos_tile.shape[0] == 2

    def flip(value, bit):
        return lax.ppermute(value, "obj", [(k, k ^ bit) for k in range(owners)])

    def pat_flip(bit):
        return lambda value: lax.ppermute(value, "pat", [(k, k ^ bit) for k in range(classes)])

    def halved(part, bit, other):
        rows = part.shape[0] // 2
        give = lax.dynamic_slice_in_dim(part, (1 - bit) * rows, rows, 0).astype(jnp.bfloat16)
        return lax.dynamic_slice_in_dim(part, bit * rows, rows, 0) + other(give).astype(jnp.float32)

    def doubled(part, bit, other):
        got = other(part)
        return jnp.where(bit == 0, jnp.concatenate([part, got]), jnp.concatenate([got, part]))

    bits = [1 << k for k in range(classes.bit_length() - 1)]
    halving = bits[1:] + bits[:1]
    own_pos = jnp.concatenate([pos_tile, pos_offset], 1)
    pos = lax.all_gather(own_pos, "obj", axis=0, tiled=True)

    first = cut(object_image, pos, me, 3, 0, 1)
    second, pieces = cut_rest(object_image, pos, me)
    second, pieces, then = lax.optimization_barrier((second, pieces, me))
    relay = [flip(first, 1), flip(second, 1)]
    sibling = flip(pieces, 1)
    merged = [cut_and_merge(object_image, relay[k], pos, then, k) for k in range(2)]
    merged[1], pos_pat = lax.optimization_barrier((merged[1], own_pos))
    across = [flip(m, 2) for m in merged]
    for bit in bits:
        pos_pat = doubled(pos_pat, my_class // bit % 2, pat_flip(bit))

    operands = (probe, amplitudes, dft_tables(PATCH))
    grad_0, term = wave(0, classes, pos, me, pos_pat, object_image, sibling, across[0], *operands, None)
    grad_0, across[1] = lax.optimization_barrier((grad_0, across[1]))
    part_0 = lax.all_to_all(grad_0, "pat", split_axis=0, concat_axis=0, tiled=True)
    grad_1, keep_term, give_term = wave(
        1, classes, pos, me, me, object_image, sibling, across[1], *operands, term
    )
    grad_1, part_0 = lax.optimization_barrier((grad_1, part_0))
    part_1 = lax.all_to_all(grad_1, "pat", split_axis=0, concat_axis=0, tiled=True)

    core = my_owner % 2
    line = my_owner // 2
    term = keep_term + flip(give_term, 1).astype(jnp.float32)
    term = halved(term, line, lambda value: flip(value, 2))
    term, then = lax.optimization_barrier((term, me))
    own_far, own_near, away_far, away_near = sum_pieces(
        pos_pat, then, part_0, part_1, owners, width
    )
    from_sibling_far = flip(away_far, 1)
    from_sibling = flip(away_near, 1)
    from_across = flip(
        (own_far + from_sibling_far.astype(jnp.float32)).astype(jnp.bfloat16), 2
    )
    for bit in halving:
        term = halved(term, my_class // bit % 2, pat_flip(bit))
    term = doubled(term.astype(jnp.bfloat16), my_class % 2, pat_flip(1))
    total = own_near + from_sibling.astype(jnp.float32) + from_across.astype(jnp.float32)
    mine = lax.dynamic_slice_in_dim(object_image, my_class * height, height, 1)
    updated = (mine.astype(jnp.float32) - OBJECT_RATE * total).astype(jnp.bfloat16)
    updated, term = lax.optimization_barrier((updated, term))
    steps = [
        functools.partial(doubled, bit=my_class // bit % 2, other=pat_flip(bit)) for bit in reversed(bits[1:])
    ]
    steps.append(functools.partial(doubled, bit=line, other=lambda value: flip(value, 2)))
    steps.append(lambda part: doubled(part[None], core, lambda value: flip(value, 1)))
    if classes in BY_PERMUTE:
        object_next, term = gather_classes(updated, me, classes, term, steps)
    else:
        object_next = lax.all_gather(updated, "pat", axis=1, tiled=True)
        for step in steps:
            term = step(term)
    probe_total = term.astype(jnp.float32)
    probe_next = probe - PROBE_RATE * probe_total
    return (object_next, probe_next)


def solution(mesh):
    return jax.shard_map(
        shards,
        mesh=mesh,
        in_specs=(
            P(None, "obj", None),
            P(),
            P(("pat", "obj"), None, None),
            P(("pat", "obj"), None),
            P(("pat", "obj"), None),
        ),
        out_specs=(P(None, "obj", None), P()),
        check_vma=False,
    )
```

```python
import functools
import math

import jax
import jax.numpy as jnp
import numpy as np
from jax import lax
from jax.experimental import pallas as pl
from jax.experimental.pallas import tpu as pltpu
from jax.sharding import PartitionSpec as P

PATCH = 512
TILE = 256
LANES = 128
WIDE = PATCH + LANES

OBJECT_RATE = 0.1
PROBE_RATE = 0.05
MAGNITUDE_FLOOR = 0.5
CUT_VMEM = 14 * 1024 * 1024
WAVE_VMEM = 56 * 1024 * 1024
SUM_VMEM = 24 * 1024 * 1024
BY_PERMUTE = (4, 8)


def dft_tables(length):
    counter = np.arange(length, dtype=np.int32)
    phase_angle = (counter[:, None] * counter[None, :] % length).astype(np.float32) * np.float32(
        2.0 * math.pi / length
    )
    factor = np.float32(1.0 / math.sqrt(length))
    cosine = (np.cos(phase_angle) * factor).astype(jnp.bfloat16)
    sine_part = (-np.sin(phase_angle) * factor).astype(jnp.bfloat16)
    return jnp.asarray(cosine), jnp.asarray(sine_part), jnp.asarray(-sine_part)


def first_row(pos, index):
    return pos[index, 0] * TILE + pos[index, 2]


def first_col(pos, index):
    return pos[index, 1] * TILE + pos[index, 3]


def shifted_left(blocks, amount):
    turned = [pltpu.roll(b, lax.rem(LANES - amount, LANES), axis=1) for b in blocks]
    lane = lax.broadcasted_iota(jnp.int32, turned[0].shape, 1)
    stay = lane < LANES - amount
    return jnp.concatenate([jnp.where(stay, a, b) for a, b in zip(turned, turned[1:])], 1)


def shifted_right(data, amount):
    count = data.shape[1] // LANES
    turned = [pltpu.roll(data[:, LANES * k : LANES * (k + 1)], amount, axis=1) for k in range(count)]
    lane = lax.broadcasted_iota(jnp.int32, turned[0].shape, 1)
    stay = lane >= amount
    before = [jnp.zeros_like(turned[0])] + turned
    after = turned + [jnp.zeros_like(turned[0])]
    return jnp.concatenate([jnp.where(stay, a, b) for a, b in zip(after, before)], 1)


def band_of_rows(row_at, start, count):
    rows = lax.broadcasted_iota(jnp.int32, (count, PATCH), 0) + start
    return row_at // PATCH + (rows < lax.rem(row_at, PATCH)).astype(jnp.int32)


CHUNK = 64
SUBLANES = 8


def rows_from(ref, plane, start, count):
    aligned = pl.multiple_of(start // SUBLANES * SUBLANES, SUBLANES)
    amount = lax.rem(start, SUBLANES)
    data = ref[plane, pl.ds(aligned, count + SUBLANES), :]
    data = data.reshape(count // SUBLANES + 1, SUBLANES, data.shape[1])
    turned = pltpu.roll(data, lax.rem(SUBLANES - amount, SUBLANES), axis=1)
    row = lax.broadcasted_iota(jnp.int32, turned[1:].shape, 1)
    data = jnp.where(row < SUBLANES - amount, turned[:-1], turned[1:])
    return data.reshape(count, data.shape[2])


def cut_rows(blocks, plane, rows, amount):
    return shifted_left([b[plane, rows, :].astype(jnp.float32) for b in blocks], amount)


def cut_kernel(flip, first, pos, me, *refs):
    blocks, out = refs[:-1], refs[-1]
    target = lax.bitwise_xor(me[0], flip)
    amount = lax.rem(first_col(pos, 2 * target + first + pl.program_id(0)), LANES)

    def body(i, carry):
        rows = pl.ds(pl.multiple_of(i * CHUNK, CHUNK), CHUNK)
        for plane in range(2):
            out[0, plane, rows, :] = cut_rows(blocks, plane, rows, amount).astype(jnp.bfloat16)
        return carry

    lax.fori_loop(0, PATCH // CHUNK, body, 0)


def cut(band, pos, me, flip, first, count):
    def block(k):
        def index(i, pos, me):
            return (0, 0, first_col(pos, 2 * lax.bitwise_xor(me[0], flip) + first + i) // LANES + k)

        return pl.BlockSpec((2, PATCH, LANES), index)

    return pl.pallas_call(
        functools.partial(cut_kernel, flip, first),
        grid_spec=pltpu.PrefetchScalarGridSpec(
            num_scalar_prefetch=2,
            grid=(count,),
            in_specs=[block(k) for k in range(WIDE // LANES)],
            out_specs=pl.BlockSpec((1, 2, PATCH, PATCH), lambda i, pos, me: (i, 0, 0, 0)),
        ),
        out_shape=jax.ShapeDtypeStruct((count, 2, PATCH, PATCH), jnp.bfloat16),
        compiler_params=pltpu.CompilerParams(vmem_limit_bytes=CUT_VMEM),
        cost_estimate=pl.CostEstimate(
            flops=count * 2 * PATCH * WIDE, bytes_accessed=count * 2300000, transcendentals=0
        ),
    )(pos, me, *([band] * (WIDE // LANES)))


def merge_kernel(which, pos, me, *refs):
    blocks, sibling, out = refs[:-2], refs[-2], refs[-1]
    index = 2 * lax.bitwise_xor(me[0], 2) + which
    amount = lax.rem(first_col(pos, index), LANES)
    row_at = first_row(pos, index)

    def body(i, carry):
        rows = pl.ds(pl.multiple_of(i * CHUNK, CHUNK), CHUNK)
        mine = band_of_rows(row_at, i * CHUNK, CHUNK) == me[0]
        for plane in range(2):
            own = cut_rows(blocks, plane, rows, amount)
            other = sibling[0, plane, rows, :].astype(jnp.float32)
            out[plane, rows, :] = jnp.where(mine, own, other).astype(jnp.bfloat16)
        return carry

    lax.fori_loop(0, PATCH // CHUNK, body, 0)


def cut_and_merge(band, sibling, pos, me, which):
    def block(k):
        def index(i, pos, me):
            return (0, 0, first_col(pos, 2 * lax.bitwise_xor(me[0], 2) + which) // LANES + k)

        return pl.BlockSpec((2, PATCH, LANES), index)

    return pl.pallas_call(
        functools.partial(merge_kernel, which),
        grid_spec=pltpu.PrefetchScalarGridSpec(
            num_scalar_prefetch=2,
            grid=(1,),
            in_specs=[block(k) for k in range(WIDE // LANES)]
            + [pl.BlockSpec((1, 2, PATCH, PATCH), lambda i, pos, me: (0, 0, 0, 0))],
            out_specs=pl.BlockSpec((2, PATCH, PATCH), lambda i, pos, me: (0, 0, 0)),
        ),
        out_shape=jax.ShapeDtypeStruct((2, PATCH, PATCH), jnp.bfloat16),
        compiler_params=pltpu.CompilerParams(vmem_limit_bytes=CUT_VMEM),
        cost_estimate=pl.CostEstimate(
            flops=2 * PATCH * WIDE, bytes_accessed=3300000, transcendentals=0
        ),
    )(pos, me, *([band] * (WIDE // LANES)), sibling)


def rest_index(step, pos, me):
    return jnp.where(step == 0, 2 * lax.bitwise_xor(me[0], 3) + 1, 2 * lax.bitwise_xor(me[0], 1) + step - 1)


def rest_kernel(pos, me, *refs):
    blocks, second, pieces = refs[:-2], refs[-2], refs[-1]
    step = pl.program_id(0)
    amount = lax.rem(first_col(pos, rest_index(step, pos, me)), LANES)

    def take(out):
        def body(i, carry):
            rows = pl.ds(pl.multiple_of(i * CHUNK, CHUNK), CHUNK)
            for plane in range(2):
                out[0, plane, rows, :] = cut_rows(blocks, plane, rows, amount).astype(jnp.bfloat16)
            return carry

        lax.fori_loop(0, PATCH // CHUNK, body, 0)

    pl.when(step == 0)(lambda: take(second))
    pl.when(step > 0)(lambda: take(pieces))


def cut_rest(band, pos, me):
    def block(k):
        def index(i, pos, me):
            return (0, 0, first_col(pos, rest_index(i, pos, me)) // LANES + k)

        return pl.BlockSpec((2, PATCH, LANES), index)

    shape = (2, PATCH, PATCH)
    return pl.pallas_call(
        rest_kernel,
        grid_spec=pltpu.PrefetchScalarGridSpec(
            num_scalar_prefetch=2,
            grid=(3,),
            in_specs=[block(k) for k in range(WIDE // LANES)],
            out_specs=[
                pl.BlockSpec((1, *shape), lambda i, pos, me: (0, 0, 0, 0)),
                pl.BlockSpec((1, *shape), lambda i, pos, me: (jnp.maximum(i - 1, 0), 0, 0, 0)),
            ],
        ),
        out_shape=[
            jax.ShapeDtypeStruct((1, *shape), jnp.bfloat16),
            jax.ShapeDtypeStruct((2, *shape), jnp.bfloat16),
        ],
        compiler_params=pltpu.CompilerParams(vmem_limit_bytes=CUT_VMEM),
        cost_estimate=pl.CostEstimate(
            flops=6 * PATCH * WIDE, bytes_accessed=7000000, transcendentals=0
        ),
    )(pos, me, *([band] * (WIDE // LANES)))


def wave_kernel(which, pos, me, spare, band, sibling, across, probe, amplitudes, *refs):
    tables, refs = refs[:3], refs[3:]
    last = which == 1
    if last:
        term_in, grad, keep_term, give_term, *scratch = refs
    else:
        grad, term_out, *scratch = refs
    window, sib_v, far_v, probe_v, amp_v, matrix, term_v, patch_v, twice, field, half, sems = scratch
    index = 2 * me[0] + which
    col_at = first_col(pos, index)
    row_at = first_row(pos, index)
    start = pl.multiple_of(col_at // LANES * LANES, LANES)
    pairs = [
        (band.at[:, :, pl.ds(start, WIDE)], window),
        (sibling.at[which], sib_v),
        (across, far_v),
        (probe, probe_v),
    ]
    cosine, sine, minus = tables
    quarters = [(slice(0, PATCH), slice(0, PATCH)), (slice(0, PATCH), slice(PATCH, 2 * PATCH))]
    quarters += [(slice(PATCH, 2 * PATCH), slice(0, PATCH)), (slice(PATCH, 2 * PATCH), slice(PATCH, 2 * PATCH))]
    pairs += [(t, matrix.at[q]) for t, q in zip((cosine, minus, sine, cosine), quarters)]
    pairs.append((amplitudes.at[which], amp_v))
    if last:
        pairs.append((term_in, term_v))
    copies = [pltpu.make_async_copy(a, b, sems.at[k]) for k, (a, b) in enumerate(pairs)]
    for copy in copies:
        copy.start()
    for copy in copies[:3]:
        copy.wait()
    amount = lax.rem(col_at, LANES)
    down = lax.rem(row_at, PATCH)
    views = [window.at[:, :, LANES * k : LANES * (k + 1)] for k in range(WIDE // LANES)]

    def assemble(i, carry):
        at = pl.multiple_of(i * CHUNK, CHUNK)
        rows = pl.ds(at, CHUNK)
        owner = band_of_rows(row_at, at, CHUNK)
        mine = owner == me[0]
        near = owner == lax.bitwise_xor(me[0], 1)
        for plane in range(2):
            own = cut_rows(views, plane, rows, amount)
            beside = sib_v[plane, rows, :].astype(jnp.float32)
            beyond = far_v[plane, rows, :].astype(jnp.float32)
            patch = jnp.where(mine, own, jnp.where(near, beside, beyond))
            twice[plane, rows, :] = patch
            twice[plane, pl.ds(pl.multiple_of(at + PATCH, CHUNK), CHUNK), :] = patch
        return carry

    lax.fori_loop(0, PATCH // CHUNK, assemble, 0)
    copies[3].wait()

    def illuminate(i, carry):
        at = pl.multiple_of(i * CHUNK, CHUNK)
        rows = pl.ds(at, CHUNK)
        patch_real = rows_from(twice, 0, at + down, CHUNK)
        patch_imag = rows_from(twice, 1, at + down, CHUNK)
        patch_v[0, rows, :] = patch_real.astype(jnp.bfloat16)
        patch_v[1, rows, :] = patch_imag.astype(jnp.bfloat16)
        probe_real = probe_v[0, rows, :]
        probe_imag = probe_v[1, rows, :]
        field[rows, :] = (probe_real * patch_real - probe_imag * patch_imag).astype(jnp.bfloat16)
        field[pl.ds(pl.multiple_of(at + PATCH, CHUNK), CHUNK), :] = (
            probe_real * patch_imag + probe_imag * patch_real
        ).astype(jnp.bfloat16)
        return carry

    lax.fori_loop(0, PATCH // CHUNK, illuminate, 0)
    for copy in copies[4:8]:
        copy.wait()

    def over_rows():
        for k in range(4):
            part = jnp.dot(
                matrix[256 * k : 256 * (k + 1), :], field[...], preferred_element_type=jnp.float32
            ).astype(jnp.bfloat16)
            at = PATCH * (1 - k // 2)
            half[256 * (k % 2) : 256 * (k % 2 + 1), at : at + PATCH] = part

    over_rows()
    copies[8].wait()
    for k in range(2):
        rows = slice(256 * k, 256 * (k + 1))
        far = jnp.dot(half[rows, :], matrix[...], preferred_element_type=jnp.float32)
        far_imag = far[:, :PATCH]
        far_real = far[:, PATCH:]
        power = far_real * far_real + far_imag * far_imag
        keep = 1.0 - amp_v[rows, :].astype(jnp.float32) * lax.rsqrt(
            jnp.maximum(power, MAGNITUDE_FLOOR * MAGNITUDE_FLOOR)
        )
        field[rows, :] = (far_imag * keep).astype(jnp.bfloat16)
        field[PATCH + 256 * k : PATCH + 256 * (k + 1), :] = (far_real * keep).astype(jnp.bfloat16)
    over_rows()
    if last:
        copies[9].wait()
        core = lax.rem(me[0], 2)
    for k in range(2):
        rows = slice(256 * k, 256 * (k + 1))
        back = jnp.dot(half[rows, :], matrix[...], preferred_element_type=jnp.float32)
        back_real = back[:, :PATCH]
        back_imag = back[:, PATCH:]
        patch_real = patch_v[0, rows, :].astype(jnp.float32)
        patch_imag = patch_v[1, rows, :].astype(jnp.float32)
        term_real = patch_real * back_real + patch_imag * back_imag
        term_imag = patch_real * back_imag - patch_imag * back_real
        if last:
            term_real = term_real + term_v[0, rows, :]
            term_imag = term_imag + term_v[1, rows, :]
            keep_term[rows, :] = jnp.where(core == 0, term_real, term_imag)
            give_term[rows, :] = jnp.where(core == 0, term_imag, term_real).astype(jnp.bfloat16)
        else:
            term_out[0, rows, :] = term_real
            term_out[1, rows, :] = term_imag
        term_v[0, rows, :] = back_real
        term_v[1, rows, :] = back_imag

    def weigh(i, carry):
        at = pl.multiple_of(i * CHUNK, CHUNK)
        rows = pl.ds(at, CHUNK)
        again = pl.ds(pl.multiple_of(at + PATCH, CHUNK), CHUNK)
        probe_real = probe_v[0, rows, :]
        probe_imag = probe_v[1, rows, :]
        back_real = term_v[0, rows, :]
        back_imag = term_v[1, rows, :]
        grad_real = probe_real * back_real + probe_imag * back_imag
        grad_imag = probe_real * back_imag - probe_imag * back_real
        twice[0, rows, :] = grad_real
        twice[0, again, :] = grad_real
        twice[1, rows, :] = grad_imag
        twice[1, again, :] = grad_imag
        return carry

    lax.fori_loop(0, PATCH // CHUNK, weigh, 0)
    classes, height = grad.shape[0], grad.shape[2]

    def spread(k, carry):
        for plane in range(2):
            grad[k, plane] = rows_from(twice, plane, PATCH - down + k * height, height).astype(
                jnp.bfloat16
            )
        return carry

    lax.fori_loop(0, classes, spread, 0)


def wave(which, classes, pos, me, spare, band, sibling, across, probe, amplitudes, tables, term):
    operands = [band, sibling, across, probe, amplitudes, *tables]
    smem = pl.BlockSpec(memory_space=pltpu.SMEM)
    hbm = pl.BlockSpec(memory_space=pl.ANY)
    vmem = pl.BlockSpec(memory_space=pltpu.VMEM)
    planes = (2, PATCH, PATCH)
    plane = (PATCH, PATCH)
    if term is None:
        terms = [jax.ShapeDtypeStruct(planes, jnp.float32)]
    else:
        operands.append(term)
        terms = [jax.ShapeDtypeStruct(plane, t) for t in (jnp.float32, jnp.bfloat16)]
    return pl.pallas_call(
        functools.partial(wave_kernel, which),
        in_specs=[smem, smem, smem] + [hbm] * len(operands),
        out_specs=[vmem] * (1 + len(terms)),
        out_shape=[
            jax.ShapeDtypeStruct((classes, 2, PATCH // classes, PATCH), jnp.bfloat16),
            *terms,
        ],
        scratch_shapes=[
            pltpu.VMEM((2, PATCH, WIDE), jnp.bfloat16),
            pltpu.VMEM(planes, jnp.bfloat16),
            pltpu.VMEM(planes, jnp.bfloat16),
            pltpu.VMEM(planes, jnp.float32),
            pltpu.VMEM((PATCH, PATCH), jnp.bfloat16),
            pltpu.VMEM((2 * PATCH, 2 * PATCH), jnp.bfloat16),
            pltpu.VMEM(planes, jnp.float32),
            pltpu.VMEM(planes, jnp.bfloat16),
            pltpu.VMEM((2, 2 * PATCH + SUBLANES, PATCH), jnp.float32),
            pltpu.VMEM((2 * PATCH, PATCH), jnp.bfloat16),
            pltpu.VMEM((PATCH, 2 * PATCH), jnp.bfloat16),
            pltpu.SemaphoreType.DMA((10,)),
        ],
        compiler_params=pltpu.CompilerParams(vmem_limit_bytes=WAVE_VMEM),
        cost_estimate=pl.CostEstimate(
            flops=32 * PATCH**3, bytes_accessed=100_000_000, transcendentals=0
        ),
    )(pos, me, spare, *operands)


def sum_kernel(pos, me, first, second, own_far, own_near, away_far, away_near, canvas):
    classes, height = first.shape[0], first.shape[2]
    start = me[1] * height
    canvas[...] = jnp.zeros_like(canvas)
    rows = lax.broadcasted_iota(jnp.int32, (2 * height, WIDE), 0)
    rows = start + jnp.where(rows >= height, rows - height, rows)

    def piece(k, source, which):
        index = 2 * k + which
        row_at = first_row(pos, index)
        col_at = first_col(pos, index)
        down = lax.rem(row_at, PATCH)
        at = pl.ds(pl.multiple_of(col_at // LANES * LANES, LANES), WIDE)
        data = source[k].astype(jnp.float32).reshape(2 * height, PATCH)
        data = shifted_right(data, lax.rem(col_at, LANES))

        @pl.when(down < start + height)
        def _():
            canvas[row_at // PATCH, :, at] += jnp.where(rows >= down, data, 0.0)

        @pl.when(down > start)
        def _():
            canvas[row_at // PATCH + 1, :, at] += jnp.where(rows < down, data, 0.0)

    def body(k, carry):
        piece(k, first, 0)
        piece(k, second, 1)
        return carry

    lax.fori_loop(0, classes, body, 0)
    shape = own_far.shape
    for k, (own, away) in enumerate([(own_far, away_far), (own_near, away_near)]):
        keep = lax.bitwise_xor(me[0], 2 - 2 * k)
        give = lax.bitwise_xor(me[0], 3 - 2 * k)
        own[...] = canvas[keep].reshape(shape)
        away[...] = canvas[give].reshape(shape).astype(jnp.bfloat16)


def sum_pieces(pos, me, first, second, bands, width):
    height = first.shape[2]
    smem = pl.BlockSpec(memory_space=pltpu.SMEM)
    vmem = pl.BlockSpec(memory_space=pltpu.VMEM)
    shape = (2, height, width)
    return pl.pallas_call(
        sum_kernel,
        in_specs=[smem, smem, vmem, vmem],
        out_specs=[vmem] * 4,
        out_shape=[
            jax.ShapeDtypeStruct(shape, kind)
            for kind in (jnp.float32, jnp.float32, jnp.bfloat16, jnp.bfloat16)
        ],
        scratch_shapes=[pltpu.VMEM((bands, 2 * height, width), jnp.float32)],
        compiler_params=pltpu.CompilerParams(vmem_limit_bytes=SUM_VMEM),
        cost_estimate=pl.CostEstimate(
            flops=8 * first.size, bytes_accessed=4 * first.size + 12 * math.prod(shape), transcendentals=0
        ),
    )(pos, me, first, second)


def assemble_kernel(length, me, *refs):
    steps = length - 1
    own, refs = refs[0], refs[1:]
    ups, downs, overs = refs[:steps], refs[steps : 2 * steps], refs[2 * steps : 3 * steps + 1]
    out, sems = refs[3 * steps + 1 :]
    height = own.shape[1]
    place = me[1] // 2
    side = lax.rem(me[1], 2)

    def copy(source, at, column, k):
        rows = pl.ds(pl.multiple_of((2 * at + column) * height, height), height)
        return pltpu.make_async_copy(source, out.at[:, rows, :], sems.at[k])

    always = [copy(own, place, side, 0)]
    for k in range(length):
        always.append(copy(overs[k], sent_over(place, k, length), 1 - side, k + 1))
    some = []
    for k in range(1, length):
        below, above = place - k, place + k
        held = length + 2 * k - 1
        some.append((below >= 0, copy(ups[k - 1], below, side, held)))
        some.append((above < length, copy(downs[k - 1], above, side, held + 1)))
    for part in always:
        part.start()
    for has, part in some:
        pl.when(has)(part.start)
    for part in always:
        part.wait()
    for has, part in some:
        pl.when(has)(part.wait)


def sent_over(place, k, length):
    low = jnp.where(place >= k, place - k, place + k)
    if k == length - 1:
        high = jnp.where(place == 0, length - 1, jnp.where(place == length - 1, 0, place + 1))
        return high
    return low


def gather_classes(own, me, classes, term, term_steps):
    length = classes // 2
    place = me[1] // 2

    def along(value, held, step):
        pairs = [(2 * z + x, 2 * (z + step) + x) for z in held if 0 <= z + step < length for x in range(2)]
        return lax.ppermute(value, "pat", pairs)

    def over(value):
        return lax.ppermute(value, "pat", [(k, k ^ 1) for k in range(classes)])

    ups, downs, overs = [own], [own], []
    for k in range(length - 1):
        overs.append(over(jnp.where(place >= k, ups[k], downs[k]) if k else own))
        ups.append(along(ups[k], range(k, length), 1))
        downs.append(along(downs[k], range(length - k), -1))
        if k == length - 2:
            for step in term_steps[:-1]:
                term = step(term)
        overs[k], ups[k + 1], downs[k + 1], term = lax.optimization_barrier(
            (overs[k], ups[k + 1], downs[k + 1], term)
        )
    end = jnp.where(place == 0, downs[-1], ups[-1])
    if length > 2:
        middle = (place > 0) & (place < length - 1)
        end = jnp.where(middle, downs[1], end)
    last, term = lax.optimization_barrier((over(end), term_steps[-1](term)))
    overs.append(last)
    operands = [own, *ups[1:], *downs[1:], *overs]
    object_next = pl.pallas_call(
        functools.partial(assemble_kernel, length),
        in_specs=[pl.BlockSpec(memory_space=pltpu.SMEM)]
        + [pl.BlockSpec(memory_space=pltpu.VMEM)] * len(operands),
        out_specs=pl.BlockSpec(memory_space=pl.ANY),
        out_shape=jax.ShapeDtypeStruct((2, classes * own.shape[1], own.shape[2]), own.dtype),
        scratch_shapes=[pltpu.SemaphoreType.DMA((3 * length - 1,))],
        compiler_params=pltpu.CompilerParams(vmem_limit_bytes=CUT_VMEM),
        cost_estimate=pl.CostEstimate(
            flops=0, bytes_accessed=4 * own.size * classes, transcendentals=0
        ),
    )(me, *operands)
    return object_next, term


def shards(object_image, probe, amplitudes, pos_tile, pos_offset):
    owners = lax.axis_size("obj")
    classes = lax.axis_size("pat")
    my_owner = lax.axis_index("obj").astype(jnp.int32)
    my_class = lax.axis_index("pat").astype(jnp.int32)
    me = jnp.stack([my_owner, my_class])
    height = PATCH // classes
    width = object_image.shape[2]
    assert owners == 4 and object_image.shape[1] == PATCH and pos_tile.shape[0] == 2

    def flip(value, bit):
        return lax.ppermute(value, "obj", [(k, k ^ bit) for k in range(owners)])

    def pat_flip(bit):
        return lambda value: lax.ppermute(value, "pat", [(k, k ^ bit) for k in range(classes)])

    def halved(part, bit, other):
        rows = part.shape[0] // 2
        give = lax.dynamic_slice_in_dim(part, (1 - bit) * rows, rows, 0).astype(jnp.bfloat16)
        return lax.dynamic_slice_in_dim(part, bit * rows, rows, 0) + other(give).astype(jnp.float32)

    def doubled(part, bit, other):
        got = other(part)
        return jnp.where(bit == 0, jnp.concatenate([part, got]), jnp.concatenate([got, part]))

    bits = [1 << k for k in range(classes.bit_length() - 1)]
    halving = bits[1:] + bits[:1]
    own_pos = jnp.concatenate([pos_tile, pos_offset], 1)
    pos = lax.all_gather(own_pos, "obj", axis=0, tiled=True)

    first = cut(object_image, pos, me, 3, 0, 1)
    second, pieces = cut_rest(object_image, pos, me)
    second, pieces, then = lax.optimization_barrier((second, pieces, me))
    relay = [flip(first, 1), flip(second, 1)]
    sibling = flip(pieces, 1)
    merged = [cut_and_merge(object_image, relay[k], pos, then, k) for k in range(2)]
    merged[1], pos_pat = lax.optimization_barrier((merged[1], own_pos))
    across = [flip(m, 2) for m in merged]
    for bit in bits:
        pos_pat = doubled(pos_pat, my_class // bit % 2, pat_flip(bit))

    operands = (probe, amplitudes, dft_tables(PATCH))
    grad_0, term = wave(0, classes, pos, me, pos_pat, object_image, sibling, across[0], *operands, None)
    grad_0, across[1] = lax.optimization_barrier((grad_0, across[1]))
    part_0 = lax.all_to_all(grad_0, "pat", split_axis=0, concat_axis=0, tiled=True)
    grad_1, keep_term, give_term = wave(
        1, classes, pos, me, me, object_image, sibling, across[1], *operands, term
    )
    grad_1, part_0 = lax.optimization_barrier((grad_1, part_0))
    part_1 = lax.all_to_all(grad_1, "pat", split_axis=0, concat_axis=0, tiled=True)

    core = my_owner % 2
    line = my_owner // 2
    term = keep_term + flip(give_term, 1).astype(jnp.float32)
    term = halved(term, line, lambda value: flip(value, 2))
    term, then = lax.optimization_barrier((term, me))
    own_far, own_near, away_far, away_near = sum_pieces(
        pos_pat, then, part_0, part_1, owners, width
    )
    from_sibling_far = flip(away_far, 1)
    from_sibling = flip(away_near, 1)
    from_across = flip(
        (own_far + from_sibling_far.astype(jnp.float32)).astype(jnp.bfloat16), 2
    )
    for bit in halving:
        term = halved(term, my_class // bit % 2, pat_flip(bit))
    term = term.astype(jnp.bfloat16)
    for bit in reversed(halving):
        term = doubled(term, my_class // bit % 2, pat_flip(bit))
    total = own_near + from_sibling.astype(jnp.float32) + from_across.astype(jnp.float32)
    mine = lax.dynamic_slice_in_dim(object_image, my_class * height, height, 1)
    updated = (mine.astype(jnp.float32) - OBJECT_RATE * total).astype(jnp.bfloat16)
    updated, term = lax.optimization_barrier((updated, term))
    steps = [functools.partial(doubled, bit=line, other=lambda value: flip(value, 2))]
    steps.append(lambda part: doubled(part[None], core, lambda value: flip(value, 1)))
    if classes in BY_PERMUTE:
        object_next, term = gather_classes(updated, me, classes, term, steps)
    else:
        object_next = lax.all_gather(updated, "pat", axis=1, tiled=True)
        for step in steps:
            term = step(term)
    probe_total = term.astype(jnp.float32)
    probe_next = probe - PROBE_RATE * probe_total
    return (object_next, probe_next)


def solution(mesh):
    return jax.shard_map(
        shards,
        mesh=mesh,
        in_specs=(
            P(None, "obj", None),
            P(),
            P(("pat", "obj"), None, None),
            P(("pat", "obj"), None),
            P(("pat", "obj"), None),
        ),
        out_specs=(P(None, "obj", None), P()),
        check_vma=False,
    )
```

```python
import functools
import math

import jax
import jax.numpy as jnp
import numpy as np
from jax import lax
from jax.experimental import pallas as pl
from jax.experimental.pallas import tpu as pltpu
from jax.sharding import PartitionSpec as P

PATCH = 512
TILE = 256
LANES = 128
WIDE = PATCH + LANES

OBJECT_RATE = 0.1
PROBE_RATE = 0.05
MAGNITUDE_FLOOR = 0.5
CUT_VMEM = 14 * 1024 * 1024
WAVE_VMEM = 56 * 1024 * 1024
SUM_VMEM = 24 * 1024 * 1024
BY_PERMUTE = (4, 8)


def dft_tables(length):
    counter = np.arange(length, dtype=np.int32)
    phase_angle = (counter[:, None] * counter[None, :] % length).astype(np.float32) * np.float32(
        2.0 * math.pi / length
    )
    factor = np.float32(1.0 / math.sqrt(length))
    cosine = (np.cos(phase_angle) * factor).astype(jnp.bfloat16)
    sine_part = (-np.sin(phase_angle) * factor).astype(jnp.bfloat16)
    return jnp.asarray(cosine), jnp.asarray(sine_part), jnp.asarray(-sine_part)


def first_row(pos, index):
    return pos[index, 0] * TILE + pos[index, 2]


def first_col(pos, index):
    return pos[index, 1] * TILE + pos[index, 3]


def shifted_left(blocks, amount):
    turned = [pltpu.roll(b, lax.rem(LANES - amount, LANES), axis=1) for b in blocks]
    lane = lax.broadcasted_iota(jnp.int32, turned[0].shape, 1)
    stay = lane < LANES - amount
    return jnp.concatenate([jnp.where(stay, a, b) for a, b in zip(turned, turned[1:])], 1)


def shifted_right(data, amount):
    count = data.shape[1] // LANES
    turned = [pltpu.roll(data[:, LANES * k : LANES * (k + 1)], amount, axis=1) for k in range(count)]
    lane = lax.broadcasted_iota(jnp.int32, turned[0].shape, 1)
    stay = lane >= amount
    before = [jnp.zeros_like(turned[0])] + turned
    after = turned + [jnp.zeros_like(turned[0])]
    return jnp.concatenate([jnp.where(stay, a, b) for a, b in zip(after, before)], 1)


def band_of_rows(row_at, start, count):
    rows = lax.broadcasted_iota(jnp.int32, (count, PATCH), 0) + start
    return row_at // PATCH + (rows < lax.rem(row_at, PATCH)).astype(jnp.int32)


CHUNK = 64
SUBLANES = 8


def rows_from(ref, plane, start, count):
    aligned = pl.multiple_of(start // SUBLANES * SUBLANES, SUBLANES)
    amount = lax.rem(start, SUBLANES)
    data = ref[plane, pl.ds(aligned, count + SUBLANES), :]
    data = data.reshape(count // SUBLANES + 1, SUBLANES, data.shape[1])
    turned = pltpu.roll(data, lax.rem(SUBLANES - amount, SUBLANES), axis=1)
    row = lax.broadcasted_iota(jnp.int32, turned[1:].shape, 1)
    data = jnp.where(row < SUBLANES - amount, turned[:-1], turned[1:])
    return data.reshape(count, data.shape[2])


def cut_rows(blocks, plane, rows, amount):
    return shifted_left([b[plane, rows, :].astype(jnp.float32) for b in blocks], amount)


def cut_kernel(flip, first, pos, me, *refs):
    blocks, out = refs[:-1], refs[-1]
    target = lax.bitwise_xor(me[0], flip)
    amount = lax.rem(first_col(pos, 2 * target + first + pl.program_id(0)), LANES)

    def body(i, carry):
        rows = pl.ds(pl.multiple_of(i * CHUNK, CHUNK), CHUNK)
        for plane in range(2):
            out[0, plane, rows, :] = cut_rows(blocks, plane, rows, amount).astype(jnp.bfloat16)
        return carry

    lax.fori_loop(0, PATCH // CHUNK, body, 0)


def cut(band, pos, me, flip, first, count):
    def block(k):
        def index(i, pos, me):
            return (0, 0, first_col(pos, 2 * lax.bitwise_xor(me[0], flip) + first + i) // LANES + k)

        return pl.BlockSpec((2, PATCH, LANES), index)

    return pl.pallas_call(
        functools.partial(cut_kernel, flip, first),
        grid_spec=pltpu.PrefetchScalarGridSpec(
            num_scalar_prefetch=2,
            grid=(count,),
            in_specs=[block(k) for k in range(WIDE // LANES)],
            out_specs=pl.BlockSpec((1, 2, PATCH, PATCH), lambda i, pos, me: (i, 0, 0, 0)),
        ),
        out_shape=jax.ShapeDtypeStruct((count, 2, PATCH, PATCH), jnp.bfloat16),
        compiler_params=pltpu.CompilerParams(vmem_limit_bytes=CUT_VMEM),
        cost_estimate=pl.CostEstimate(
            flops=count * 2 * PATCH * WIDE, bytes_accessed=count * 2300000, transcendentals=0
        ),
    )(pos, me, *([band] * (WIDE // LANES)))


def merge_kernel(which, pos, me, *refs):
    blocks, sibling, out = refs[:-2], refs[-2], refs[-1]
    index = 2 * lax.bitwise_xor(me[0], 2) + which
    amount = lax.rem(first_col(pos, index), LANES)
    row_at = first_row(pos, index)

    def body(i, carry):
        rows = pl.ds(pl.multiple_of(i * CHUNK, CHUNK), CHUNK)
        mine = band_of_rows(row_at, i * CHUNK, CHUNK) == me[0]
        for plane in range(2):
            own = cut_rows(blocks, plane, rows, amount)
            other = sibling[0, plane, rows, :].astype(jnp.float32)
            out[plane, rows, :] = jnp.where(mine, own, other).astype(jnp.bfloat16)
        return carry

    lax.fori_loop(0, PATCH // CHUNK, body, 0)


def cut_and_merge(band, sibling, pos, me, which):
    def block(k):
        def index(i, pos, me):
            return (0, 0, first_col(pos, 2 * lax.bitwise_xor(me[0], 2) + which) // LANES + k)

        return pl.BlockSpec((2, PATCH, LANES), index)

    return pl.pallas_call(
        functools.partial(merge_kernel, which),
        grid_spec=pltpu.PrefetchScalarGridSpec(
            num_scalar_prefetch=2,
            grid=(1,),
            in_specs=[block(k) for k in range(WIDE // LANES)]
            + [pl.BlockSpec((1, 2, PATCH, PATCH), lambda i, pos, me: (0, 0, 0, 0))],
            out_specs=pl.BlockSpec((2, PATCH, PATCH), lambda i, pos, me: (0, 0, 0)),
        ),
        out_shape=jax.ShapeDtypeStruct((2, PATCH, PATCH), jnp.bfloat16),
        compiler_params=pltpu.CompilerParams(vmem_limit_bytes=CUT_VMEM),
        cost_estimate=pl.CostEstimate(
            flops=2 * PATCH * WIDE, bytes_accessed=3300000, transcendentals=0
        ),
    )(pos, me, *([band] * (WIDE // LANES)), sibling)


def rest_index(step, pos, me):
    return jnp.where(step == 0, 2 * lax.bitwise_xor(me[0], 3) + 1, 2 * lax.bitwise_xor(me[0], 1) + step - 1)


def rest_kernel(pos, me, *refs):
    blocks, second, pieces = refs[:-2], refs[-2], refs[-1]
    step = pl.program_id(0)
    amount = lax.rem(first_col(pos, rest_index(step, pos, me)), LANES)

    def take(out):
        def body(i, carry):
            rows = pl.ds(pl.multiple_of(i * CHUNK, CHUNK), CHUNK)
            for plane in range(2):
                out[0, plane, rows, :] = cut_rows(blocks, plane, rows, amount).astype(jnp.bfloat16)
            return carry

        lax.fori_loop(0, PATCH // CHUNK, body, 0)

    pl.when(step == 0)(lambda: take(second))
    pl.when(step > 0)(lambda: take(pieces))


def cut_rest(band, pos, me):
    def block(k):
        def index(i, pos, me):
            return (0, 0, first_col(pos, rest_index(i, pos, me)) // LANES + k)

        return pl.BlockSpec((2, PATCH, LANES), index)

    shape = (2, PATCH, PATCH)
    return pl.pallas_call(
        rest_kernel,
        grid_spec=pltpu.PrefetchScalarGridSpec(
            num_scalar_prefetch=2,
            grid=(3,),
            in_specs=[block(k) for k in range(WIDE // LANES)],
            out_specs=[
                pl.BlockSpec((1, *shape), lambda i, pos, me: (0, 0, 0, 0)),
                pl.BlockSpec((1, *shape), lambda i, pos, me: (jnp.maximum(i - 1, 0), 0, 0, 0)),
            ],
        ),
        out_shape=[
            jax.ShapeDtypeStruct((1, *shape), jnp.bfloat16),
            jax.ShapeDtypeStruct((2, *shape), jnp.bfloat16),
        ],
        compiler_params=pltpu.CompilerParams(vmem_limit_bytes=CUT_VMEM),
        cost_estimate=pl.CostEstimate(
            flops=6 * PATCH * WIDE, bytes_accessed=7000000, transcendentals=0
        ),
    )(pos, me, *([band] * (WIDE // LANES)))


def wave_kernel(which, pos, me, spare, band, sibling, across, probe, amplitudes, *refs):
    tables, refs = refs[:3], refs[3:]
    last = which == 1
    if last:
        term_in, grad, keep_term, give_term, *scratch = refs
    else:
        grad, term_out, *scratch = refs
    window, sib_v, far_v, probe_v, amp_v, matrix, term_v, patch_v, twice, field, half, sems = scratch
    index = 2 * me[0] + which
    col_at = first_col(pos, index)
    row_at = first_row(pos, index)
    start = pl.multiple_of(col_at // LANES * LANES, LANES)
    pairs = [
        (band.at[:, :, pl.ds(start, WIDE)], window),
        (sibling.at[which], sib_v),
        (across, far_v),
        (probe, probe_v),
    ]
    cosine, sine, minus = tables
    quarters = [(slice(0, PATCH), slice(0, PATCH)), (slice(0, PATCH), slice(PATCH, 2 * PATCH))]
    quarters += [(slice(PATCH, 2 * PATCH), slice(0, PATCH)), (slice(PATCH, 2 * PATCH), slice(PATCH, 2 * PATCH))]
    pairs += [(t, matrix.at[q]) for t, q in zip((cosine, minus, sine, cosine), quarters)]
    pairs.append((amplitudes.at[which], amp_v))
    if last:
        pairs.append((term_in, term_v))
    copies = [pltpu.make_async_copy(a, b, sems.at[k]) for k, (a, b) in enumerate(pairs)]
    for copy in copies:
        copy.start()
    for copy in copies[:3]:
        copy.wait()
    amount = lax.rem(col_at, LANES)
    down = lax.rem(row_at, PATCH)
    views = [window.at[:, :, LANES * k : LANES * (k + 1)] for k in range(WIDE // LANES)]

    def assemble(i, carry):
        at = pl.multiple_of(i * CHUNK, CHUNK)
        rows = pl.ds(at, CHUNK)
        owner = band_of_rows(row_at, at, CHUNK)
        mine = owner == me[0]
        near = owner == lax.bitwise_xor(me[0], 1)
        for plane in range(2):
            own = cut_rows(views, plane, rows, amount)
            beside = sib_v[plane, rows, :].astype(jnp.float32)
            beyond = far_v[plane, rows, :].astype(jnp.float32)
            patch = jnp.where(mine, own, jnp.where(near, beside, beyond))
            twice[plane, rows, :] = patch
            twice[plane, pl.ds(pl.multiple_of(at + PATCH, CHUNK), CHUNK), :] = patch
        return carry

    lax.fori_loop(0, PATCH // CHUNK, assemble, 0)
    copies[3].wait()

    def illuminate(i, carry):
        at = pl.multiple_of(i * CHUNK, CHUNK)
        rows = pl.ds(at, CHUNK)
        patch_real = rows_from(twice, 0, at + down, CHUNK)
        patch_imag = rows_from(twice, 1, at + down, CHUNK)
        patch_v[0, rows, :] = patch_real.astype(jnp.bfloat16)
        patch_v[1, rows, :] = patch_imag.astype(jnp.bfloat16)
        probe_real = probe_v[0, rows, :]
        probe_imag = probe_v[1, rows, :]
        field[rows, :] = (probe_real * patch_real - probe_imag * patch_imag).astype(jnp.bfloat16)
        field[pl.ds(pl.multiple_of(at + PATCH, CHUNK), CHUNK), :] = (
            probe_real * patch_imag + probe_imag * patch_real
        ).astype(jnp.bfloat16)
        return carry

    lax.fori_loop(0, PATCH // CHUNK, illuminate, 0)
    for copy in copies[4:8]:
        copy.wait()

    def over_rows():
        for k in range(4):
            part = jnp.dot(
                matrix[256 * k : 256 * (k + 1), :], field[...], preferred_element_type=jnp.float32
            ).astype(jnp.bfloat16)
            at = PATCH * (1 - k // 2)
            half[256 * (k % 2) : 256 * (k % 2 + 1), at : at + PATCH] = part

    over_rows()
    copies[8].wait()
    for k in range(2):
        rows = slice(256 * k, 256 * (k + 1))
        far = jnp.dot(half[rows, :], matrix[...], preferred_element_type=jnp.float32)
        far_imag = far[:, :PATCH]
        far_real = far[:, PATCH:]
        power = far_real * far_real + far_imag * far_imag
        keep = 1.0 - amp_v[rows, :].astype(jnp.float32) * lax.rsqrt(
            jnp.maximum(power, MAGNITUDE_FLOOR * MAGNITUDE_FLOOR)
        )
        field[rows, :] = (far_imag * keep).astype(jnp.bfloat16)
        field[PATCH + 256 * k : PATCH + 256 * (k + 1), :] = (far_real * keep).astype(jnp.bfloat16)
    over_rows()
    if last:
        copies[9].wait()
        core = lax.rem(me[0], 2)
    for k in range(2):
        rows = slice(256 * k, 256 * (k + 1))
        back = jnp.dot(half[rows, :], matrix[...], preferred_element_type=jnp.float32)
        back_real = back[:, :PATCH]
        back_imag = back[:, PATCH:]
        patch_real = patch_v[0, rows, :].astype(jnp.float32)
        patch_imag = patch_v[1, rows, :].astype(jnp.float32)
        term_real = patch_real * back_real + patch_imag * back_imag
        term_imag = patch_real * back_imag - patch_imag * back_real
        if last:
            term_real = term_real + term_v[0, rows, :]
            term_imag = term_imag + term_v[1, rows, :]
            keep_term[rows, :] = jnp.where(core == 0, term_real, term_imag)
            give_term[rows, :] = jnp.where(core == 0, term_imag, term_real).astype(jnp.bfloat16)
        else:
            term_out[0, rows, :] = term_real
            term_out[1, rows, :] = term_imag
        term_v[0, rows, :] = back_real
        term_v[1, rows, :] = back_imag

    def weigh(i, carry):
        at = pl.multiple_of(i * CHUNK, CHUNK)
        rows = pl.ds(at, CHUNK)
        again = pl.ds(pl.multiple_of(at + PATCH, CHUNK), CHUNK)
        probe_real = probe_v[0, rows, :]
        probe_imag = probe_v[1, rows, :]
        back_real = term_v[0, rows, :]
        back_imag = term_v[1, rows, :]
        grad_real = probe_real * back_real + probe_imag * back_imag
        grad_imag = probe_real * back_imag - probe_imag * back_real
        twice[0, rows, :] = grad_real
        twice[0, again, :] = grad_real
        twice[1, rows, :] = grad_imag
        twice[1, again, :] = grad_imag
        return carry

    lax.fori_loop(0, PATCH // CHUNK, weigh, 0)
    classes, height = grad.shape[0], grad.shape[2]

    def spread(k, carry):
        for plane in range(2):
            grad[k, plane] = rows_from(twice, plane, PATCH - down + k * height, height).astype(
                jnp.bfloat16
            )
        return carry

    lax.fori_loop(0, classes, spread, 0)


def wave(which, classes, pos, me, spare, band, sibling, across, probe, amplitudes, tables, term):
    operands = [band, sibling, across, probe, amplitudes, *tables]
    smem = pl.BlockSpec(memory_space=pltpu.SMEM)
    hbm = pl.BlockSpec(memory_space=pl.ANY)
    vmem = pl.BlockSpec(memory_space=pltpu.VMEM)
    planes = (2, PATCH, PATCH)
    plane = (PATCH, PATCH)
    if term is None:
        terms = [jax.ShapeDtypeStruct(planes, jnp.float32)]
    else:
        operands.append(term)
        terms = [jax.ShapeDtypeStruct(plane, t) for t in (jnp.float32, jnp.bfloat16)]
    return pl.pallas_call(
        functools.partial(wave_kernel, which),
        in_specs=[smem, smem, smem] + [hbm] * len(operands),
        out_specs=[vmem] * (1 + len(terms)),
        out_shape=[
            jax.ShapeDtypeStruct((classes, 2, PATCH // classes, PATCH), jnp.bfloat16),
            *terms,
        ],
        scratch_shapes=[
            pltpu.VMEM((2, PATCH, WIDE), jnp.bfloat16),
            pltpu.VMEM(planes, jnp.bfloat16),
            pltpu.VMEM(planes, jnp.bfloat16),
            pltpu.VMEM(planes, jnp.float32),
            pltpu.VMEM((PATCH, PATCH), jnp.bfloat16),
            pltpu.VMEM((2 * PATCH, 2 * PATCH), jnp.bfloat16),
            pltpu.VMEM(planes, jnp.float32),
            pltpu.VMEM(planes, jnp.bfloat16),
            pltpu.VMEM((2, 2 * PATCH + SUBLANES, PATCH), jnp.float32),
            pltpu.VMEM((2 * PATCH, PATCH), jnp.bfloat16),
            pltpu.VMEM((PATCH, 2 * PATCH), jnp.bfloat16),
            pltpu.SemaphoreType.DMA((10,)),
        ],
        compiler_params=pltpu.CompilerParams(vmem_limit_bytes=WAVE_VMEM),
        cost_estimate=pl.CostEstimate(
            flops=32 * PATCH**3, bytes_accessed=100_000_000, transcendentals=0
        ),
    )(pos, me, spare, *operands)


def sum_kernel(pos, me, first, second, own_far, own_near, away_far, away_near, canvas):
    classes, height = first.shape[0], first.shape[2]
    start = me[1] * height
    canvas[...] = jnp.zeros_like(canvas)
    rows = lax.broadcasted_iota(jnp.int32, (2 * height, WIDE), 0)
    rows = start + jnp.where(rows >= height, rows - height, rows)

    def piece(k, source, which):
        index = 2 * k + which
        row_at = first_row(pos, index)
        col_at = first_col(pos, index)
        down = lax.rem(row_at, PATCH)
        at = pl.ds(pl.multiple_of(col_at // LANES * LANES, LANES), WIDE)
        data = source[k].astype(jnp.float32).reshape(2 * height, PATCH)
        data = shifted_right(data, lax.rem(col_at, LANES))

        @pl.when(down < start + height)
        def _():
            canvas[row_at // PATCH, :, at] += jnp.where(rows >= down, data, 0.0)

        @pl.when(down > start)
        def _():
            canvas[row_at // PATCH + 1, :, at] += jnp.where(rows < down, data, 0.0)

    def body(k, carry):
        piece(k, first, 0)
        piece(k, second, 1)
        return carry

    lax.fori_loop(0, classes, body, 0)
    shape = own_far.shape
    for k, (own, away) in enumerate([(own_far, away_far), (own_near, away_near)]):
        keep = lax.bitwise_xor(me[0], 2 - 2 * k)
        give = lax.bitwise_xor(me[0], 3 - 2 * k)
        own[...] = canvas[keep].reshape(shape)
        away[...] = canvas[give].reshape(shape).astype(jnp.bfloat16)


def sum_pieces(pos, me, first, second, bands, width):
    height = first.shape[2]
    smem = pl.BlockSpec(memory_space=pltpu.SMEM)
    vmem = pl.BlockSpec(memory_space=pltpu.VMEM)
    shape = (2, height, width)
    return pl.pallas_call(
        sum_kernel,
        in_specs=[smem, smem, vmem, vmem],
        out_specs=[vmem] * 4,
        out_shape=[
            jax.ShapeDtypeStruct(shape, kind)
            for kind in (jnp.float32, jnp.float32, jnp.bfloat16, jnp.bfloat16)
        ],
        scratch_shapes=[pltpu.VMEM((bands, 2 * height, width), jnp.float32)],
        compiler_params=pltpu.CompilerParams(vmem_limit_bytes=SUM_VMEM),
        cost_estimate=pl.CostEstimate(
            flops=8 * first.size, bytes_accessed=4 * first.size + 12 * math.prod(shape), transcendentals=0
        ),
    )(pos, me, first, second)


def assemble_kernel(length, me, *refs):
    steps = length - 1
    own, refs = refs[0], refs[1:]
    ups, downs, overs = refs[:steps], refs[steps : 2 * steps], refs[2 * steps : 3 * steps + 1]
    out, sems = refs[3 * steps + 1 :]
    height = own.shape[1]
    place = me[1] // 2
    side = lax.rem(me[1], 2)

    def copy(source, at, column, k):
        rows = pl.ds(pl.multiple_of((2 * at + column) * height, height), height)
        return pltpu.make_async_copy(source, out.at[:, rows, :], sems.at[k])

    always = [copy(own, place, side, 0)]
    for k in range(length):
        always.append(copy(overs[k], sent_over(place, k, length), 1 - side, k + 1))
    some = []
    for k in range(1, length):
        below, above = place - k, place + k
        held = length + 2 * k - 1
        some.append((below >= 0, copy(ups[k - 1], below, side, held)))
        some.append((above < length, copy(downs[k - 1], above, side, held + 1)))
    for part in always:
        part.start()
    for has, part in some:
        pl.when(has)(part.start)
    for part in always:
        part.wait()
    for has, part in some:
        pl.when(has)(part.wait)


def sent_over(place, k, length):
    low = jnp.where(place >= k, place - k, place + k)
    if k == length - 1:
        high = jnp.where(place == 0, length - 1, jnp.where(place == length - 1, 0, place + 1))
        return high
    return low


def gather_classes(own, me, classes, term, term_steps):
    length = classes // 2
    place = me[1] // 2

    def along(value, held, step):
        pairs = [(2 * z + x, 2 * (z + step) + x) for z in held if 0 <= z + step < length for x in range(2)]
        return lax.ppermute(value, "pat", pairs)

    def over(value):
        return lax.ppermute(value, "pat", [(k, k ^ 1) for k in range(classes)])

    ups, downs, overs = [own], [own], []
    for k in range(length - 1):
        overs.append(over(jnp.where(place >= k, ups[k], downs[k]) if k else own))
        ups.append(along(ups[k], range(k, length), 1))
        downs.append(along(downs[k], range(length - k), -1))
        if k == length - 2:
            for step in term_steps:
                term = step(term)
        overs[k], ups[k + 1], downs[k + 1], term = lax.optimization_barrier(
            (overs[k], ups[k + 1], downs[k + 1], term)
        )
    end = jnp.where(place == 0, downs[-1], ups[-1])
    if length > 2:
        middle = (place > 0) & (place < length - 1)
        end = jnp.where(middle, downs[1], end)
    overs.append(over(end))
    operands = [own, *ups[1:], *downs[1:], *overs]
    object_next = pl.pallas_call(
        functools.partial(assemble_kernel, length),
        in_specs=[pl.BlockSpec(memory_space=pltpu.SMEM)]
        + [pl.BlockSpec(memory_space=pltpu.VMEM)] * len(operands),
        out_specs=pl.BlockSpec(memory_space=pl.ANY),
        out_shape=jax.ShapeDtypeStruct((2, classes * own.shape[1], own.shape[2]), own.dtype),
        scratch_shapes=[pltpu.SemaphoreType.DMA((3 * length - 1,))],
        compiler_params=pltpu.CompilerParams(vmem_limit_bytes=CUT_VMEM),
        cost_estimate=pl.CostEstimate(
            flops=0, bytes_accessed=4 * own.size * classes, transcendentals=0
        ),
    )(me, *operands)
    return object_next, term


def shards(object_image, probe, amplitudes, pos_tile, pos_offset):
    owners = lax.axis_size("obj")
    classes = lax.axis_size("pat")
    my_owner = lax.axis_index("obj").astype(jnp.int32)
    my_class = lax.axis_index("pat").astype(jnp.int32)
    me = jnp.stack([my_owner, my_class])
    height = PATCH // classes
    width = object_image.shape[2]
    assert owners == 4 and object_image.shape[1] == PATCH and pos_tile.shape[0] == 2

    def flip(value, bit):
        return lax.ppermute(value, "obj", [(k, k ^ bit) for k in range(owners)])

    def pat_flip(bit):
        return lambda value: lax.ppermute(value, "pat", [(k, k ^ bit) for k in range(classes)])

    def halved(part, bit, other):
        rows = part.shape[0] // 2
        give = lax.dynamic_slice_in_dim(part, (1 - bit) * rows, rows, 0).astype(jnp.bfloat16)
        return lax.dynamic_slice_in_dim(part, bit * rows, rows, 0) + other(give).astype(jnp.float32)

    def doubled(part, bit, other):
        got = other(part)
        return jnp.where(bit == 0, jnp.concatenate([part, got]), jnp.concatenate([got, part]))

    bits = [1 << k for k in range(classes.bit_length() - 1)]
    halving = bits[1:] + bits[:1]
    own_pos = jnp.concatenate([pos_tile, pos_offset], 1)
    pos = lax.all_gather(own_pos, "obj", axis=0, tiled=True)

    first = cut(object_image, pos, me, 3, 0, 1)
    second, pieces = cut_rest(object_image, pos, me)
    second, pieces, then = lax.optimization_barrier((second, pieces, me))
    relay = [flip(first, 1), flip(second, 1)]
    sibling = flip(pieces, 1)
    merged = [cut_and_merge(object_image, relay[k], pos, then, k) for k in range(2)]
    merged[1], pos_pat = lax.optimization_barrier((merged[1], own_pos))
    across = [flip(m, 2) for m in merged]
    for bit in bits:
        pos_pat = doubled(pos_pat, my_class // bit % 2, pat_flip(bit))

    operands = (probe, amplitudes, dft_tables(PATCH))
    grad_0, term = wave(0, classes, pos, me, pos_pat, object_image, sibling, across[0], *operands, None)
    grad_0, across[1] = lax.optimization_barrier((grad_0, across[1]))
    part_0 = lax.all_to_all(grad_0, "pat", split_axis=0, concat_axis=0, tiled=True)
    grad_1, keep_term, give_term = wave(
        1, classes, pos, me, me, object_image, sibling, across[1], *operands, term
    )
    grad_1, part_0 = lax.optimization_barrier((grad_1, part_0))
    part_1 = lax.all_to_all(grad_1, "pat", split_axis=0, concat_axis=0, tiled=True)

    core = my_owner % 2
    line = my_owner // 2
    term = keep_term + flip(give_term, 1).astype(jnp.float32)
    term = halved(term, line, lambda value: flip(value, 2))
    term, then = lax.optimization_barrier((term, me))
    own_far, own_near, away_far, away_near = sum_pieces(
        pos_pat, then, part_0, part_1, owners, width
    )
    from_sibling_far = flip(away_far, 1)
    from_sibling = flip(away_near, 1)
    from_across = flip(
        (own_far + from_sibling_far.astype(jnp.float32)).astype(jnp.bfloat16), 2
    )
    for bit in halving:
        term = halved(term, my_class // bit % 2, pat_flip(bit))
    term = term.astype(jnp.bfloat16)
    for bit in reversed(halving):
        term = doubled(term, my_class // bit % 2, pat_flip(bit))
    total = own_near + from_sibling.astype(jnp.float32) + from_across.astype(jnp.float32)
    mine = lax.dynamic_slice_in_dim(object_image, my_class * height, height, 1)
    updated = (mine.astype(jnp.float32) - OBJECT_RATE * total).astype(jnp.bfloat16)
    updated, term = lax.optimization_barrier((updated, term))
    steps = [functools.partial(doubled, bit=line, other=lambda value: flip(value, 2))]
    steps.append(lambda part: doubled(part[None], core, lambda value: flip(value, 1)))
    if classes in BY_PERMUTE:
        object_next, term = gather_classes(updated, me, classes, term, steps)
    else:
        object_next = lax.all_gather(updated, "pat", axis=1, tiled=True)
        for step in steps:
            term = step(term)
    probe_total = term.astype(jnp.float32)
    probe_next = probe - PROBE_RATE * probe_total
    return (object_next, probe_next)


def solution(mesh):
    return jax.shard_map(
        shards,
        mesh=mesh,
        in_specs=(
            P(None, "obj", None),
            P(),
            P(("pat", "obj"), None, None),
            P(("pat", "obj"), None),
            P(("pat", "obj"), None),
        ),
        out_specs=(P(None, "obj", None), P()),
        check_vma=False,
    )
```
